32 devices in a mesh: pix: 8 (over z, x), ch: 4 (over y, core).
Axes of the slice: x: 2, y: 2, z: 4, core: 2. Of those that a mesh axis runs over, the one named last changes fastest.
Arguments:
- pixels: bfloat16 [384, 32768], P('pix', 'ch'), may hold values from -6 to 6
- cotangent: bfloat16 [384, 32768], P('pix', 'ch'), may hold values from -6 to 6
- crop_rows: int32 [16], replicated, may hold values from 1 to 32, 384 in all
- condition: bfloat16 [16, 1024], replicated, may hold values from -6 to 6
- context: bfloat16 [16, 4, 1024], replicated, may hold values from -6 to 6
- kernels: bfloat16 [1024, 18432], P('pix', 'ch'), may hold values from -0.0625 to 0.0625
- attention: bfloat16 [1024, 6144], P('pix', 'ch'), as said below
- embedding: bfloat16 [1024, 2048], P('pix', 'ch'), may hold values from -0.1875 to 0.1875
- gains: float32 [3, 1024], P(None, 'ch'), may hold values from 0.1 to 1.9
- shifts: float32 [3, 1024], P(None, 'ch'), may hold values from -2 to 2
- offsets: float32 [4, 1024], P(None, 'ch'), may hold values from -2 to 2
Outputs:
- result: float32 [384, 32768], P('pix', 'ch')
- grad_pixels: float32 [384, 32768], P('pix', 'ch')
- grad_kernels: float32 [1024, 18432], P('pix', 'ch')
- grad_attention: float32 [1024, 6144], P('pix', 'ch')
- grad_embedding: float32 [1024, 2048], P('pix', 'ch')
- grad_gains: float32 [3, 1024], P(None, 'ch')
- grad_shifts: float32 [3, 1024], P(None, 'ch')
- grad_offsets: float32 [4, 1024], P(None, 'ch')
The draws below stay inside these ranges and needn't reach their ends.
Inputs may be any that keep to these rules, and one draw needn't show every extreme that they name: crop_rows sums to 384; the largest entry is 32. `attention`: drawn as weights scaled by the fan-in of each matrix.
All inputs are finite; a program needn't handle non-finite values.
Results may differ from the reference program's by a relative error of at most 0.025.
Values may be sent and summed in bfloat16 or wider, within the bound.
No kernel may reach another device: no remote copies, remote signals or barrier semaphores. Data moves between devices by JAX's collectives and lax.ppermute only.
A program may use at most 448 MiB of HBM per device.

```python
import math
import jax
import jax.numpy as jnp
import numpy as np
from jax import lax

C = 1024
HEADS = 16
HEAD_DIM = 64
GROUPS = 32
W = 32
CROP_ROWS = 32
CTX = 4
NCROP = 16
ROWS = 384
TOKENS = 12288
GSIZE = 32


def draw_attention(key, part):
    key = jax.random.fold_in(key, 7)
    base = jnp.clip(jax.random.normal(key, (C, C * 6), jnp.float32), -6.0, 6.0)
    column = jnp.arange(C * 6, dtype=jnp.int32) % 6
    scale = jnp.where(column == 5, (C // 32) ** (-0.5), (C // 2) ** (-0.5)).astype(jnp.float32)
    return (base * scale[None, :]).astype(jnp.bfloat16)


def block_scale(key, shape, shards, least, high):
    gain = 1.0
    for position, shards_of in shards:
        draws = jax.random.uniform(jax.random.fold_in(jax.random.fold_in(key, 6), position), (shards_of,), jnp.float32, least / len(shards), high / len(shards))
        gain = gain * jnp.repeat(jnp.exp(draws), shape[position] // shards_of).reshape((-1,) + (1,) * (len(shape) - 1 - position))
    return gain


def profile(count, total, bound, slope):
    weights = [(1 << 20) // math.isqrt(grade ** slope) + 1 for grade in range(2, count + 1)]
    spare, holding = total - bound - (count - 1), [1] * (count - 1)
    while spare > 0:
        movable = [i for i in range(count - 1) if holding[i] < bound]
        whole, left = sum([weights[i] for i in movable]), spare
        for i in movable:
            extra = min(bound - holding[i], max(1, left * weights[i] // whole), spare)
            holding[i] = holding[i] + extra
            spare = spare - extra
    return np.array([bound] + holding)


def ragged_sizes(stream_key, count, total, reach, slope):
    if count == 2:
        one = jax.random.randint(stream_key, (), max(1, total - reach), min(reach, total - 1) + 1)
        return jnp.stack([one, total - one])
    tallies = jnp.asarray(profile(count, total, reach, slope), jnp.int32)
    pairs = (count - 1) // 2
    source_of, receiver = tallies[1:1 + 2 * pairs:2], tallies[2:2 + 2 * pairs:2]
    slack = jnp.minimum(source_of - 1, reach - receiver)
    moved = jax.random.randint(jax.random.fold_in(stream_key, 1), (pairs,), 0, 1 << 20) % (slack + 1)
    tallies = tallies.at[1:1 + 2 * pairs:2].set(source_of - moved).at[2:2 + 2 * pairs:2].set(receiver + moved)
    return tallies[jax.random.permutation(jax.random.fold_in(stream_key, 2), count)]


def noise(own_key, extent, width, bound, shards=(), kind=jnp.bfloat16):
    array = width * jax.random.normal(own_key, extent, jnp.float32)
    if shards:
        array = array * block_scale(own_key, extent, shards, -0.22, 0.18)
    return jnp.clip(array, -bound, bound).astype(kind)


def setup_inputs(seed: int = 0) -> dict:
    splits = jax.random.split(jax.random.key(seed), 12)
    pixels = noise(splits[0], (ROWS, C * W), 1.0, 6.0, ((0, 8), (1, 4)))
    cotangent = noise(splits[1], (ROWS, C * W), 1.0, 6.0, ((0, 8), (1, 4)))
    crop_rows = ragged_sizes(splits[2], NCROP, ROWS, CROP_ROWS, 2).astype(jnp.int32)
    condition = noise(splits[3], (NCROP, C), 1.0, 6.0)
    context = noise(splits[4], (NCROP, CTX, C), 1.0, 6.0)
    kernels = noise(splits[5], (C, 18 * C), (9 * C) ** -0.5, 0.0625, ((0, 8), (1, 4)))
    attention = draw_attention(jax.random.fold_in(splits[11], 71), 0)
    embedding = noise(splits[7], (C, 2 * C), C ** -0.5, 0.1875, ((0, 8), (1, 4)))
    gains = jnp.clip(1.0 + 0.18 * jax.random.normal(splits[8], (3, C), jnp.float32), 0.1, 1.9)
    shifts = noise(splits[9], (3, C), 0.3, 2.0, ((1, 4),), jnp.float32)
    offsets = noise(splits[10], (4, C), 0.3, 2.0, ((1, 4),), jnp.float32)
    return dict(pixels=pixels, cotangent=cotangent, crop_rows=crop_rows, condition=condition, context=context, kernels=kernels, attention=attention, embedding=embedding, gains=gains, shifts=shifts, offsets=offsets)


@jax.custom_vjp
def low(v):
    return lax.optimization_barrier(v.astype(jnp.bfloat16)).astype(jnp.float32)

@jax.custom_vjp
def low_back(v):
    return v

def low_keep(v):
    return (low(v), None)

def low_pass(kept, grad):
    return (grad,)

def back_keep(v):
    return (v, None)

def back_low(kept, grad):
    return (low(grad),)
low.defvjp(low_keep, low_pass)
low_back.defvjp(back_keep, back_low)
HIGHEST = lax.Precision.HIGHEST
EPSILON = 1e-05
NEGATIVE = -1e+30

def product(left, right):
    return jnp.dot(left, right, precision=HIGHEST, preferred_element_type=jnp.float32)

def unpack_pixels(packed):
    return packed.reshape(ROWS, C, W).transpose(0, 2, 1).reshape(TOKENS, C)

def pack_pixels(flat):
    return flat.reshape(ROWS, W, C).transpose(0, 2, 1).reshape(ROWS, C * W)

def unpack_matrices(packed, count):
    return packed.reshape(C, C, count).transpose(2, 0, 1)

def crop_of_pixels(crop_rows):
    bounds = jnp.cumsum(crop_rows) * W
    places = jnp.arange(TOKENS, dtype=jnp.int32)
    return lax.optimization_barrier(jnp.sum((places[:, None] >= bounds[None, :]).astype(jnp.int32), axis=1))

def tap_masks(crop_ids):
    places = jnp.arange(TOKENS, dtype=jnp.int32)
    column = places % W
    edge_fill = jnp.full((W + 1,), -1, jnp.int32)
    padded = jnp.concatenate([edge_fill, crop_ids, edge_fill])
    collected = []
    for tap_index in range(9):
        step_x = tap_index % 3 - 1
        window_start = W + 1 + (tap_index // 3 - 1) * W + step_x
        source = padded[window_start:window_start + TOKENS]
        inside = (source == crop_ids) & (column + step_x >= 0) & (column + step_x < W)
        collected.append(inside.astype(jnp.float32))
    return jnp.stack(collected)

def convolve(values, weights, tap_mask):
    padded = jnp.pad(values, ((W + 1, W + 1), (0, 0)))
    summed = jnp.zeros((TOKENS, C), jnp.float32)
    for tap_index in range(9):
        window_start = W + 1 + (tap_index // 3 - 1) * W + tap_index % 3 - 1
        shifted = tap_mask[tap_index][:, None] * padded[window_start:window_start + TOKENS]
        summed = summed + product(shifted, weights[tap_index])
    return summed

def group_norm(values, gain_row, shift_row, crop_ids, counts):
    grouped = values.reshape(TOKENS, GROUPS, GSIZE)
    first_sum = jax.ops.segment_sum(lax.optimization_barrier(jnp.sum(grouped, axis=2)), crop_ids, num_segments=NCROP)
    second_sum = jax.ops.segment_sum(lax.optimization_barrier(jnp.sum(grouped * grouped, axis=2)), crop_ids, num_segments=NCROP)
    mean_crop = first_sum / counts[:, None]
    inverse = lax.rsqrt(second_sum / counts[:, None] - mean_crop * mean_crop + EPSILON)
    normal = (grouped - mean_crop[crop_ids][:, :, None]) * inverse[crop_ids][:, :, None]
    return normal.reshape(TOKENS, C) * gain_row + shift_row

def attend(queries, keys_own, values_own, keys_context, values_context, crop_ids):
    span = CROP_ROWS * W
    block_rows = min(512, TOKENS)
    block_count = TOKENS // block_rows
    window = block_rows + 2 * span
    score_scale = HEAD_DIM ** (-0.5)
    keys_pad = jnp.pad(keys_own, ((span, span), (0, 0)))
    values_pad = jnp.pad(values_own, ((span, span), (0, 0)))
    edge_fill = jnp.full((span,), -1, jnp.int32)
    crops_pad = jnp.concatenate([edge_fill, crop_ids, edge_fill])
    context_crops = jnp.repeat(jnp.arange(NCROP, dtype=jnp.int32), CTX)

    def one_block(inputs):
        block_query, block_crop, block_start = inputs
        block_query = block_query.reshape(block_rows, HEADS, HEAD_DIM)
        keys_window = jnp.concatenate([lax.dynamic_slice_in_dim(keys_pad, block_start, window), keys_context]).reshape(-1, HEADS, HEAD_DIM)
        values_window = jnp.concatenate([lax.dynamic_slice_in_dim(values_pad, block_start, window), values_context]).reshape(-1, HEADS, HEAD_DIM)
        crops_window = jnp.concatenate([lax.dynamic_slice_in_dim(crops_pad, block_start, window), context_crops])
        scores = low_back(jnp.einsum('qhd,khd->hqk', block_query, keys_window, precision=HIGHEST) * score_scale)
        scores = jnp.where(block_crop[None, :, None] == crops_window[None, None, :], scores, NEGATIVE)
        largest = lax.optimization_barrier(jnp.max(scores, axis=2, keepdims=True))
        expo = jnp.exp(scores - largest)
        prob_rows = low(expo / lax.optimization_barrier(jnp.sum(expo, axis=2, keepdims=True)))
        mixed = jnp.einsum('hqk,khd->qhd', prob_rows, values_window, precision=HIGHEST)
        return mixed.reshape(block_rows, C)
    starts = jnp.arange(block_count, dtype=jnp.int32) * block_rows
    outputs = lax.map(jax.checkpoint(one_block), (queries.reshape(block_count, block_rows, C), crop_ids.reshape(block_count, block_rows), starts))
    return outputs.reshape(TOKENS, C)

def layer(pixels_f, kernels_f, projections_f, encoder_f, embedding_f, readout_f, gains_f, shifts_f, offsets_f, condition_f, context_f, crop_ids, tap_mask, counts):
    active_one = low(jax.nn.silu(group_norm(pixels_f, gains_f[0], shifts_f[0], crop_ids, counts)))
    conv_one = low_back(convolve(active_one, kernels_f[:9], tap_mask))
    embed_terms = jnp.einsum('nc,jcd->njd', condition_f, embedding_f, precision=HIGHEST) + offsets_f[2:4][None]
    growth = 1.0 + embed_terms[:, 0][crop_ids]
    shift_add = embed_terms[:, 1][crop_ids]
    inner_two = group_norm(conv_one, gains_f[1], shifts_f[1], crop_ids, counts) * growth + shift_add
    active_two = low(jax.nn.silu(inner_two))
    conv_two = low_back(convolve(active_two, kernels_f[9:], tap_mask))
    residual = pixels_f + conv_two + offsets_f[0]
    normed = low(group_norm(residual, gains_f[2], shifts_f[2], crop_ids, counts))
    queries = low_back(low(product(normed, projections_f[0])))
    keys_own = low_back(low(product(normed, projections_f[1])))
    values_own = low_back(low(product(normed, projections_f[2])))
    keys_context = low(jnp.einsum('nkc,cd->nkd', context_f, encoder_f[0], precision=HIGHEST)).reshape(NCROP * CTX, C)
    values_context = low(jnp.einsum('nkc,cd->nkd', context_f, encoder_f[1], precision=HIGHEST)).reshape(NCROP * CTX, C)
    attended = low_back(low(attend(queries, keys_own, values_own, keys_context, values_context, crop_ids)))
    return residual + product(attended, readout_f) + offsets_f[1]

def reference(pixels, cotangent, crop_rows, condition, context, kernels, attention, embedding, gains, shifts, offsets):
    crop_ids = crop_of_pixels(crop_rows)
    tap_mask = tap_masks(crop_ids)
    counts = (crop_rows * (W * GSIZE)).astype(jnp.float32)
    condition_f = condition.astype(jnp.float32)
    context_f = context.astype(jnp.float32)

    def forward(pixels_p, kernels_p, attention_p, embedding_p, gains_f, shifts_f, offsets_f):
        pixels_f = unpack_pixels(pixels_p)
        kernels_f = unpack_matrices(kernels_p, 18)
        maps = unpack_matrices(attention_p, 6)
        embedding_f = unpack_matrices(embedding_p, 2)
        flat_out = layer(pixels_f, kernels_f, maps[:3], maps[3:5], embedding_f, maps[5].T, gains_f, shifts_f, offsets_f, condition_f, context_f, crop_ids, tap_mask, counts)
        return pack_pixels(flat_out)
    result, pullback = jax.vjp(forward, pixels.astype(jnp.float32), kernels.astype(jnp.float32), attention.astype(jnp.float32), embedding.astype(jnp.float32), gains.astype(jnp.float32), shifts.astype(jnp.float32), offsets.astype(jnp.float32))
    grad_pixels, grad_kernels, grad_attention, grad_embedding, grad_gains, grad_shifts, grad_offsets = pullback(cotangent.astype(jnp.float32))
    return (result, grad_pixels, grad_kernels, grad_attention, grad_embedding, grad_gains, grad_shifts, grad_offsets)
```

```python
import functools

import jax
import jax.numpy as jnp
from jax import lax
from jax.experimental import pallas as pl
from jax.experimental.pallas import tpu as pltpu
from jax.sharding import PartitionSpec as P

HEAD_DIM = 64
W = 32
CROP_ROWS = 32
CTX = 4
GSIZE = 32
HALO = (CROP_ROWS - 1) * W
QB = 256
KB = 256

HIGHEST = lax.Precision.HIGHEST
EPSILON = 1e-05
NEGATIVE = -1e30
BF = jnp.bfloat16
F32 = jnp.float32
VMEM_LIMIT = 58 * 1024 * 1024


def dot(left, right, dims):
    return lax.dot_general(left, right, (dims, ((), ())), preferred_element_type=F32)


NN = ((1,), (0,))
NT = ((1,), (1,))
TN = ((0,), (0,))


def params(**more):
    return pltpu.CompilerParams(vmem_limit_bytes=VMEM_LIMIT, **more)


def cost(flops, moved, exps=0):
    return pl.CostEstimate(flops=flops, bytes_accessed=moved, transcendentals=exps)


WITH_PREV, WITH_NEXT, INVERSE = 3, 4, 5
EDGE = 40


def exact(left, right):
    return lax.dot_general(
        left, right, (NN, ((), ())), precision=HIGHEST, preferred_element_type=F32
    )


def write_totals(first, second, same_ref, totals_ref, next_ref, prev_ref):
    lines, width = first.shape
    row = lax.broadcasted_iota(jnp.int32, (width, width), 0) // GSIZE
    column = lax.broadcasted_iota(jnp.int32, (width, width), 1) // GSIZE
    group = (row == column).astype(F32)
    for place, value in ((0, first), (1, second)):
        total = exact(same_ref[...], exact(value, group))
        totals_ref[place] = total
        next_ref[W + place : W + place + 1, :] = total[lines - 1 : lines, :]
        prev_ref[W + place : W + place + 1, :] = total[0:1, :]
    for target in (next_ref, prev_ref):
        target[W + 2 : EDGE, :] = jnp.zeros((EDGE - W - 2, width), F32)


def crop_means(totals_ref, before_ref, after_ref, rows_ref):
    found = []
    for place in range(2):
        line = slice(W + place, W + place + 1)
        total = totals_ref[place] + rows_ref[WITH_PREV] * before_ref[line, :]
        total = total + rows_ref[WITH_NEXT] * after_ref[line, :]
        found.append(total * rows_ref[INVERSE])
    return found


def square_sums(value_ref, sums_ref):
    lines = sums_ref.shape[1]

    def one(line, carry):
        cells = value_ref[pl.ds(pl.multiple_of(line * W, W), W), :]
        sums_ref[0, pl.ds(line, 1), :] = jnp.sum(cells, axis=0, keepdims=True)
        sums_ref[1, pl.ds(line, 1), :] = jnp.sum(cells * cells, axis=0, keepdims=True)
        return carry

    lax.fori_loop(0, lines, one, 0, unroll=4)


def stats_shapes(lines, width):
    return (
        jax.ShapeDtypeStruct((2, lines, width), F32),
        jax.ShapeDtypeStruct((EDGE, width), F32),
        jax.ShapeDtypeStruct((EDGE, width), F32),
    )


def stats_body(value_ref, same_ref, totals_ref, next_ref, prev_ref, sums_ref):
    tokens = value_ref.shape[0]
    square_sums(value_ref, sums_ref)
    write_totals(sums_ref[0], sums_ref[1], same_ref, totals_ref, next_ref, prev_ref)
    next_ref[0:W, :] = value_ref[tokens - W :, :]
    prev_ref[0:W, :] = value_ref[0:W, :]


def stats(value, same):
    tokens, width = value.shape
    return pl.pallas_call(
        stats_body,
        out_shape=stats_shapes(tokens // W, width),
        scratch_shapes=[pltpu.VMEM((2, tokens // W, width), F32)],
        compiler_params=params(),
        cost_estimate=cost(tokens * width * 4, tokens * width * 4),
        name="stats",
    )(value, same)


def norm_body(active, wide, *refs):
    value_ref, totals_ref, before_ref, after_ref, rows_ref, gain_ref, shift_ref = refs[:7]
    refs = refs[7:]
    if active == "mixed":
        growth_ref, add_ref = refs[:2]
        refs = refs[2:]
    out_ref, stats_ref, scale_ref, bias_ref = refs
    lines = totals_ref.shape[1]
    mean, square = crop_means(totals_ref, before_ref, after_ref, rows_ref)
    scale = lax.rsqrt(square - mean * mean + EPSILON)
    stats_ref[0] = mean
    stats_ref[1] = scale
    if active == "mixed":
        scale_ref[...] = scale * gain_ref[...] * growth_ref[...]
        bias_ref[...] = shift_ref[...] * growth_ref[...] + add_ref[...]
    else:
        scale_ref[...] = scale * gain_ref[...]
        bias_ref[...] = jnp.broadcast_to(shift_ref[...], bias_ref.shape)

    def cells_of(cells, line):
        here = pl.ds(line, 1)
        value = (cells - stats_ref[0, here, :]) * scale_ref[here, :] + bias_ref[here, :]
        if active is not None:
            value = value / (1.0 + jnp.exp(-value))
        return value.astype(BF)

    base = W if wide else 0

    def one(line, carry):
        start = pl.multiple_of(line * W, W)
        out_ref[pl.ds(start + base, W), :] = cells_of(value_ref[pl.ds(start, W), :], line)
        return carry

    lax.fori_loop(0, lines, one, 0, unroll=4)
    if wide:
        out_ref[0:W, :] = cells_of(before_ref[0:W, :], 0)
        out_ref[(lines + 1) * W :, :] = cells_of(after_ref[0:W, :], lines - 1)


def norm(value, totals, before, after, rows, gain, shift, mixed=None, active="plain", wide=True):
    tokens, width = value.shape
    lines = tokens // W
    operands = [value, totals, before, after, rows, gain, shift]
    if mixed is not None:
        operands += list(mixed)
        active = "mixed"
    return pl.pallas_call(
        functools.partial(norm_body, active, wide),
        out_shape=(
            jax.ShapeDtypeStruct((tokens + (2 * W if wide else 0), width), BF),
            jax.ShapeDtypeStruct((2, lines, width), F32),
        ),
        scratch_shapes=[pltpu.VMEM((lines, width), F32), pltpu.VMEM((lines, width), F32)],
        compiler_params=params(),
        cost_estimate=cost(tokens * width * 12, tokens * width * 6, tokens * width),
        name="norm",
    )(*operands)


def sums_body(count, active, *refs):
    parts = refs[:count]
    value_ref, stats_ref, gain_ref, shift_ref, same_ref = refs[count : count + 5]
    refs = refs[count + 5 :]
    if active == "mixed":
        growth_ref, add_ref = refs[:2]
        refs = refs[2:]
    grad_ref, raw_ref, totals_ref, next_ref, prev_ref = refs
    tokens, width = value_ref.shape
    lines = tokens // W

    def one(line, carry):
        here = pl.ds(line, 1)
        cells = pl.ds(pl.multiple_of(line * W, W), W)
        grad = parts[0][cells, :].astype(F32)
        for part in parts[1:]:
            grad = grad + part[cells, :].astype(F32)
        normal = (value_ref[cells, :] - stats_ref[0, here, :]) * stats_ref[1, here, :]
        if active is not None:
            inner = normal * gain_ref[...] + shift_ref[...]
            if active == "mixed":
                inner = inner * growth_ref[here, :] + add_ref[here, :]
            sigmoid = 1.0 / (1.0 + jnp.exp(-inner))
            grad = grad * sigmoid * (1.0 + inner * (1.0 - sigmoid))
        raw_ref[0, here, :] = jnp.sum(grad, axis=0, keepdims=True)
        raw_ref[1, here, :] = jnp.sum(grad * normal, axis=0, keepdims=True)
        if active == "mixed":
            grad = grad * growth_ref[here, :]
        grad_ref[cells, :] = grad
        return carry

    lax.fori_loop(0, lines, one, 0, unroll=4)
    first, second = raw_ref[0] * gain_ref[...], raw_ref[1] * gain_ref[...]
    if active == "mixed":
        first, second = first * growth_ref[...], second * growth_ref[...]
    write_totals(first, second, same_ref, totals_ref, next_ref, prev_ref)
    next_ref[0:W, :] = grad_ref[tokens - W :, :]
    prev_ref[0:W, :] = grad_ref[0:W, :]


def gradient_sums(parts, value, stats_found, gain, shift, same, mixed=None, active=None):
    tokens, width = value.shape
    operands = [*parts, value, stats_found, gain, shift, same]
    if mixed is not None:
        operands += list(mixed)
        active = "mixed"
    return pl.pallas_call(
        functools.partial(sums_body, len(parts), active),
        out_shape=(
            jax.ShapeDtypeStruct((tokens, width), F32),
            jax.ShapeDtypeStruct((2, tokens // W, width), F32),
        )
        + stats_shapes(tokens // W, width),
        compiler_params=params(),
        cost_estimate=cost(tokens * width * 20, tokens * width * 14, tokens * width),
        name="gradient_sums",
    )(*operands)


def norm_gradient(grad, value, line, stats_ref, mean_ref, gain_ref):
    here = pl.ds(line, 1)
    scale = stats_ref[1, here, :]
    normal = (value - stats_ref[0, here, :]) * scale
    return scale * (grad * gain_ref[...] - mean_ref[0, here, :] - normal * mean_ref[1, here, :])


def taps_body(based, ids, *refs):
    grad_ref, value_ref, value_before, value_after, stats_ref, totals_ref = refs[:6]
    before_ref, after_ref, rows_ref, gain_ref = refs[6:10]
    refs = refs[10:]
    if based:
        base_ref, base_before, base_after = refs[:3]
        refs = refs[3:]
    map_ref = refs[0]
    refs = refs[1:]
    if based:
        full_ref = refs[0]
        refs = refs[1:]
    taps_ref = refs[0]
    refs = refs[1:]
    same_core, other_core, wide_ref, mean_ref = refs
    tokens, width = grad_ref.shape
    lines = tokens // W
    padded = tokens + 2 * W

    @pl.when(pl.program_id(0) == 0)
    def _():
        mean_ref[0], mean_ref[1] = crop_means(totals_ref, before_ref, after_ref, rows_ref)

        def one(line, carry):
            start = pl.multiple_of(line * W, W)
            cells = pl.ds(start, W)
            found = norm_gradient(
                grad_ref[cells, :], value_ref[cells, :], line, stats_ref, mean_ref, gain_ref
            )
            if based:
                found = found + base_ref[cells, :].astype(F32)
                full_ref[cells, :] = found
            wide_ref[pl.ds(start + W, W), :] = found
            return carry

        lax.fori_loop(0, lines, one, 0, unroll=4)
        for edge_ref, edge_value, line, start in (
            (before_ref, value_before, 0, 0),
            (after_ref, value_after, lines - 1, padded - W),
        ):
            found = norm_gradient(
                edge_ref[0:W, :], edge_value[0:W, :], line, stats_ref, mean_ref, gain_ref
            )
            if based:
                found = found + (base_before if line == 0 else base_after)[0:W, :].astype(F32)
            wide_ref[start : start + W, :] = found

        column = lax.broadcasted_iota(jnp.int32, (W, width), 0)

        def spread_row(line, carry):
            start = pl.multiple_of(line * W, W)
            target = pl.ds(start, W)
            for up in range(3):
                mask = rows_ref[up, pl.ds(line, 1), :]
                values = wide_ref[pl.ds(start + up * W, W), :] * mask
                left = jnp.where(column > 0, pltpu.roll(values, 1, 0), 0.0)
                right = jnp.where(column < W - 1, pltpu.roll(values, W - 1, 0), 0.0)
                for side, moved in enumerate((left, values, right)):
                    tap = 8 - (3 * up + side)
                    taps_ref[target, tap * width : (tap + 1) * width] = moved.astype(BF)
            return carry

        lax.fori_loop(0, lines, spread_row, 0, unroll=2)

    core = ids[ids.shape[0] - 1]
    write_products(taps_ref, map_ref, core, same_core, other_core)


def write_products(grad_ref, map_ref, core, same_core, other_core):
    tokens, width = same_core.shape[1:]
    for place, target in ((core, same_core), (1 - core, other_core)):
        rows = pl.ds(pl.multiple_of(place * width, width), width)
        for start in range(0, tokens, 512):
            here = slice(start, start + 512)
            target[0, here, :] = dot(grad_ref[here, :], map_ref[rows, :], NT).astype(BF)


def gradient_taps(
    grad, value, beside, stats_found, totals, before, after, rows, gain, base, ids, maps
):
    tokens, width = grad.shape
    lines = tokens // W
    count = ids.shape[0] - 1
    wide = 9 * width
    operands = [grad, value, *beside, stats_found, totals, before, after, rows, gain]
    if base is not None:
        operands += list(base)
    whole = lambda array: pl.BlockSpec(array.shape, lambda step, ids: (0,) * len(array.shape))
    in_specs = [whole(operand) for operand in operands]
    operands.append(maps)
    in_specs.append(pl.BlockSpec((2 * width, wide), lambda step, ids: (ids[step], 0)))
    taps_shape = jax.ShapeDtypeStruct((tokens, wide), BF)
    shapes, out_specs = [taps_shape], [whole(taps_shape)]
    if base is not None:
        full_shape = jax.ShapeDtypeStruct((tokens, width), F32)
        shapes, out_specs = [full_shape] + shapes, [whole(full_shape)] + out_specs
    shapes += [jax.ShapeDtypeStruct((count, tokens, width), BF)] * 2
    out_specs += [pl.BlockSpec((1, tokens, width), lambda step, ids: (step, 0, 0))] * 2
    return pl.pallas_call(
        functools.partial(taps_body, base is not None),
        out_shape=shapes,
        grid_spec=pltpu.PrefetchScalarGridSpec(
            num_scalar_prefetch=1,
            grid=(count,),
            in_specs=in_specs,
            out_specs=out_specs,
            scratch_shapes=[
                pltpu.VMEM((tokens + 2 * W, width), F32),
                pltpu.VMEM((2, lines, width), F32),
            ],
        ),
        compiler_params=params(),
        cost_estimate=cost(2 * tokens * count * width * wide, tokens * wide * 4),
        name="gradient_taps",
    )(ids, *operands)


def last_body(grad_ref, value_ref, stats_ref, totals_ref, before_ref, after_ref, rows_ref, gain_ref,
              base_ref, out_ref, mean_ref):
    mean_ref[0], mean_ref[1] = crop_means(totals_ref, before_ref, after_ref, rows_ref)

    def one(line, carry):
        cells = pl.ds(pl.multiple_of(line * W, W), W)
        out_ref[cells, :] = base_ref[cells, :] + norm_gradient(
            grad_ref[cells, :], value_ref[cells, :], line, stats_ref, mean_ref, gain_ref
        )
        return carry

    lax.fori_loop(0, grad_ref.shape[0] // W, one, 0, unroll=4)


def last_gradient(grad, value, stats_found, totals, before, after, rows, gain, base):
    tokens, width = grad.shape
    return pl.pallas_call(
        last_body,
        out_shape=jax.ShapeDtypeStruct((tokens, width), F32),
        scratch_shapes=[pltpu.VMEM((2, tokens // W, width), F32)],
        compiler_params=params(),
        cost_estimate=cost(tokens * width * 10, tokens * width * 16),
        name="last_gradient",
    )(grad, value, stats_found, totals, before, after, rows, gain, base)


def conv_body(prior, resid, ids, *refs):
    own_ref, mate_ref, kernel_ref, rows_ref = refs[:4]
    refs = refs[4:]
    prior_ref = refs[0] if prior else None
    refs = refs[1:] if prior else refs
    if resid:
        input_ref, bias_ref = refs[:2]
        refs = refs[2:]
    if resid is not None:
        same_ref, out_ref, totals_ref, next_ref, prev_ref, both_ref, sums_ref = refs
    else:
        out_ref, both_ref = refs
    tokens, width = out_ref.shape
    first = ids[1]
    for place, block in ((first, own_ref), (1 - first, mate_ref)):
        both_ref[:, pl.ds(pl.multiple_of(place * width, width), width)] = block[...]
    chunk = 256
    lines = chunk // W
    for start in range(0, tokens, chunk):
        here = slice(start, start + chunk)
        sides = [None] * 3
        for up in range(3):
            taps = kernel_ref[:, up * 3 * width : (up + 1) * 3 * width]
            part = dot(both_ref[up * W + start : up * W + start + chunk, :], taps, NN)
            part = part.reshape(lines, W, 3 * width)
            mask = rows_ref[up, start // W : start // W + lines, :][:, None, :]
            for side in range(3):
                piece = part[:, :, side * width : (side + 1) * width]
                piece = piece if up == 1 else piece * mask
                sides[side] = piece if sides[side] is None else sides[side] + piece
        sides = [piece.reshape(chunk, width) for piece in sides]
        column = lax.broadcasted_iota(jnp.int32, (chunk, width), 0) % W
        left = jnp.where(column > 0, pltpu.roll(sides[0], 1, 0), 0.0)
        right = jnp.where(column < W - 1, pltpu.roll(sides[2], chunk - 1, 0), 0.0)
        total = sides[1] + left + right
        if prior:
            total += prior_ref[here, :]
        if resid:
            total += input_ref[here, :] + bias_ref[...]
        out_ref[here, :] = total
    if resid is not None:
        square_sums(out_ref, sums_ref)
        write_totals(sums_ref[0], sums_ref[1], same_ref, totals_ref, next_ref, prev_ref)
        next_ref[0:W, :] = out_ref[tokens - W :, :]
        prev_ref[0:W, :] = out_ref[0:W, :]


def conv_pair(own, mate, ids, kernel, rows, prior=None, resid=None, same=None):
    padded, width = own.shape
    tokens = padded - 2 * W
    lines = tokens // W
    wide = 9 * width

    def whole(array):
        return pl.BlockSpec(array.shape, lambda step, ids: (0,) * len(array.shape))

    operands = [own, mate, kernel, rows]
    in_specs = [whole(own), whole(mate)]
    in_specs += [pl.BlockSpec((2 * width, wide), lambda step, ids: (ids[0], 0)), whole(rows)]
    for extra in ([prior] if prior is not None else []) + list(resid or ()):
        operands.append(extra)
        in_specs.append(whole(extra))
    shapes = [jax.ShapeDtypeStruct((tokens, width), F32)]
    scratch = [pltpu.VMEM((padded, 2 * width), BF)]
    if resid is not None:
        operands.append(same)
        in_specs.append(whole(same))
        shapes += list(stats_shapes(lines, width))
        scratch.append(pltpu.VMEM((2, lines, width), F32))
    found = pl.pallas_call(
        functools.partial(conv_body, prior is not None, None if resid is None else len(resid)),
        out_shape=shapes,
        grid_spec=pltpu.PrefetchScalarGridSpec(
            num_scalar_prefetch=1,
            grid=(1,),
            in_specs=in_specs,
            out_specs=[whole(shape) for shape in shapes],
            scratch_shapes=scratch,
        ),
        compiler_params=params(),
        cost_estimate=cost(4 * tokens * width * wide, 4 * width * wide + tokens * width * 12),
        name="conv_pair",
    )(ids, *operands)
    return found if resid is not None else found[0]


def convolve(blocks, far, ids, kernel, rows, same, resid):
    pairs = lax.axis_size("ch") // 2
    found = None
    for pair in range(pairs):
        place = jnp.stack([ids[2 * pair] // 2, ids[2 * pair] % 2])
        final = pair == pairs - 1
        found = conv_pair(
            blocks[2 * pair], blocks[2 * pair + 1], place, kernel, rows, found,
            resid if final else None, same,
        )
        if pair == 0 and far:
            found, *far = tie(found, *far)
            blocks = blocks + with_mates(far)
    return blocks, found


def project_body(count, width, ids, *refs):
    blocks = refs[:count]
    map_ref, out_ref, all_ref = refs[count:]

    @pl.when(pl.program_id(0) == 0)
    def _():
        for place in range(count):
            first = pl.multiple_of(ids[place] * width, width)
            all_ref[:, pl.ds(first, width)] = blocks[place][...]

    for start in range(0, out_ref.shape[0], 512):
        here = slice(start, start + 512)
        out_ref[here, :] = dot(all_ref[here, :], map_ref[...], NN).astype(out_ref.dtype)


def project(blocks, ids, maps, first, wide):
    count = len(blocks)
    tokens, width = blocks[0].shape
    depth = maps.shape[0]
    start = first // width
    return pl.pallas_call(
        functools.partial(project_body, count, width),
        out_shape=jax.ShapeDtypeStruct((tokens, wide), BF),
        grid_spec=pltpu.PrefetchScalarGridSpec(
            num_scalar_prefetch=1,
            grid=(wide // width,),
            in_specs=[pl.BlockSpec((tokens, width), lambda step, ids: (0, 0))] * count
            + [pl.BlockSpec((depth, width), lambda step, ids: (0, start + step))],
            out_specs=pl.BlockSpec((tokens, width), lambda step, ids: (0, step)),
            scratch_shapes=[pltpu.VMEM((tokens, depth), BF)],
        ),
        compiler_params=params(),
        cost_estimate=cost(2 * tokens * depth * wide, (tokens + depth) * wide * 2),
        name="project",
    )(ids, *blocks, maps)


def spread_body(ids, grad_ref, *refs):
    core = ids[ids.shape[0] - 1]
    write_products(grad_ref, refs[0], core, *refs[1:])


def spread(grad, ids, maps, first=0):
    tokens, wide = grad.shape
    count = ids.shape[0] - 1
    width = maps.shape[0] // lax.axis_size("ch")
    start = first // wide
    return pl.pallas_call(
        spread_body,
        out_shape=[jax.ShapeDtypeStruct((count, tokens, width), BF)] * 2,
        grid_spec=pltpu.PrefetchScalarGridSpec(
            num_scalar_prefetch=1,
            grid=(count,),
            in_specs=[
                pl.BlockSpec((tokens, wide), lambda step, ids: (0, 0)),
                pl.BlockSpec((2 * width, wide), lambda step, ids: (ids[step], start)),
            ],
            out_specs=[pl.BlockSpec((1, tokens, width), lambda step, ids: (step, 0, 0))] * 2,
        ),
        compiler_params=params(),
        cost_estimate=cost(4 * tokens * count * width * wide, (tokens + count * width) * wide * 2),
        name="spread",
    )(ids, grad, maps)


def outer_body(count, shift, ids, *refs):
    blocks = refs[:count]
    grad_ref, out_ref, turned_ref = refs[count:]
    tokens = grad_ref.shape[0]
    width = blocks[0].shape[1]

    @pl.when(pl.program_id(0) == 0)
    def _():
        for place in range(count):
            first = pl.multiple_of(ids[place] * width, width)
            turned_ref[pl.ds(first, width), :] = blocks[place][shift : shift + tokens, :].T

    depth = turned_ref.shape[0]
    for start in range(0, depth, 512):
        here = slice(start, start + 512)
        out_ref[here, :] = dot(turned_ref[here, :], grad_ref[...], NN).astype(BF)


def outer(blocks, ids, grad, shift=0, columns=None):
    count = len(blocks)
    tokens = grad.shape[0]
    first, wide = columns or (0, grad.shape[1])
    padded, width = blocks[0].shape
    depth = count * width
    tile = min(wide, 3 * width)
    before = first // tile
    return pl.pallas_call(
        functools.partial(outer_body, count, shift),
        out_shape=jax.ShapeDtypeStruct((depth, wide), BF),
        grid_spec=pltpu.PrefetchScalarGridSpec(
            num_scalar_prefetch=1,
            grid=(wide // tile,),
            in_specs=[pl.BlockSpec((padded, width), lambda step, ids: (0, 0))] * count
            + [pl.BlockSpec((tokens, tile), lambda step, ids: (0, before + step))],
            out_specs=pl.BlockSpec((depth, tile), lambda step, ids: (0, step)),
            scratch_shapes=[pltpu.VMEM((depth, tokens), BF)],
        ),
        compiler_params=params(),
        cost_estimate=cost(2 * tokens * depth * wide, (tokens + depth) * wide * 2),
        name="outer",
    )(ids, *blocks, grad)


def attention_body(
    heads, starts, counts, crops, query_ref, grad_ref, low_ref, own_ref, high_ref, ckey_ref,
    cval_ref, qcrop_ref, ccrop_ref, att_ref, dquery_ref, dlow_ref, down_ref, dhigh_ref, dckey_ref,
    dcval_ref, keys, values, keys_t, values_t, dkeys, dvalues, kcrop_ref, score_ref, prob_ref,
    cscore_ref, cprob_ref, qt_ref, qn_ref, gt_ref, gn_ref, att_t, dq_t,
):
    step = pl.program_id(0)
    window, width = keys.shape
    tokens = own_ref.shape[0]

    @pl.when(step == 0)
    def _():
        def label(line, carry):
            here = pl.ds(pl.multiple_of(line * W, W), W)
            kcrop_ref[here, :] = jnp.full((W, 128), crops[line], jnp.int32)
            return carry

        lax.fori_loop(0, window // W, label, 0, unroll=2)
        for place, target, turned in ((0, keys, keys_t), (1, values, values_t)):
            part = slice(place * width, (place + 1) * width)
            target[0:HALO, :] = low_ref[:, part]
            shifted = slice((place + 1) * width, (place + 2) * width)
            target[HALO : HALO + tokens, :] = own_ref[:, shifted]
            target[HALO + tokens : 2 * HALO + tokens, :] = high_ref[:, part]
            rest = window - 2 * HALO - tokens
            target[2 * HALO + tokens :, :] = jnp.zeros((rest, width), BF)
            for place in range(0, window, KB):
                turned[:, place : place + KB] = target[place : place + KB, :].T
        dkeys[...] = jnp.zeros_like(dkeys)
        dvalues[...] = jnp.zeros_like(dvalues)
        dckey_ref[...] = jnp.zeros_like(dckey_ref)
        dcval_ref[...] = jnp.zeros_like(dcval_ref)

    first = starts[step]
    blocks = counts[step]
    query = (query_ref[...].astype(F32) * (HEAD_DIM**-0.5)).astype(BF)
    query_t = query.T
    grad_t = grad_ref[...].T
    lane = lax.broadcasted_iota(jnp.int32, (QB, width), 1)
    for head in range(heads):
        mine = slice(head * HEAD_DIM, (head + 1) * HEAD_DIM)
        qt_ref[head] = jnp.zeros((width, QB), BF)
        qt_ref[head, mine, :] = query_t[mine, :]
        gt_ref[head] = jnp.zeros((width, QB), BF)
        in_head = (lane >= head * HEAD_DIM) & (lane < (head + 1) * HEAD_DIM)
        qn_ref[head] = jnp.where(in_head, query, jnp.zeros_like(query))
    crop_row = qcrop_ref[...].reshape(1, QB)
    ccrop = ccrop_ref[...]
    same_context = jnp.concatenate([ccrop] * (QB // 128), axis=1) == crop_row

    def span(block):
        return pl.ds(pl.multiple_of(first + block * KB, 128), KB)

    largest = []
    for head in range(heads):
        scores = jnp.where(same_context, dot(ckey_ref[...], qt_ref[head], NN), NEGATIVE)
        cscore_ref[head] = scores
        largest.append(jnp.max(scores.reshape(-1, 8, QB), axis=0))

    def pass_one(block, carry):
        here = span(block)
        crops = kcrop_ref[here, :]
        same = jnp.concatenate([crops] * (QB // 128), axis=1) == crop_row
        rows = keys[here, :]
        out = []
        for head in range(heads):
            scores = jnp.where(same, dot(rows, qt_ref[head], NN), NEGATIVE)
            score_ref[head, block] = scores
            out.append(jnp.maximum(carry[head], jnp.max(scores.reshape(-1, 8, QB), axis=0)))
        return tuple(out)

    largest = lax.fori_loop(0, blocks, pass_one, tuple(largest))
    largest = [jnp.max(value, axis=0, keepdims=True) for value in largest]

    sums = []
    for head in range(heads):
        mine = slice(head * HEAD_DIM, (head + 1) * HEAD_DIM)
        prob = jnp.exp(cscore_ref[head] - largest[head])
        sums.append(jnp.sum(prob.reshape(-1, 8, QB), axis=0))
        low = prob.astype(BF)
        cprob_ref[head] = low
        att_t[mine, :] = dot(cval_ref[...], low, TN)[mine, :]

    def pass_two(block, carry):
        here = span(block)
        out = []
        for head in range(heads):
            mine = slice(head * HEAD_DIM, (head + 1) * HEAD_DIM)
            prob = jnp.exp(score_ref[head, block] - largest[head])
            out.append(carry[head] + jnp.sum(prob.reshape(-1, 8, QB), axis=0))
            low = prob.astype(BF)
            prob_ref[head, block] = low
            att_t[mine, :] += dot(values_t[mine, here], low, NN)
        return tuple(out)

    sums = lax.fori_loop(0, blocks, pass_two, tuple(sums))
    offsets = []
    for head in range(heads):
        mine = slice(head * HEAD_DIM, (head + 1) * HEAD_DIM)
        inverse = 1.0 / jnp.sum(sums[head], axis=0, keepdims=True)
        attended = att_t[mine, :] * inverse
        att_t[mine, :] = attended
        scaled = grad_t[mine, :].astype(F32) * inverse
        gt_ref[head, mine, :] = scaled.astype(BF)
        offsets.append(jnp.sum(scaled * attended, axis=0, keepdims=True))
        gn_ref[head] = gt_ref[head].T
    att_ref[...] = att_t[...].T.astype(BF)

    for head in range(heads):
        mine = slice(head * HEAD_DIM, (head + 1) * HEAD_DIM)
        prob = cprob_ref[head]
        slope = dot(cval_ref[...], gt_ref[head], NN)
        dscore = (prob.astype(F32) * (slope - offsets[head])).astype(BF)
        dcval_ref[...] += dot(prob, gn_ref[head], NN)
        dckey_ref[...] += dot(dscore, qn_ref[head], NN)
        dq_t[mine, :] = dot(ckey_ref[...], dscore, TN)[mine, :]

    def pass_three(block, carry):
        here = span(block)
        rows = values[here, :]
        value_sum = None
        key_sum = None
        for head in range(heads):
            mine = slice(head * HEAD_DIM, (head + 1) * HEAD_DIM)
            prob = prob_ref[head, block]
            slope = dot(rows, gt_ref[head], NN)
            dscore = (prob.astype(F32) * (slope - offsets[head])).astype(BF)
            value_part = dot(prob, gn_ref[head], NN)
            key_part = dot(dscore, qn_ref[head], NN)
            value_sum = value_part if value_sum is None else value_sum + value_part
            key_sum = key_part if key_sum is None else key_sum + key_part
            dq_t[mine, :] += dot(keys_t[mine, here], dscore, NN)
        dvalues[here, :] += value_sum
        dkeys[here, :] += key_sum
        return carry

    lax.fori_loop(0, blocks, pass_three, 0)
    dquery_ref[...] = (dq_t[...] * (HEAD_DIM**-0.5)).T.astype(BF)

    @pl.when(step == pl.num_programs(0) - 1)
    def _():
        for place, source in ((0, dkeys), (1, dvalues)):
            part = slice(place * width, (place + 1) * width)
            dlow_ref[:, part] = source[0:HALO, :].astype(BF)
            down_ref[:, part] = source[HALO : HALO + tokens, :]
            dhigh_ref[:, part] = source[HALO + tokens : 2 * HALO + tokens, :].astype(BF)


def attend(qkv, grad, low, high, ckey, cval, tables):
    starts, counts, crops, qcrop, ccrop = tables
    tokens, width = grad.shape
    heads = width // HEAD_DIM
    window = crops.shape[0] * W
    context = ckey.shape[0]
    most = ((QB // W + 2 * (CROP_ROWS - 1)) * W + 127 + KB - 1) // KB
    q_block = pl.BlockSpec((QB, width), lambda step, *_: (step, 0))

    def whole(array):
        return pl.BlockSpec(array.shape, lambda step, *_: (0,) * len(array.shape))

    full = [low, qkv, high, ckey, cval]
    shapes = (
        jax.ShapeDtypeStruct((tokens, width), BF),
        jax.ShapeDtypeStruct((tokens, width), BF),
        jax.ShapeDtypeStruct((HALO, 2 * width), BF),
        jax.ShapeDtypeStruct((tokens, 2 * width), F32),
        jax.ShapeDtypeStruct((HALO, 2 * width), BF),
        jax.ShapeDtypeStruct((context, width), F32),
        jax.ShapeDtypeStruct((context, width), F32),
    )
    flops = 12 * tokens * 1280 * width
    return pl.pallas_call(
        functools.partial(attention_body, heads),
        out_shape=shapes,
        grid_spec=pltpu.PrefetchScalarGridSpec(
            num_scalar_prefetch=3,
            grid=(tokens // QB,),
            in_specs=[q_block, q_block]
            + [whole(array) for array in full]
            + [pl.BlockSpec((1, 1, QB), lambda step, *_: (step, 0, 0)), whole(ccrop)],
            out_specs=[q_block, q_block] + [whole(shape) for shape in shapes[2:]],
            scratch_shapes=[
                pltpu.VMEM((window, width), BF),
                pltpu.VMEM((window, width), BF),
                pltpu.VMEM((width, window), BF),
                pltpu.VMEM((width, window), BF),
                pltpu.VMEM((window, width), F32),
                pltpu.VMEM((window, width), F32),
                pltpu.VMEM((window, 128), jnp.int32),
                pltpu.VMEM((heads, most, KB, QB), F32),
                pltpu.VMEM((heads, most, KB, QB), BF),
                pltpu.VMEM((heads, context, QB), F32),
                pltpu.VMEM((heads, context, QB), BF),
                pltpu.VMEM((heads, width, QB), BF),
                pltpu.VMEM((heads, QB, width), BF),
                pltpu.VMEM((heads, width, QB), BF),
                pltpu.VMEM((heads, QB, width), BF),
                pltpu.VMEM((width, QB), F32),
                pltpu.VMEM((width, QB), F32),
            ],
        ),
        compiler_params=params(),
        cost_estimate=cost(flops // 3, 20 * tokens * width, tokens * 1280 * heads),
        name="attend",
    )(starts, counts, crops, qkv, grad, *full, qcrop, ccrop)


def along_pix(value, by):
    size = lax.axis_size("pix")
    return lax.ppermute(value, "pix", [(i, i + by) for i in range(size) if 0 <= i + by < size])


def across_pix(value, bit):
    return lax.ppermute(value, "pix", [(i, i ^ bit) for i in range(lax.axis_size("pix"))])


def pix_sum(value):
    bit = 1
    while bit < lax.axis_size("pix"):
        value = value + across_pix(value, bit)
        bit *= 2
    return value


def to_mate(value):
    return lax.ppermute(value, "ch", [(i, i ^ 1) for i in range(lax.axis_size("ch"))])


def to_chip(value, by):
    size = lax.axis_size("ch")
    return lax.ppermute(value, "ch", [(i, (i + 2 * by) % size) for i in range(size)])


def gather_rows(value):
    return lax.all_gather(value, "pix", axis=0, tiled=True)


def scatter_rows(value):
    return lax.psum_scatter(value, "pix", scatter_dimension=0, tiled=True)


def block_ids():
    size = lax.axis_size("ch")
    here = lax.axis_index("ch")
    ids = [here, here ^ 1]
    for by in range(1, size // 2):
        other = lax.rem(here + size - 2 * by, size)
        ids += [other, other ^ 1]
    return jnp.stack(ids).astype(jnp.int32)


def chip_ids():
    size = lax.axis_size("ch")
    here = lax.axis_index("ch")
    chips = [lax.rem(here // 2 + by, size // 2) for by in range(1, size // 2)]
    home = jnp.stack([here // 2, here % 2]).astype(jnp.int32)
    return home, jnp.stack(chips + [here % 2]).astype(jnp.int32)


def tie(*values):
    return lax.optimization_barrier(values)


def far_blocks(value):
    return [to_chip(value, by) for by in range(1, lax.axis_size("ch") // 2)]


def with_mates(blocks):
    found = []
    for block in blocks:
        found += [block, to_mate(block)]
    return found


def gather_blocks(value):
    far = far_blocks(value)
    return [value, to_mate(value)] + with_mates(far)


def chip_sums(parts):
    own, mate = parts
    return [
        (own[i].astype(F32) + to_mate(mate[i]).astype(F32)).astype(BF) for i in range(own.shape[0])
    ]


def sent_sums(sums):
    return [to_chip(piece, by + 1) for by, piece in enumerate(sums)]


def home_parts(parts):
    return [parts[0][0], to_mate(parts[1][0])]


def unpack_rows(packed):
    lines = packed.shape[0]
    width = packed.shape[1] // W
    return packed.reshape(lines, width, W).transpose(0, 2, 1).reshape(lines * W, width)


def pack_rows(cells):
    width = cells.shape[1]
    lines = cells.shape[0] // W
    return cells.reshape(lines, W, width).transpose(0, 2, 1).reshape(lines, width * W)


def small(left, right):
    return jnp.dot(left, right, precision=HIGHEST)


def turned(left, right):
    return lax.dot_general(left, right, (TN, ((), ())), precision=HIGHEST)


def beside_rows(messages):
    to_next, to_prev = messages
    return along_pix(to_next, 1), along_pix(to_prev, -1)


def local(
    pixels,
    cotangent,
    crop_rows,
    condition,
    context,
    kernels,
    attention,
    embedding,
    gains,
    shifts,
    offsets,
):
    lines = pixels.shape[0]
    width = pixels.shape[1] // W
    tokens = lines * W
    depth_here = kernels.shape[0]
    crop_count = crop_rows.shape[0]
    place = lax.axis_index("pix")
    kernel_local = (
        kernels.reshape(depth_here, width, 18).transpose(0, 2, 1).reshape(depth_here, 18 * width)
    )
    maps_local = (
        attention.reshape(depth_here, width, 6).transpose(0, 2, 1).reshape(depth_here, 6 * width)
    )
    kernel_one = gather_rows(kernel_local[:, : 9 * width])
    two_local = kernel_local[:, 9 * width :]
    four = jnp.concatenate([maps_local[:, : 3 * width], maps_local[:, 5 * width :]], axis=1)
    embedding_local = (
        embedding.reshape(depth_here, width, 2).transpose(0, 2, 1).reshape(depth_here, 2 * width)
    )
    context_flat = context.reshape(-1, context.shape[2])
    own_rows = place * depth_here
    context_own = lax.dynamic_slice_in_dim(context_flat, own_rows, depth_here, axis=1)
    condition_own = lax.dynamic_slice_in_dim(condition, own_rows, depth_here, axis=1)
    summed = pix_sum(
        jnp.concatenate(
            [
                dot(condition_own, embedding_local, NN),
                dot(context_own, maps_local[:, 3 * width : 5 * width], NN),
            ],
            axis=0,
        )
    )
    embed_terms = summed[:crop_count]
    ckey = summed[crop_count:, :width].astype(BF)
    cval = summed[crop_count:, width:].astype(BF)
    bounds = jnp.cumsum(crop_rows)
    line = place * lines + jnp.arange(-(CROP_ROWS - 1), lines + CROP_ROWS - 1, dtype=jnp.int32)
    found = jnp.sum((line[:, None] >= bounds[None, :]).astype(jnp.int32), axis=1)
    crop_wide = jnp.where((line >= 0) & (line < bounds[-1]), found, -1)
    near = crop_wide[CROP_ROWS - 2 : CROP_ROWS + lines]
    crop_row = near[1:-1]
    same = (crop_row[:, None] == crop_row[None, :]).astype(F32)
    member = (crop_row[:, None] == jnp.arange(crop_count)[None, :]).astype(F32)
    sizes = jnp.sum(jnp.where(member > 0, crop_rows[None, :], 0), axis=1)
    rows = jnp.stack(
        [
            (near[:-2] == crop_row).astype(F32),
            jnp.ones((lines,), F32),
            (near[2:] == crop_row).astype(F32),
            (crop_row == near[0]).astype(F32),
            (crop_row == near[-1]).astype(F32),
            1.0 / (sizes * (W * GSIZE)).astype(F32),
        ]
    )
    rows = jnp.broadcast_to(rows[:, :, None], (6, lines, width))
    crop_end = jnp.sum(jnp.where(member > 0, bounds[None, :], 0), axis=1)
    crop_start = crop_end - sizes
    base = place * lines - (CROP_ROWS - 1)
    step = QB // W
    window_low = (crop_start[::step] - base) * W
    window_high = (crop_end[step - 1 :: step] - base) * W
    starts = window_low // 128 * 128
    counts = (window_high - starts + KB - 1) // KB
    window = -(-(2 * HALO + tokens + KB) // KB) * KB
    key_crop = jnp.pad(
        crop_wide, (0, window // W - crop_wide.shape[0]), constant_values=-2
    ).astype(jnp.int32)
    context_crop = jnp.broadcast_to(
        jnp.repeat(jnp.arange(crop_count, dtype=jnp.int32), CTX)[:, None], (crop_count * CTX, 128)
    )
    query_crop = jnp.repeat(crop_row, W).reshape(-1, 1, QB)
    tables = (starts.astype(jnp.int32), counts.astype(jnp.int32), key_crop, query_crop, context_crop)

    ids = block_ids()
    home, away = chip_ids()
    gain = [gains[i : i + 1] for i in range(3)]
    shift = [shifts[i : i + 1] for i in range(3)]
    inputs = unpack_rows(pixels).astype(F32)
    dy_low = unpack_rows(cotangent)
    dy_beside = along_pix(dy_low[-W:], 1), along_pix(dy_low[:W], -1)
    totals, *messages = stats(inputs, same)
    input_beside = beside_rows(messages)
    a_one, stats_one = norm(inputs, totals, *input_beside, rows, gain[0], shift[0])
    far = far_blocks(a_one)
    blocks = [a_one, to_mate(a_one)]
    blocks, kernel_one, two_local = tie(blocks, kernel_one, two_local)
    kernel_two = gather_rows(two_local)
    one_blocks, (c_one, totals, *messages) = convolve(blocks, far, ids, kernel_one, rows, same, ())
    growth = 1.0 + small(member, embed_terms[:, :width] + offsets[2])
    shift_add = small(member, embed_terms[:, width:] + offsets[3])
    mixed = (growth, shift_add)
    c_beside = beside_rows(messages)
    a_two, stats_two = norm(c_one, totals, *c_beside, rows, gain[1], shift[1], mixed)
    far = far_blocks(a_two)
    blocks = [a_two, to_mate(a_two)]
    blocks, kernel_two, four = tie(blocks, kernel_two, four)
    four = gather_rows(four)
    two_blocks, (resid, totals, *messages) = convolve(
        blocks, far, ids, kernel_two, rows, same, (inputs, offsets[0:1])
    )
    resid_beside = beside_rows(messages)
    n_three, stats_three = norm(
        resid, totals, *resid_beside, rows, gain[2], shift[2], active=None, wide=False
    )
    dy_low, n_three = tie(dy_low, n_three)
    three_blocks = gather_blocks(n_three)
    dy_blocks = gather_blocks(dy_low)
    qkv = project(three_blocks, ids, four, 0, 3 * width)
    first_dy, qkv = lax.optimization_barrier((dy_blocks[0], qkv))
    datt = project([first_dy] + dy_blocks[1:], ids, four, 3 * width, width)
    low = along_pix(qkv[tokens - HALO :, width:], 1)
    high = along_pix(qkv[:HALO, width:], -1)
    att, dquery, dlow, down, dhigh, dckey, dcval = attend(qkv, datt, low, high, ckey, cval, tables)
    from_prev, from_next = along_pix(dhigh, 1), along_pix(dlow, -1)
    arrived = sent_sums(chip_sums(spread(att, away, four, 3 * width)))
    result = resid + offsets[1:2]
    for piece in home_parts(spread(att, home, four, 3 * width)) + arrived:
        result = result + piece.astype(F32)
    result = pack_rows(result)
    dmap_out = outer(dy_blocks, ids, att)
    from_prev, from_next, result, dmap_out = tie(from_prev, from_next, result, dmap_out)
    gap = ((0, tokens - HALO), (0, 0)), ((tokens - HALO, 0), (0, 0))
    down = down + jnp.pad(from_prev.astype(F32), gap[0]) + jnp.pad(from_next.astype(F32), gap[1])
    dqkv = jnp.concatenate([dquery, down.astype(BF)], axis=1)
    sums_three = chip_sums(spread(dqkv, away, four))
    dqkv, sums_three = tie(dqkv, sums_three)
    arrived = sent_sums(sums_three)
    parts = spread(dqkv, home, four)
    dqkv, parts = tie(dqkv, parts)
    dmaps = jnp.concatenate([outer(three_blocks, ids, dqkv), dmap_out], axis=1)
    parts, arrived, dmaps = tie(home_parts(parts), arrived, dmaps)
    parts = parts + arrived
    dmaps = scatter_rows(dmaps)
    e_three, raw_three, totals, *messages = gradient_sums(
        parts, resid, stats_three, gain[2], shift[2], same
    )
    e_beside = beside_rows(messages)
    dresid, taps_two, *parts = gradient_taps(
        e_three, resid, resid_beside, stats_three, totals, *e_beside, rows, gain[2],
        (dy_low, *dy_beside), away, kernel_two,
    )
    sums_two = chip_sums(parts)
    taps_two, sums_two = tie(taps_two, sums_two)
    arrived = sent_sums(sums_two)
    parts = spread(taps_two, home, kernel_two)
    taps_two, parts = tie(taps_two, parts)
    dkernel_two = outer(two_blocks, ids, taps_two, W)
    parts, arrived, dkernel_two, dmaps = tie(home_parts(parts), arrived, dkernel_two, dmaps)
    parts = parts + arrived
    dkernel_two = scatter_rows(dkernel_two)
    e_two, raw_two, totals, *messages = gradient_sums(
        parts, c_one, stats_two, gain[1], shift[1], same, mixed
    )
    e_beside = beside_rows(messages)
    taps_one, *parts = gradient_taps(
        e_two, c_one, c_beside, stats_two, totals, *e_beside, rows, gain[1], None, away, kernel_one
    )
    sums_one = chip_sums(parts)
    taps_one, sums_one = tie(taps_one, sums_one)
    arrived = sent_sums(sums_one)
    parts = spread(taps_one, home, kernel_one)
    taps_one, parts = tie(taps_one, parts)
    dkernel_one = outer(one_blocks, ids, taps_one, W)
    parts, arrived, dkernel_one, dkernel_two = tie(
        home_parts(parts), arrived, dkernel_one, dkernel_two
    )
    parts = parts + arrived
    dkernel_one = scatter_rows(dkernel_one)
    demb = jnp.concatenate(
        [turned(member, raw_two[1] * gain[1] + raw_two[0] * shift[1]), turned(member, raw_two[0])]
    )
    e_one, raw_one, totals, *messages = gradient_sums(
        parts, inputs, stats_one, gain[0], shift[0], same, active="plain"
    )
    grad_pixels = last_gradient(
        e_one, inputs, stats_one, totals, *beside_rows(messages), rows, gain[0], dresid
    )
    sums = jnp.concatenate(
        [
            (raw_two[1] * growth).sum(0)[None],
            raw_three[1].sum(0)[None],
            (raw_two[0] * growth).sum(0)[None],
            raw_three[0].sum(0)[None],
            dresid.sum(0)[None],
            dy_low.astype(F32).sum(0)[None],
            jnp.zeros((2, width), F32),
            demb,
            dckey,
            dcval,
        ],
        axis=0,
    )
    sums = pix_sum(sums)
    last = pix_sum(raw_one.sum(1))
    grad_gains = jnp.concatenate([last[1:2], sums[0:2]])
    grad_shifts = jnp.concatenate([last[0:1], sums[2:4]])
    demb = sums[8 : 8 + 2 * crop_count].reshape(2, crop_count, width)
    grad_offsets = jnp.concatenate([sums[4:6], demb.sum(1)])
    dcontext = sums[8 + 2 * crop_count :].reshape(2, crop_count * CTX, width)
    own_condition = condition_own.astype(F32)
    grad_embedding = jnp.stack([turned(own_condition, demb[i]) for i in range(2)], axis=2)
    own_context = context_own.astype(F32)
    dcontext_maps = [turned(own_context, dcontext[i]) for i in range(2)]
    dmaps = dmaps.astype(F32).reshape(depth_here, 4, width)
    grad_attention = jnp.stack(
        [dmaps[:, 0], dmaps[:, 1], dmaps[:, 2], *dcontext_maps, dmaps[:, 3]], axis=2
    )
    dkernels = jnp.concatenate([dkernel_one, dkernel_two], axis=1)
    grad_kernels = dkernels.reshape(depth_here, 18, width).transpose(0, 2, 1)
    return (
        result,
        pack_rows(grad_pixels),
        grad_kernels.reshape(depth_here, 18 * width).astype(F32),
        grad_attention.reshape(depth_here, 6 * width),
        grad_embedding.reshape(depth_here, 2 * width),
        grad_gains,
        grad_shifts,
        grad_offsets,
    )


def solution(mesh):
    split = P("pix", "ch")
    tall = P(None, "ch")
    return jax.shard_map(
        local,
        mesh=mesh,
        in_specs=(split, split, P(), P(), P(), split, split, split, tall, tall, tall),
        out_specs=(split, split, split, split, split, tall, tall, tall),
        check_vma=False,
    )
```

```python
import functools

import jax
import jax.numpy as jnp
from jax import lax
from jax.experimental import pallas as pl
from jax.experimental.pallas import tpu as pltpu
from jax.sharding import PartitionSpec as P

HEAD_DIM = 64
W = 32
CROP_ROWS = 32
CTX = 4
GSIZE = 32
HALO = (CROP_ROWS - 1) * W
QB = 256
KB = 256

HIGHEST = lax.Precision.HIGHEST
EPSILON = 1e-05
NEGATIVE = -1e30
BF = jnp.bfloat16
F32 = jnp.float32
VMEM_LIMIT = 58 * 1024 * 1024


def dot(left, right, dims):
    return lax.dot_general(left, right, (dims, ((), ())), preferred_element_type=F32)


NN = ((1,), (0,))
NT = ((1,), (1,))
TN = ((0,), (0,))


def params(**more):
    return pltpu.CompilerParams(vmem_limit_bytes=VMEM_LIMIT, **more)


def cost(flops, moved, exps=0):
    return pl.CostEstimate(flops=flops, bytes_accessed=moved, transcendentals=exps)


WITH_PREV, WITH_NEXT, INVERSE = 3, 4, 5
EDGE = 40


def exact(left, right):
    return lax.dot_general(
        left, right, (NN, ((), ())), precision=HIGHEST, preferred_element_type=F32
    )


def write_totals(first, second, same_ref, totals_ref, next_ref, prev_ref):
    lines, width = first.shape
    row = lax.broadcasted_iota(jnp.int32, (width, width), 0) // GSIZE
    column = lax.broadcasted_iota(jnp.int32, (width, width), 1) // GSIZE
    group = (row == column).astype(F32)
    for place, value in ((0, first), (1, second)):
        total = exact(same_ref[...], exact(value, group))
        totals_ref[place] = total
        next_ref[W + place : W + place + 1, :] = total[lines - 1 : lines, :]
        prev_ref[W + place : W + place + 1, :] = total[0:1, :]
    for target in (next_ref, prev_ref):
        target[W + 2 : EDGE, :] = jnp.zeros((EDGE - W - 2, width), F32)


def crop_means(totals_ref, before_ref, after_ref, rows_ref):
    found = []
    for place in range(2):
        line = slice(W + place, W + place + 1)
        total = totals_ref[place] + rows_ref[WITH_PREV] * before_ref[line, :]
        total = total + rows_ref[WITH_NEXT] * after_ref[line, :]
        found.append(total * rows_ref[INVERSE])
    return found


def square_sums(value_ref, sums_ref):
    lines = sums_ref.shape[1]

    def one(line, carry):
        cells = value_ref[pl.ds(pl.multiple_of(line * W, W), W), :]
        sums_ref[0, pl.ds(line, 1), :] = jnp.sum(cells, axis=0, keepdims=True)
        sums_ref[1, pl.ds(line, 1), :] = jnp.sum(cells * cells, axis=0, keepdims=True)
        return carry

    lax.fori_loop(0, lines, one, 0, unroll=4)


def stats_shapes(lines, width):
    return (
        jax.ShapeDtypeStruct((2, lines, width), F32),
        jax.ShapeDtypeStruct((EDGE, width), F32),
        jax.ShapeDtypeStruct((EDGE, width), F32),
    )


def stats_body(value_ref, same_ref, totals_ref, next_ref, prev_ref, sums_ref):
    tokens = value_ref.shape[0]
    square_sums(value_ref, sums_ref)
    write_totals(sums_ref[0], sums_ref[1], same_ref, totals_ref, next_ref, prev_ref)
    next_ref[0:W, :] = value_ref[tokens - W :, :]
    prev_ref[0:W, :] = value_ref[0:W, :]


def stats(value, same):
    tokens, width = value.shape
    return pl.pallas_call(
        stats_body,
        out_shape=stats_shapes(tokens // W, width),
        scratch_shapes=[pltpu.VMEM((2, tokens // W, width), F32)],
        compiler_params=params(),
        cost_estimate=cost(tokens * width * 4, tokens * width * 4),
        name="stats",
    )(value, same)


def norm_body(active, wide, *refs):
    value_ref, totals_ref, before_ref, after_ref, rows_ref, gain_ref, shift_ref = refs[:7]
    refs = refs[7:]
    if active == "mixed":
        growth_ref, add_ref = refs[:2]
        refs = refs[2:]
    out_ref, stats_ref, scale_ref, bias_ref = refs
    lines = totals_ref.shape[1]
    mean, square = crop_means(totals_ref, before_ref, after_ref, rows_ref)
    scale = lax.rsqrt(square - mean * mean + EPSILON)
    stats_ref[0] = mean
    stats_ref[1] = scale
    if active == "mixed":
        scale_ref[...] = scale * gain_ref[...] * growth_ref[...]
        bias_ref[...] = shift_ref[...] * growth_ref[...] + add_ref[...]
    else:
        scale_ref[...] = scale * gain_ref[...]
        bias_ref[...] = jnp.broadcast_to(shift_ref[...], bias_ref.shape)

    def cells_of(cells, line):
        here = pl.ds(line, 1)
        value = (cells - stats_ref[0, here, :]) * scale_ref[here, :] + bias_ref[here, :]
        if active is not None:
            value = value / (1.0 + jnp.exp(-value))
        return value.astype(BF)

    base = W if wide else 0

    def one(line, carry):
        start = pl.multiple_of(line * W, W)
        out_ref[pl.ds(start + base, W), :] = cells_of(value_ref[pl.ds(start, W), :], line)
        return carry

    lax.fori_loop(0, lines, one, 0, unroll=4)
    if wide:
        out_ref[0:W, :] = cells_of(before_ref[0:W, :], 0)
        out_ref[(lines + 1) * W :, :] = cells_of(after_ref[0:W, :], lines - 1)


def norm(value, totals, before, after, rows, gain, shift, mixed=None, active="plain", wide=True):
    tokens, width = value.shape
    lines = tokens // W
    operands = [value, totals, before, after, rows, gain, shift]
    if mixed is not None:
        operands += list(mixed)
        active = "mixed"
    return pl.pallas_call(
        functools.partial(norm_body, active, wide),
        out_shape=(
            jax.ShapeDtypeStruct((tokens + (2 * W if wide else 0), width), BF),
            jax.ShapeDtypeStruct((2, lines, width), F32),
        ),
        scratch_shapes=[pltpu.VMEM((lines, width), F32), pltpu.VMEM((lines, width), F32)],
        compiler_params=params(),
        cost_estimate=cost(tokens * width * 12, tokens * width * 6, tokens * width),
        name="norm",
    )(*operands)


def sums_body(count, active, *refs):
    parts = refs[:count]
    value_ref, stats_ref, gain_ref, shift_ref, same_ref = refs[count : count + 5]
    refs = refs[count + 5 :]
    if active == "mixed":
        growth_ref, add_ref = refs[:2]
        refs = refs[2:]
    grad_ref, raw_ref, totals_ref, next_ref, prev_ref = refs
    tokens, width = value_ref.shape
    lines = tokens // W

    def one(line, carry):
        here = pl.ds(line, 1)
        cells = pl.ds(pl.multiple_of(line * W, W), W)
        grad = parts[0][cells, :].astype(F32)
        for part in parts[1:]:
            grad = grad + part[cells, :].astype(F32)
        normal = (value_ref[cells, :] - stats_ref[0, here, :]) * stats_ref[1, here, :]
        if active is not None:
            inner = normal * gain_ref[...] + shift_ref[...]
            if active == "mixed":
                inner = inner * growth_ref[here, :] + add_ref[here, :]
            sigmoid = 1.0 / (1.0 + jnp.exp(-inner))
            grad = grad * sigmoid * (1.0 + inner * (1.0 - sigmoid))
        raw_ref[0, here, :] = jnp.sum(grad, axis=0, keepdims=True)
        raw_ref[1, here, :] = jnp.sum(grad * normal, axis=0, keepdims=True)
        if active == "mixed":
            grad = grad * growth_ref[here, :]
        grad_ref[cells, :] = grad
        return carry

    lax.fori_loop(0, lines, one, 0, unroll=4)
    first, second = raw_ref[0] * gain_ref[...], raw_ref[1] * gain_ref[...]
    if active == "mixed":
        first, second = first * growth_ref[...], second * growth_ref[...]
    write_totals(first, second, same_ref, totals_ref, next_ref, prev_ref)
    next_ref[0:W, :] = grad_ref[tokens - W :, :]
    prev_ref[0:W, :] = grad_ref[0:W, :]


def gradient_sums(parts, value, stats_found, gain, shift, same, mixed=None, active=None):
    tokens, width = value.shape
    operands = [*parts, value, stats_found, gain, shift, same]
    if mixed is not None:
        operands += list(mixed)
        active = "mixed"
    return pl.pallas_call(
        functools.partial(sums_body, len(parts), active),
        out_shape=(
            jax.ShapeDtypeStruct((tokens, width), F32),
            jax.ShapeDtypeStruct((2, tokens // W, width), F32),
        )
        + stats_shapes(tokens // W, width),
        compiler_params=params(),
        cost_estimate=cost(tokens * width * 20, tokens * width * 14, tokens * width),
        name="gradient_sums",
    )(*operands)


def norm_gradient(grad, value, line, stats_ref, mean_ref, gain_ref):
    here = pl.ds(line, 1)
    scale = stats_ref[1, here, :]
    normal = (value - stats_ref[0, here, :]) * scale
    return scale * (grad * gain_ref[...] - mean_ref[0, here, :] - normal * mean_ref[1, here, :])


def write_taps(wide_ref, rows_ref, taps_ref):
    tokens = taps_ref.shape[0]
    width = wide_ref.shape[1]
    column = lax.broadcasted_iota(jnp.int32, (W, width), 0)

    def spread_row(line, carry):
        start = pl.multiple_of(line * W, W)
        target = pl.ds(start, W)
        for up in range(3):
            mask = rows_ref[up, pl.ds(line, 1), :]
            values = wide_ref[pl.ds(start + up * W, W), :].astype(F32) * mask
            left = jnp.where(column > 0, pltpu.roll(values, 1, 0), 0.0)
            right = jnp.where(column < W - 1, pltpu.roll(values, W - 1, 0), 0.0)
            for side, moved in enumerate((left, values, right)):
                tap = 8 - (3 * up + side)
                taps_ref[target, tap * width : (tap + 1) * width] = moved.astype(BF)
        return carry

    lax.fori_loop(0, tokens // W, spread_row, 0, unroll=2)


def taps_body(based, ids, *refs):
    grad_ref, value_ref, value_before, value_after, stats_ref, totals_ref = refs[:6]
    before_ref, after_ref, rows_ref, gain_ref = refs[6:10]
    refs = refs[10:]
    if based:
        base_ref, base_before, base_after = refs[:3]
        refs = refs[3:]
    map_ref = refs[0]
    refs = refs[1:]
    if based:
        full_ref = refs[0]
        refs = refs[1:]
    taps_ref = refs[0]
    refs = refs[1:]
    low_ref, same_core, other_core, wide_ref, mean_ref = refs
    tokens, width = grad_ref.shape
    lines = tokens // W
    padded = tokens + 2 * W

    @pl.when(pl.program_id(0) == 0)
    def _():
        mean_ref[0], mean_ref[1] = crop_means(totals_ref, before_ref, after_ref, rows_ref)

        def one(line, carry):
            start = pl.multiple_of(line * W, W)
            cells = pl.ds(start, W)
            found = norm_gradient(
                grad_ref[cells, :], value_ref[cells, :], line, stats_ref, mean_ref, gain_ref
            )
            if based:
                found = found + base_ref[cells, :].astype(F32)
                full_ref[cells, :] = found
            wide_ref[pl.ds(start + W, W), :] = found
            return carry

        lax.fori_loop(0, lines, one, 0, unroll=4)
        for edge_ref, edge_value, line, start in (
            (before_ref, value_before, 0, 0),
            (after_ref, value_after, lines - 1, padded - W),
        ):
            found = norm_gradient(
                edge_ref[0:W, :], edge_value[0:W, :], line, stats_ref, mean_ref, gain_ref
            )
            if based:
                found = found + (base_before if line == 0 else base_after)[0:W, :].astype(F32)
            wide_ref[start : start + W, :] = found

        write_taps(wide_ref, rows_ref, taps_ref)
        low_ref[...] = wide_ref[...].astype(BF)

    core = ids[ids.shape[0] - 1]
    write_products(taps_ref, map_ref, core, same_core, other_core)


def write_products(grad_ref, map_ref, core, same_core, other_core):
    tokens, width = same_core.shape[1:]
    for place, target in ((core, same_core), (1 - core, other_core)):
        rows = pl.ds(pl.multiple_of(place * width, width), width)
        for start in range(0, tokens, 512):
            here = slice(start, start + 512)
            target[0, here, :] = dot(grad_ref[here, :], map_ref[rows, :], NT).astype(BF)


def gradient_taps(
    grad, value, beside, stats_found, totals, before, after, rows, gain, base, ids, maps
):
    tokens, width = grad.shape
    lines = tokens // W
    count = ids.shape[0] - 1
    wide = 9 * width
    operands = [grad, value, *beside, stats_found, totals, before, after, rows, gain]
    if base is not None:
        operands += list(base)
    whole = lambda array: pl.BlockSpec(array.shape, lambda step, ids: (0,) * len(array.shape))
    in_specs = [whole(operand) for operand in operands]
    operands.append(maps)
    in_specs.append(pl.BlockSpec((2 * width, wide), lambda step, ids: (ids[step], 0)))
    taps_shape = jax.ShapeDtypeStruct((tokens, wide), BF)
    shapes, out_specs = [taps_shape], [whole(taps_shape)]
    if base is not None:
        full_shape = jax.ShapeDtypeStruct((tokens, width), F32)
        shapes, out_specs = [full_shape] + shapes, [whole(full_shape)] + out_specs
    low_shape = jax.ShapeDtypeStruct((tokens + 2 * W, width), BF)
    shapes.append(low_shape)
    out_specs.append(whole(low_shape))
    shapes += [jax.ShapeDtypeStruct((count, tokens, width), BF)] * 2
    out_specs += [pl.BlockSpec((1, tokens, width), lambda step, ids: (step, 0, 0))] * 2
    return pl.pallas_call(
        functools.partial(taps_body, base is not None),
        out_shape=shapes,
        grid_spec=pltpu.PrefetchScalarGridSpec(
            num_scalar_prefetch=1,
            grid=(count,),
            in_specs=in_specs,
            out_specs=out_specs,
            scratch_shapes=[
                pltpu.VMEM((tokens + 2 * W, width), F32),
                pltpu.VMEM((2, lines, width), F32),
            ],
        ),
        compiler_params=params(),
        cost_estimate=cost(2 * tokens * count * width * wide, tokens * wide * 4),
        name="gradient_taps",
    )(ids, *operands)


def last_body(grad_ref, value_ref, stats_ref, totals_ref, before_ref, after_ref, rows_ref, gain_ref,
              base_ref, out_ref, mean_ref):
    mean_ref[0], mean_ref[1] = crop_means(totals_ref, before_ref, after_ref, rows_ref)

    def one(line, carry):
        cells = pl.ds(pl.multiple_of(line * W, W), W)
        out_ref[cells, :] = base_ref[cells, :] + norm_gradient(
            grad_ref[cells, :], value_ref[cells, :], line, stats_ref, mean_ref, gain_ref
        )
        return carry

    lax.fori_loop(0, grad_ref.shape[0] // W, one, 0, unroll=4)


def last_gradient(grad, value, stats_found, totals, before, after, rows, gain, base):
    tokens, width = grad.shape
    return pl.pallas_call(
        last_body,
        out_shape=jax.ShapeDtypeStruct((tokens, width), F32),
        scratch_shapes=[pltpu.VMEM((2, tokens // W, width), F32)],
        compiler_params=params(),
        cost_estimate=cost(tokens * width * 10, tokens * width * 16),
        name="last_gradient",
    )(grad, value, stats_found, totals, before, after, rows, gain, base)


def conv_body(prior, resid, ids, *refs):
    own_ref, mate_ref, kernel_ref, rows_ref = refs[:4]
    refs = refs[4:]
    prior_ref = refs[0] if prior else None
    refs = refs[1:] if prior else refs
    if resid:
        input_ref, bias_ref = refs[:2]
        refs = refs[2:]
    if resid is not None:
        same_ref, out_ref, totals_ref, next_ref, prev_ref, both_ref, sums_ref = refs
    else:
        out_ref, both_ref = refs
    tokens, width = out_ref.shape
    first = ids[1]
    for place, block in ((first, own_ref), (1 - first, mate_ref)):
        both_ref[:, pl.ds(pl.multiple_of(place * width, width), width)] = block[...]
    chunk = 256
    lines = chunk // W
    for start in range(0, tokens, chunk):
        here = slice(start, start + chunk)
        sides = [None] * 3
        for up in range(3):
            taps = kernel_ref[:, up * 3 * width : (up + 1) * 3 * width]
            part = dot(both_ref[up * W + start : up * W + start + chunk, :], taps, NN)
            part = part.reshape(lines, W, 3 * width)
            mask = rows_ref[up, start // W : start // W + lines, :][:, None, :]
            for side in range(3):
                piece = part[:, :, side * width : (side + 1) * width]
                piece = piece if up == 1 else piece * mask
                sides[side] = piece if sides[side] is None else sides[side] + piece
        sides = [piece.reshape(chunk, width) for piece in sides]
        column = lax.broadcasted_iota(jnp.int32, (chunk, width), 0) % W
        left = jnp.where(column > 0, pltpu.roll(sides[0], 1, 0), 0.0)
        right = jnp.where(column < W - 1, pltpu.roll(sides[2], chunk - 1, 0), 0.0)
        total = sides[1] + left + right
        if prior:
            total += prior_ref[here, :]
        if resid:
            total += input_ref[here, :] + bias_ref[...]
        out_ref[here, :] = total
    if resid is not None:
        square_sums(out_ref, sums_ref)
        write_totals(sums_ref[0], sums_ref[1], same_ref, totals_ref, next_ref, prev_ref)
        next_ref[0:W, :] = out_ref[tokens - W :, :]
        prev_ref[0:W, :] = out_ref[0:W, :]


def conv_pair(own, mate, ids, kernel, rows, prior=None, resid=None, same=None):
    padded, width = own.shape
    tokens = padded - 2 * W
    lines = tokens // W
    wide = 9 * width

    def whole(array):
        return pl.BlockSpec(array.shape, lambda step, ids: (0,) * len(array.shape))

    operands = [own, mate, kernel, rows]
    in_specs = [whole(own), whole(mate)]
    in_specs += [pl.BlockSpec((2 * width, wide), lambda step, ids: (ids[0], 0)), whole(rows)]
    for extra in ([prior] if prior is not None else []) + list(resid or ()):
        operands.append(extra)
        in_specs.append(whole(extra))
    shapes = [jax.ShapeDtypeStruct((tokens, width), F32)]
    scratch = [pltpu.VMEM((padded, 2 * width), BF)]
    if resid is not None:
        operands.append(same)
        in_specs.append(whole(same))
        shapes += list(stats_shapes(lines, width))
        scratch.append(pltpu.VMEM((2, lines, width), F32))
    found = pl.pallas_call(
        functools.partial(conv_body, prior is not None, None if resid is None else len(resid)),
        out_shape=shapes,
        grid_spec=pltpu.PrefetchScalarGridSpec(
            num_scalar_prefetch=1,
            grid=(1,),
            in_specs=in_specs,
            out_specs=[whole(shape) for shape in shapes],
            scratch_shapes=scratch,
        ),
        compiler_params=params(),
        cost_estimate=cost(4 * tokens * width * wide, 4 * width * wide + tokens * width * 12),
        name="conv_pair",
    )(ids, *operands)
    return found if resid is not None else found[0]


def convolve(blocks, ids, kernel, rows, same, resid):
    found = None
    for pair in range(len(blocks) // 2):
        place = jnp.stack([ids[2 * pair] // 2, ids[2 * pair] % 2])
        final = 2 * pair + 2 == len(blocks)
        found = conv_pair(
            blocks[2 * pair], blocks[2 * pair + 1], place, kernel, rows, found,
            resid if final else None, same,
        )
    return found


def project_body(count, width, ids, *refs):
    blocks = refs[:count]
    map_ref, out_ref, all_ref = refs[count:]

    @pl.when(pl.program_id(0) == 0)
    def _():
        for place in range(count):
            first = pl.multiple_of(ids[place] * width, width)
            all_ref[:, pl.ds(first, width)] = blocks[place][...]

    for start in range(0, out_ref.shape[0], 512):
        here = slice(start, start + 512)
        out_ref[here, :] = dot(all_ref[here, :], map_ref[...], NN).astype(out_ref.dtype)


def project(blocks, ids, maps, first, wide):
    count = len(blocks)
    tokens, width = blocks[0].shape
    depth = maps.shape[0]
    start = first // width
    return pl.pallas_call(
        functools.partial(project_body, count, width),
        out_shape=jax.ShapeDtypeStruct((tokens, wide), BF),
        grid_spec=pltpu.PrefetchScalarGridSpec(
            num_scalar_prefetch=1,
            grid=(wide // width,),
            in_specs=[pl.BlockSpec((tokens, width), lambda step, ids: (0, 0))] * count
            + [pl.BlockSpec((depth, width), lambda step, ids: (0, start + step))],
            out_specs=pl.BlockSpec((tokens, width), lambda step, ids: (0, step)),
            scratch_shapes=[pltpu.VMEM((tokens, depth), BF)],
        ),
        compiler_params=params(),
        cost_estimate=cost(2 * tokens * depth * wide, (tokens + depth) * wide * 2),
        name="project",
    )(ids, *blocks, maps)


def spread_body(ids, grad_ref, *refs):
    core = ids[ids.shape[0] - 1]
    write_products(grad_ref, refs[0], core, *refs[1:])


def spread(grad, ids, maps, first=0):
    tokens, wide = grad.shape
    count = ids.shape[0] - 1
    width = maps.shape[0] // lax.axis_size("ch")
    start = first // wide
    return pl.pallas_call(
        spread_body,
        out_shape=[jax.ShapeDtypeStruct((count, tokens, width), BF)] * 2,
        grid_spec=pltpu.PrefetchScalarGridSpec(
            num_scalar_prefetch=1,
            grid=(count,),
            in_specs=[
                pl.BlockSpec((tokens, wide), lambda step, ids: (0, 0)),
                pl.BlockSpec((2 * width, wide), lambda step, ids: (ids[step], start)),
            ],
            out_specs=[pl.BlockSpec((1, tokens, width), lambda step, ids: (step, 0, 0))] * 2,
        ),
        compiler_params=params(),
        cost_estimate=cost(4 * tokens * count * width * wide, (tokens + count * width) * wide * 2),
        name="spread",
    )(ids, grad, maps)


def half_own_body(count, ids, *refs):
    blocks = refs[:count]
    grad_ref, out_ref, turned_ref = refs[count:]
    tokens = grad_ref.shape[0]
    half = blocks[0].shape[1] // 2

    @pl.when(pl.program_id(0) == 0)
    def _():
        lanes = pl.ds(pl.multiple_of(ids[count] * half, half), half)
        for place in range(count):
            rows = pl.ds(pl.multiple_of(ids[place] * half, half), half)
            turned_ref[rows, :] = blocks[place][W : W + tokens, lanes].T

    out_ref[...] = dot(turned_ref[...], grad_ref[...], NN)


def half_own(blocks, ids, grad):
    count = len(blocks)
    tokens, wide = grad.shape
    padded, width = blocks[0].shape
    depth, tile = count * width // 2, 3 * width
    return pl.pallas_call(
        functools.partial(half_own_body, count),
        out_shape=jax.ShapeDtypeStruct((depth, wide), F32),
        grid_spec=pltpu.PrefetchScalarGridSpec(
            num_scalar_prefetch=1,
            grid=(wide // tile,),
            in_specs=[pl.BlockSpec((padded, width), lambda step, ids: (0, 0))] * count
            + [pl.BlockSpec((tokens, tile), lambda step, ids: (0, step))],
            out_specs=pl.BlockSpec((depth, tile), lambda step, ids: (0, step)),
            scratch_shapes=[pltpu.VMEM((depth, tokens), BF)],
        ),
        compiler_params=params(),
        cost_estimate=cost(2 * tokens * depth * wide, (tokens + 2 * depth) * wide * 2),
        name="half_own",
    )(ids, *blocks, grad)


def half_beside_body(count, ids, *refs):
    pairs = refs[:2]
    wide_ref, rows_ref, own_ref, out_ref, turned_ref, taps_ref = refs[2:]
    tokens = taps_ref.shape[0]
    half = pairs[0].shape[1] // (count // 2)
    tile = out_ref.shape[1]
    step = pl.program_id(0)

    @pl.when(step == 0)
    def _():
        write_taps(wide_ref, rows_ref, taps_ref)
        for place in range(count):
            rows = pl.ds(pl.multiple_of(ids[place] * half, half), half)
            lanes = slice(place // 2 * half, (place // 2 + 1) * half)
            turned_ref[rows, :] = pairs[place % 2][:, lanes].T

    columns = pl.ds(pl.multiple_of(step * tile, tile), tile)
    out_ref[...] = (own_ref[...] + dot(turned_ref[...], taps_ref[:, columns], NN)).astype(BF)


def half_beside(pairs, ids, wide_grad, row_masks, own):
    count = ids.shape[0] - 1
    tokens, both = pairs[0].shape
    depth, wide = own.shape
    padded, width = wide_grad.shape
    tile = 3 * width
    once = lambda step, ids: (0, 0)
    return pl.pallas_call(
        functools.partial(half_beside_body, count),
        out_shape=jax.ShapeDtypeStruct((depth, wide), BF),
        grid_spec=pltpu.PrefetchScalarGridSpec(
            num_scalar_prefetch=1,
            grid=(wide // tile,),
            in_specs=[
                pl.BlockSpec((tokens, both), once),
                pl.BlockSpec((tokens, both), once),
                pl.BlockSpec((padded, width), once),
                pl.BlockSpec(row_masks.shape, lambda step, ids: (0, 0, 0)),
                pl.BlockSpec((depth, tile), lambda step, ids: (0, step)),
            ],
            out_specs=pl.BlockSpec((depth, tile), lambda step, ids: (0, step)),
            scratch_shapes=[pltpu.VMEM((depth, tokens), BF), pltpu.VMEM((tokens, wide), BF)],
        ),
        compiler_params=params(),
        cost_estimate=cost(2 * tokens * depth * wide, (tokens + 3 * depth) * wide * 2),
        name="half_beside",
    )(ids, *pairs, wide_grad, row_masks, own)


def outer_body(count, shift, ids, *refs):
    blocks = refs[:count]
    grad_ref, out_ref, turned_ref = refs[count:]
    tokens = grad_ref.shape[0]
    width = blocks[0].shape[1]

    @pl.when(pl.program_id(0) == 0)
    def _():
        for place in range(count):
            first = pl.multiple_of(ids[place] * width, width)
            turned_ref[pl.ds(first, width), :] = blocks[place][shift : shift + tokens, :].T

    depth = turned_ref.shape[0]
    for start in range(0, depth, 512):
        here = slice(start, start + 512)
        out_ref[here, :] = dot(turned_ref[here, :], grad_ref[...], NN).astype(BF)


def outer(blocks, ids, grad, shift=0, columns=None):
    count = len(blocks)
    tokens = grad.shape[0]
    first, wide = columns or (0, grad.shape[1])
    padded, width = blocks[0].shape
    depth = count * width
    tile = min(wide, 3 * width)
    before = first // tile
    return pl.pallas_call(
        functools.partial(outer_body, count, shift),
        out_shape=jax.ShapeDtypeStruct((depth, wide), BF),
        grid_spec=pltpu.PrefetchScalarGridSpec(
            num_scalar_prefetch=1,
            grid=(wide // tile,),
            in_specs=[pl.BlockSpec((padded, width), lambda step, ids: (0, 0))] * count
            + [pl.BlockSpec((tokens, tile), lambda step, ids: (0, before + step))],
            out_specs=pl.BlockSpec((depth, tile), lambda step, ids: (0, step)),
            scratch_shapes=[pltpu.VMEM((depth, tokens), BF)],
        ),
        compiler_params=params(),
        cost_estimate=cost(2 * tokens * depth * wide, (tokens + depth) * wide * 2),
        name="outer",
    )(ids, *blocks, grad)


def attention_body(
    heads, starts, counts, crops, query_ref, grad_ref, low_ref, own_ref, high_ref, ckey_ref,
    cval_ref, qcrop_ref, ccrop_ref, att_ref, dquery_ref, dlow_ref, down_ref, dhigh_ref, dckey_ref,
    dcval_ref, keys, values, keys_t, values_t, dkeys, dvalues, kcrop_ref, score_ref, prob_ref,
    cscore_ref, cprob_ref, slope_ref, cslope_ref, qt_ref, qn_ref, gt_ref, gn_ref, att_t, dq_t,
):
    step = pl.program_id(0)
    window, width = keys.shape
    tokens = own_ref.shape[0]

    @pl.when(step == 0)
    def _():
        def label(line, carry):
            here = pl.ds(pl.multiple_of(line * W, W), W)
            kcrop_ref[here, :] = jnp.full((W, 128), crops[line], jnp.int32)
            return carry

        lax.fori_loop(0, window // W, label, 0, unroll=2)
        for place, target, turned in ((0, keys, keys_t), (1, values, values_t)):
            part = slice(place * width, (place + 1) * width)
            target[0:HALO, :] = low_ref[:, part]
            shifted = slice((place + 1) * width, (place + 2) * width)
            target[HALO : HALO + tokens, :] = own_ref[:, shifted]
            target[HALO + tokens : 2 * HALO + tokens, :] = high_ref[:, part]
            rest = window - 2 * HALO - tokens
            target[2 * HALO + tokens :, :] = jnp.zeros((rest, width), BF)
            for place in range(0, window, KB):
                turned[:, place : place + KB] = target[place : place + KB, :].T
        dkeys[...] = jnp.zeros_like(dkeys)
        dvalues[...] = jnp.zeros_like(dvalues)
        dckey_ref[...] = jnp.zeros_like(dckey_ref)
        dcval_ref[...] = jnp.zeros_like(dcval_ref)

    first = starts[step]
    blocks = counts[step]
    query = (query_ref[...].astype(F32) * (HEAD_DIM**-0.5)).astype(BF)
    query_t = query.T
    grad_t = grad_ref[...].T
    lane = lax.broadcasted_iota(jnp.int32, (QB, width), 1)
    zero = jnp.zeros((width, QB), BF)
    mine = [slice(head * HEAD_DIM, (head + 1) * HEAD_DIM) for head in range(heads)]
    part = [slice(head * QB, (head + 1) * QB) for head in range(heads)]
    for head in range(heads):
        qt_ref[:, part[head]] = zero
        qt_ref[mine[head], part[head]] = query_t[mine[head], :]
        gt_ref[:, part[head]] = zero
        in_head = (lane >= head * HEAD_DIM) & (lane < (head + 1) * HEAD_DIM)
        qn_ref[part[head], :] = jnp.where(in_head, query, jnp.zeros_like(query))
    crop_row = qcrop_ref[...].reshape(1, QB)
    same_context = jnp.concatenate([ccrop_ref[...]] * (QB // 128), axis=1) == crop_row

    def span(block):
        return pl.ds(pl.multiple_of(first + block * KB, 128), KB)

    def folded(values, combine):
        return combine(values.reshape(-1, 8, QB), axis=0)

    largest = []
    products = dot(ckey_ref[...], qt_ref[...], NN)
    for head in range(heads):
        scores = jnp.where(same_context, products[:, part[head]], NEGATIVE)
        cscore_ref[:, part[head]] = scores
        largest.append(folded(scores, jnp.max))

    def pass_one(block, carry):
        here = span(block)
        same = jnp.concatenate([kcrop_ref[here, :]] * (QB // 128), axis=1) == crop_row
        products = dot(keys[here, :], qt_ref[...], NN)
        out = []
        for head in range(heads):
            scores = jnp.where(same, products[:, part[head]], NEGATIVE)
            score_ref[block, :, part[head]] = scores
            out.append(jnp.maximum(carry[head], folded(scores, jnp.max)))
        return tuple(out)

    largest = lax.fori_loop(0, blocks, pass_one, tuple(largest))
    largest = [jnp.max(value, axis=0, keepdims=True) for value in largest]

    sums = []
    for head in range(heads):
        prob = jnp.exp(cscore_ref[:, part[head]] - largest[head])
        sums.append(folded(prob, jnp.sum))
        low = prob.astype(BF)
        cprob_ref[:, part[head]] = low
        att_t[mine[head], :] = dot(cval_ref[...], low, TN)[mine[head], :]

    def pass_two(block, carry):
        here = span(block)
        out = []
        for head in range(heads):
            prob = jnp.exp(score_ref[block, :, part[head]] - largest[head])
            out.append(carry[head] + folded(prob, jnp.sum))
            low = prob.astype(BF)
            prob_ref[block, :, part[head]] = low
            att_t[mine[head], :] += dot(values_t[mine[head], here], low, NN)
        return tuple(out)

    sums = lax.fori_loop(0, blocks, pass_two, tuple(sums))
    offsets = []
    for head in range(heads):
        inverse = 1.0 / jnp.sum(sums[head], axis=0, keepdims=True)
        attended = att_t[mine[head], :] * inverse
        att_t[mine[head], :] = attended
        scaled = grad_t[mine[head], :].astype(F32) * inverse
        gt_ref[mine[head], part[head]] = scaled.astype(BF)
        offsets.append(jnp.sum(scaled * attended, axis=0, keepdims=True))
        gn_ref[part[head], :] = gt_ref[:, part[head]].T
    att_ref[...] = att_t[...].T.astype(BF)

    slope = dot(cval_ref[...], gt_ref[...], NN)
    for head in range(heads):
        prob = cprob_ref[:, part[head]].astype(F32)
        dscore = (prob * (slope[:, part[head]] - offsets[head])).astype(BF)
        cslope_ref[:, part[head]] = dscore
        dq_t[mine[head], :] = dot(ckey_ref[...], dscore, TN)[mine[head], :]
    dcval_ref[...] += dot(cprob_ref[...], gn_ref[...], NN)
    dckey_ref[...] += dot(cslope_ref[...], qn_ref[...], NN)

    def pass_three(block, carry):
        here = span(block)
        slope = dot(values[here, :], gt_ref[...], NN)
        for head in range(heads):
            prob = prob_ref[block, :, part[head]].astype(F32)
            dscore = (prob * (slope[:, part[head]] - offsets[head])).astype(BF)
            slope_ref[:, part[head]] = dscore
            dq_t[mine[head], :] += dot(keys_t[mine[head], here], dscore, NN)
        dvalues[here, :] += dot(prob_ref[block], gn_ref[...], NN)
        dkeys[here, :] += dot(slope_ref[...], qn_ref[...], NN)
        return carry

    lax.fori_loop(0, blocks, pass_three, 0)
    dquery_ref[...] = (dq_t[...] * (HEAD_DIM**-0.5)).T.astype(BF)

    @pl.when(step == pl.num_programs(0) - 1)
    def _():
        for place, source in ((0, dkeys), (1, dvalues)):
            part = slice(place * width, (place + 1) * width)
            dlow_ref[:, part] = source[0:HALO, :].astype(BF)
            down_ref[:, part] = source[HALO : HALO + tokens, :]
            dhigh_ref[:, part] = source[HALO + tokens : 2 * HALO + tokens, :].astype(BF)


def attend(qkv, grad, low, high, ckey, cval, tables):
    starts, counts, crops, qcrop, ccrop = tables
    tokens, width = grad.shape
    heads = width // HEAD_DIM
    window = crops.shape[0] * W
    context = ckey.shape[0]
    most = ((QB // W + 2 * (CROP_ROWS - 1)) * W + 127 + KB - 1) // KB
    q_block = pl.BlockSpec((QB, width), lambda step, *_: (step, 0))

    def whole(array):
        return pl.BlockSpec(array.shape, lambda step, *_: (0,) * len(array.shape))

    full = [low, qkv, high, ckey, cval]
    shapes = (
        jax.ShapeDtypeStruct((tokens, width), BF),
        jax.ShapeDtypeStruct((tokens, width), BF),
        jax.ShapeDtypeStruct((HALO, 2 * width), BF),
        jax.ShapeDtypeStruct((tokens, 2 * width), F32),
        jax.ShapeDtypeStruct((HALO, 2 * width), BF),
        jax.ShapeDtypeStruct((context, width), F32),
        jax.ShapeDtypeStruct((context, width), F32),
    )
    flops = 12 * tokens * 1280 * width
    return pl.pallas_call(
        functools.partial(attention_body, heads),
        out_shape=shapes,
        grid_spec=pltpu.PrefetchScalarGridSpec(
            num_scalar_prefetch=3,
            grid=(tokens // QB,),
            in_specs=[q_block, q_block]
            + [whole(array) for array in full]
            + [pl.BlockSpec((1, 1, QB), lambda step, *_: (step, 0, 0)), whole(ccrop)],
            out_specs=[q_block, q_block] + [whole(shape) for shape in shapes[2:]],
            scratch_shapes=[
                pltpu.VMEM((window, width), BF),
                pltpu.VMEM((window, width), BF),
                pltpu.VMEM((width, window), BF),
                pltpu.VMEM((width, window), BF),
                pltpu.VMEM((window, width), F32),
                pltpu.VMEM((window, width), F32),
                pltpu.VMEM((window, 128), jnp.int32),
                pltpu.VMEM((most, KB, heads * QB), F32),
                pltpu.VMEM((most, KB, heads * QB), BF),
                pltpu.VMEM((context, heads * QB), F32),
                pltpu.VMEM((context, heads * QB), BF),
                pltpu.VMEM((KB, heads * QB), BF),
                pltpu.VMEM((context, heads * QB), BF),
                pltpu.VMEM((width, heads * QB), BF),
                pltpu.VMEM((heads * QB, width), BF),
                pltpu.VMEM((width, heads * QB), BF),
                pltpu.VMEM((heads * QB, width), BF),
                pltpu.VMEM((width, QB), F32),
                pltpu.VMEM((width, QB), F32),
            ],
        ),
        compiler_params=params(),
        cost_estimate=cost(flops // 3, 20 * tokens * width, tokens * 1280 * heads),
        name="attend",
    )(starts, counts, crops, qkv, grad, *full, qcrop, ccrop)


def along_pix(value, by):
    size = lax.axis_size("pix")
    return lax.ppermute(value, "pix", [(i, i + by) for i in range(size) if 0 <= i + by < size])


def across_pix(value, bit):
    return lax.ppermute(value, "pix", [(i, i ^ bit) for i in range(lax.axis_size("pix"))])


def pix_sum(value):
    bit = 1
    while bit < lax.axis_size("pix"):
        value = value + across_pix(value, bit)
        bit *= 2
    return value


def to_mate(value):
    return lax.ppermute(value, "ch", [(i, i ^ 1) for i in range(lax.axis_size("ch"))])


def to_chip(value, by):
    size = lax.axis_size("ch")
    return lax.ppermute(value, "ch", [(i, (i + 2 * by) % size) for i in range(size)])


def gather_rows(value):
    return lax.all_gather(value, "pix", axis=0, tiled=True)


def paired():
    return lax.axis_size("ch") == 4 and lax.axis_size("pix") == 8


def scatter_lines(value):
    size = lax.axis_size("pix")
    lines = [[2 * i + side for i in range(size // 2)] for side in range(2)]
    return lax.psum_scatter(
        value, "pix", scatter_dimension=0, tiled=True, axis_index_groups=lines
    )


def halves_to_send(blocks, side):
    half = blocks[0].shape[1] // 2
    sent = [
        lax.dynamic_slice_in_dim(block[W:-W], (1 - side) * half, half, axis=1)
        for block in blocks[::2]
    ]
    return jnp.concatenate(sent, axis=1)


def scatter_rows(value):
    return lax.psum_scatter(value, "pix", scatter_dimension=0, tiled=True)


def block_ids():
    size = lax.axis_size("ch")
    here = lax.axis_index("ch")
    ids = [here, here ^ 1]
    for by in range(1, size // 2):
        other = lax.rem(here + size - 2 * by, size)
        ids += [other, other ^ 1]
    return jnp.stack(ids).astype(jnp.int32)


def chip_ids():
    size = lax.axis_size("ch")
    here = lax.axis_index("ch")
    chips = [lax.rem(here // 2 + by, size // 2) for by in range(1, size // 2)]
    home = jnp.stack([here // 2, here % 2]).astype(jnp.int32)
    return home, jnp.stack(chips + [here % 2]).astype(jnp.int32)


def tie(*values):
    return lax.optimization_barrier(values)


def far_blocks(value):
    return [to_chip(value, by) for by in range(1, lax.axis_size("ch") // 2)]


def with_mates(blocks):
    found = []
    for block in blocks:
        found += [block, to_mate(block)]
    return found


def gather_blocks(value):
    far = far_blocks(value)
    return [value, to_mate(value)] + with_mates(far)


def chip_sums(parts):
    own, mate = parts
    return [
        (own[i].astype(F32) + to_mate(mate[i]).astype(F32)).astype(BF) for i in range(own.shape[0])
    ]


def sent_sums(sums):
    return [to_chip(piece, by + 1) for by, piece in enumerate(sums)]


def home_parts(parts):
    return [parts[0][0], to_mate(parts[1][0])]


def unpack_rows(packed):
    lines = packed.shape[0]
    width = packed.shape[1] // W
    return packed.reshape(lines, width, W).transpose(0, 2, 1).reshape(lines * W, width)


def pack_rows(cells):
    width = cells.shape[1]
    lines = cells.shape[0] // W
    return cells.reshape(lines, W, width).transpose(0, 2, 1).reshape(lines, width * W)


def small(left, right):
    return jnp.dot(left, right, precision=HIGHEST)


def turned(left, right):
    return lax.dot_general(left, right, (TN, ((), ())), precision=HIGHEST)


def beside_rows(messages):
    to_next, to_prev = messages
    return along_pix(to_next, 1), along_pix(to_prev, -1)


def local(
    pixels,
    cotangent,
    crop_rows,
    condition,
    context,
    kernels,
    attention,
    embedding,
    gains,
    shifts,
    offsets,
):
    lines = pixels.shape[0]
    width = pixels.shape[1] // W
    tokens = lines * W
    depth_here = kernels.shape[0]
    crop_count = crop_rows.shape[0]
    place = lax.axis_index("pix")
    kernel_local = (
        kernels.reshape(depth_here, width, 18).transpose(0, 2, 1).reshape(depth_here, 18 * width)
    )
    maps_local = (
        attention.reshape(depth_here, width, 6).transpose(0, 2, 1).reshape(depth_here, 6 * width)
    )
    kernel_one = gather_rows(kernel_local[:, : 9 * width])
    two_local = kernel_local[:, 9 * width :]
    four = jnp.concatenate([maps_local[:, : 3 * width], maps_local[:, 5 * width :]], axis=1)
    embedding_local = (
        embedding.reshape(depth_here, width, 2).transpose(0, 2, 1).reshape(depth_here, 2 * width)
    )
    context_flat = context.reshape(-1, context.shape[2])
    own_rows = place * depth_here
    context_own = lax.dynamic_slice_in_dim(context_flat, own_rows, depth_here, axis=1)
    condition_own = lax.dynamic_slice_in_dim(condition, own_rows, depth_here, axis=1)
    summed = pix_sum(
        jnp.concatenate(
            [
                dot(condition_own, embedding_local, NN),
                dot(context_own, maps_local[:, 3 * width : 5 * width], NN),
            ],
            axis=0,
        )
    )
    bounds = jnp.cumsum(crop_rows)
    line = place * lines + jnp.arange(-(CROP_ROWS - 1), lines + CROP_ROWS - 1, dtype=jnp.int32)
    found = jnp.sum((line[:, None] >= bounds[None, :]).astype(jnp.int32), axis=1)
    crop_wide = jnp.where((line >= 0) & (line < bounds[-1]), found, -1)
    near = crop_wide[CROP_ROWS - 2 : CROP_ROWS + lines]
    crop_row = near[1:-1]
    same = (crop_row[:, None] == crop_row[None, :]).astype(F32)
    member = (crop_row[:, None] == jnp.arange(crop_count)[None, :]).astype(F32)
    sizes = jnp.sum(jnp.where(member > 0, crop_rows[None, :], 0), axis=1)
    rows = jnp.stack(
        [
            (near[:-2] == crop_row).astype(F32),
            jnp.ones((lines,), F32),
            (near[2:] == crop_row).astype(F32),
            (crop_row == near[0]).astype(F32),
            (crop_row == near[-1]).astype(F32),
            1.0 / (sizes * (W * GSIZE)).astype(F32),
        ]
    )
    rows = jnp.broadcast_to(rows[:, :, None], (6, lines, width))
    if paired():
        other = (place ^ 1) * lines + jnp.arange(-1, lines + 1, dtype=jnp.int32)
        found = jnp.sum((other[:, None] >= bounds[None, :]).astype(jnp.int32), axis=1)
        found = jnp.where((other >= 0) & (other < bounds[-1]), found, -1)
        other_rows = jnp.stack(
            [
                (found[:-2] == found[1:-1]).astype(F32),
                jnp.ones((lines,), F32),
                (found[2:] == found[1:-1]).astype(F32),
            ]
        )
        other_rows = jnp.broadcast_to(other_rows[:, :, None], (3, lines, width))
        side = place % 2
    crop_end = jnp.sum(jnp.where(member > 0, bounds[None, :], 0), axis=1)
    crop_start = crop_end - sizes
    base = place * lines - (CROP_ROWS - 1)
    step = QB // W
    window_low = (crop_start[::step] - base) * W
    window_high = (crop_end[step - 1 :: step] - base) * W
    starts = window_low // 128 * 128
    counts = (window_high - starts + KB - 1) // KB
    window = -(-(2 * HALO + tokens + KB) // KB) * KB
    key_crop = jnp.pad(
        crop_wide, (0, window // W - crop_wide.shape[0]), constant_values=-2
    ).astype(jnp.int32)
    context_crop = jnp.broadcast_to(
        jnp.repeat(jnp.arange(crop_count, dtype=jnp.int32), CTX)[:, None], (crop_count * CTX, 128)
    )
    query_crop = jnp.repeat(crop_row, W).reshape(-1, 1, QB)
    tables = (starts.astype(jnp.int32), counts.astype(jnp.int32), key_crop, query_crop, context_crop)

    ids = block_ids()
    home, away = chip_ids()
    if paired():
        half_ids = jnp.concatenate([ids, side.astype(jnp.int32)[None]])
    gain = [gains[i : i + 1] for i in range(3)]
    shift = [shifts[i : i + 1] for i in range(3)]
    inputs = unpack_rows(pixels).astype(F32)
    dy_low = unpack_rows(cotangent)
    dy_beside = along_pix(dy_low[-W:], 1), along_pix(dy_low[:W], -1)
    totals, *messages = stats(inputs, same)
    input_beside = beside_rows(messages)
    a_one, stats_one = norm(inputs, totals, *input_beside, rows, gain[0], shift[0])
    one_blocks, kernel_one, two_local, summed = tie(
        gather_blocks(a_one), kernel_one, two_local, summed
    )
    embed_terms = summed[:crop_count]
    ckey = summed[crop_count:, :width].astype(BF)
    cval = summed[crop_count:, width:].astype(BF)
    kernel_two = gather_rows(two_local)
    c_one, totals, *messages = convolve(one_blocks, ids, kernel_one, rows, same, ())
    growth = 1.0 + small(member, embed_terms[:, :width] + offsets[2])
    shift_add = small(member, embed_terms[:, width:] + offsets[3])
    mixed = (growth, shift_add)
    c_beside = beside_rows(messages)
    a_two, stats_two = norm(c_one, totals, *c_beside, rows, gain[1], shift[1], mixed)
    two_blocks, kernel_two, four = tie(gather_blocks(a_two), kernel_two, four)
    four = gather_rows(four)
    resid, totals, *messages = convolve(
        two_blocks, ids, kernel_two, rows, same, (inputs, offsets[0:1])
    )
    resid_beside = beside_rows(messages)
    n_three, stats_three = norm(
        resid, totals, *resid_beside, rows, gain[2], shift[2], active=None, wide=False
    )
    dy_low, n_three = tie(dy_low, n_three)
    three_blocks = gather_blocks(n_three)
    dy_blocks = gather_blocks(dy_low)
    qkv = project(three_blocks, ids, four, 0, 3 * width)
    first_dy, qkv = lax.optimization_barrier((dy_blocks[0], qkv))
    datt = project([first_dy] + dy_blocks[1:], ids, four, 3 * width, width)
    low = along_pix(qkv[tokens - HALO :, width:], 1)
    high = along_pix(qkv[:HALO, width:], -1)
    low, high, one_blocks, two_blocks = tie(low, high, one_blocks, two_blocks)
    if paired():
        sent = [halves_to_send(blocks, side) for blocks in (one_blocks, two_blocks)]
        sent, qkv, datt = tie(sent, qkv, datt)
        sent = [across_pix(part, 1) for part in sent]
    found = attend(qkv, datt, low, high, ckey, cval, tables)
    if paired():
        found, sent = tie(found, sent)
        one_pairs, two_pairs = [(part, to_mate(part)) for part in sent]
    att, dquery, dlow, down, dhigh, dckey, dcval = found
    from_prev, from_next = along_pix(dhigh, 1), along_pix(dlow, -1)
    arrived = sent_sums(chip_sums(spread(att, away, four, 3 * width)))
    result = resid + offsets[1:2]
    for piece in home_parts(spread(att, home, four, 3 * width)) + arrived:
        result = result + piece.astype(F32)
    result = pack_rows(result)
    dmap_out = outer(dy_blocks, ids, att)
    from_prev, from_next, result, dmap_out = tie(from_prev, from_next, result, dmap_out)
    gap = ((0, tokens - HALO), (0, 0)), ((tokens - HALO, 0), (0, 0))
    down = down + jnp.pad(from_prev.astype(F32), gap[0]) + jnp.pad(from_next.astype(F32), gap[1])
    dqkv = jnp.concatenate([dquery, down.astype(BF)], axis=1)
    sums_three = chip_sums(spread(dqkv, away, four))
    dqkv, sums_three = tie(dqkv, sums_three)
    arrived = sent_sums(sums_three)
    parts = spread(dqkv, home, four)
    dqkv, parts = tie(dqkv, parts)
    dmaps = jnp.concatenate([outer(three_blocks, ids, dqkv), dmap_out], axis=1)
    parts, arrived, dmaps = tie(home_parts(parts), arrived, dmaps)
    parts = parts + arrived
    dmaps = scatter_rows(dmaps)
    e_three, raw_three, totals, *messages = gradient_sums(
        parts, resid, stats_three, gain[2], shift[2], same
    )
    e_beside = beside_rows(messages)
    dresid, taps_two, wide_two, *parts = gradient_taps(
        e_three, resid, resid_beside, stats_three, totals, *e_beside, rows, gain[2],
        (dy_low, *dy_beside), away, kernel_two,
    )
    sums_two = chip_sums(parts)
    taps_two, sums_two = tie(taps_two, sums_two)
    arrived = sent_sums(sums_two)
    parts = spread(taps_two, home, kernel_two)
    taps_two, parts = tie(taps_two, parts)
    if paired():
        beside_two = across_pix(wide_two, 1)
        dkernel_two = half_own(two_blocks, half_ids, taps_two)
        dkernel_two = half_beside(two_pairs, half_ids, beside_two, other_rows, dkernel_two)
    else:
        dkernel_two = outer(two_blocks, ids, taps_two, W)
    parts, arrived, dkernel_two = tie(home_parts(parts), arrived, dkernel_two)
    parts = parts + arrived
    dkernel_two, dmaps = tie(dkernel_two, dmaps)
    dkernel_two = scatter_lines(dkernel_two) if paired() else scatter_rows(dkernel_two)
    e_two, raw_two, totals, *messages = gradient_sums(
        parts, c_one, stats_two, gain[1], shift[1], same, mixed
    )
    e_beside = beside_rows(messages)
    taps_one, wide_one, *parts = gradient_taps(
        e_two, c_one, c_beside, stats_two, totals, *e_beside, rows, gain[1], None, away, kernel_one
    )
    sums_one = chip_sums(parts)
    taps_one, sums_one = tie(taps_one, sums_one)
    arrived = sent_sums(sums_one)
    parts = spread(taps_one, home, kernel_one)
    taps_one, parts = tie(taps_one, parts)
    if paired():
        beside_one = across_pix(wide_one, 1)
        dkernel_one = half_own(one_blocks, half_ids, taps_one)
        dkernel_one = half_beside(one_pairs, half_ids, beside_one, other_rows, dkernel_one)
    else:
        dkernel_one = outer(one_blocks, ids, taps_one, W)
    parts, arrived, dkernel_one, dkernel_two = tie(
        home_parts(parts), arrived, dkernel_one, dkernel_two
    )
    parts = parts + arrived
    dkernel_one = scatter_lines(dkernel_one) if paired() else scatter_rows(dkernel_one)
    demb = jnp.concatenate(
        [turned(member, raw_two[1] * gain[1] + raw_two[0] * shift[1]), turned(member, raw_two[0])]
    )
    e_one, raw_one, totals, *messages = gradient_sums(
        parts, inputs, stats_one, gain[0], shift[0], same, active="plain"
    )
    grad_pixels = last_gradient(
        e_one, inputs, stats_one, totals, *beside_rows(messages), rows, gain[0], dresid
    )
    grad_pixels, raw_one = tie(grad_pixels, raw_one)
    sums = jnp.concatenate(
        [
            raw_one[1].sum(0)[None],
            (raw_two[1] * growth).sum(0)[None],
            raw_three[1].sum(0)[None],
            raw_one[0].sum(0)[None],
            (raw_two[0] * growth).sum(0)[None],
            raw_three[0].sum(0)[None],
            dresid.sum(0)[None],
            dy_low.astype(F32).sum(0)[None],
            demb,
            dckey,
            dcval,
        ],
        axis=0,
    )
    sums = pix_sum(sums)
    grad_gains, grad_shifts = sums[0:3], sums[3:6]
    demb = sums[8 : 8 + 2 * crop_count].reshape(2, crop_count, width)
    grad_offsets = jnp.concatenate([sums[6:8], demb.sum(1)])
    dcontext = sums[8 + 2 * crop_count :].reshape(2, crop_count * CTX, width)
    own_condition = condition_own.astype(F32)
    grad_embedding = jnp.stack([turned(own_condition, demb[i]) for i in range(2)], axis=2)
    own_context = context_own.astype(F32)
    dcontext_maps = [turned(own_context, dcontext[i]) for i in range(2)]
    dmaps = dmaps.astype(F32).reshape(depth_here, 4, width)
    grad_attention = jnp.stack(
        [dmaps[:, 0], dmaps[:, 1], dmaps[:, 2], *dcontext_maps, dmaps[:, 3]], axis=2
    )
    dkernels = jnp.concatenate([dkernel_one, dkernel_two], axis=1)
    grad_kernels = dkernels.reshape(depth_here, 18, width).transpose(0, 2, 1)
    return (
        result,
        pack_rows(grad_pixels),
        grad_kernels.reshape(depth_here, 18 * width).astype(F32),
        grad_attention.reshape(depth_here, 6 * width),
        grad_embedding.reshape(depth_here, 2 * width),
        grad_gains,
        grad_shifts,
        grad_offsets,
    )


def solution(mesh):
    split = P("pix", "ch")
    tall = P(None, "ch")
    return jax.shard_map(
        local,
        mesh=mesh,
        in_specs=(split, split, P(), P(), P(), split, split, split, tall, tall, tall),
        out_specs=(split, split, split, split, split, tall, tall, tall),
        check_vma=False,
    )
```

```python
import functools

import jax
import jax.numpy as jnp
from jax import lax
from jax.experimental import pallas as pl
from jax.experimental.pallas import tpu as pltpu
from jax.sharding import PartitionSpec as P

HEAD_DIM = 64
W = 32
CROP_ROWS = 32
CTX = 4
GSIZE = 32
HALO = (CROP_ROWS - 1) * W
QB = 256
KB = 256

HIGHEST = lax.Precision.HIGHEST
EPSILON = 1e-05
NEGATIVE = -1e30
BF = jnp.bfloat16
F32 = jnp.float32
VMEM_LIMIT = 58 * 1024 * 1024


def dot(left, right, dims):
    return lax.dot_general(left, right, (dims, ((), ())), preferred_element_type=F32)


NN = ((1,), (0,))
NT = ((1,), (1,))
TN = ((0,), (0,))


def params(**more):
    return pltpu.CompilerParams(vmem_limit_bytes=VMEM_LIMIT, **more)


def cost(flops, moved, exps=0):
    return pl.CostEstimate(flops=flops, bytes_accessed=moved, transcendentals=exps)


WITH_PREV, WITH_NEXT, INVERSE = 3, 4, 5
EDGE = 40


def exact(left, right):
    return lax.dot_general(
        left, right, (NN, ((), ())), precision=HIGHEST, preferred_element_type=F32
    )


def write_totals(first, second, same_ref, totals_ref, next_ref, prev_ref):
    lines, width = first.shape
    row = lax.broadcasted_iota(jnp.int32, (width, width), 0) // GSIZE
    column = lax.broadcasted_iota(jnp.int32, (width, width), 1) // GSIZE
    group = (row == column).astype(F32)
    for place, value in ((0, first), (1, second)):
        total = exact(same_ref[...], exact(value, group))
        totals_ref[place] = total
        next_ref[W + place : W + place + 1, :] = total[lines - 1 : lines, :]
        prev_ref[W + place : W + place + 1, :] = total[0:1, :]
    for target in (next_ref, prev_ref):
        target[W + 2 : EDGE, :] = jnp.zeros((EDGE - W - 2, width), F32)


def crop_means(totals_ref, before_ref, after_ref, rows_ref):
    found = []
    for place in range(2):
        line = slice(W + place, W + place + 1)
        total = totals_ref[place] + rows_ref[WITH_PREV] * before_ref[line, :]
        total = total + rows_ref[WITH_NEXT] * after_ref[line, :]
        found.append(total * rows_ref[INVERSE])
    return found


def square_sums(value_ref, sums_ref):
    lines = sums_ref.shape[1]

    def one(line, carry):
        cells = value_ref[pl.ds(pl.multiple_of(line * W, W), W), :]
        sums_ref[0, pl.ds(line, 1), :] = jnp.sum(cells, axis=0, keepdims=True)
        sums_ref[1, pl.ds(line, 1), :] = jnp.sum(cells * cells, axis=0, keepdims=True)
        return carry

    lax.fori_loop(0, lines, one, 0, unroll=4)


def stats_shapes(lines, width):
    return (
        jax.ShapeDtypeStruct((2, lines, width), F32),
        jax.ShapeDtypeStruct((EDGE, width), F32),
        jax.ShapeDtypeStruct((EDGE, width), F32),
    )


def stats_body(value_ref, same_ref, totals_ref, next_ref, prev_ref, sums_ref):
    tokens = value_ref.shape[0]
    square_sums(value_ref, sums_ref)
    write_totals(sums_ref[0], sums_ref[1], same_ref, totals_ref, next_ref, prev_ref)
    next_ref[0:W, :] = value_ref[tokens - W :, :]
    prev_ref[0:W, :] = value_ref[0:W, :]


def stats(value, same):
    tokens, width = value.shape
    return pl.pallas_call(
        stats_body,
        out_shape=stats_shapes(tokens // W, width),
        scratch_shapes=[pltpu.VMEM((2, tokens // W, width), F32)],
        compiler_params=params(),
        cost_estimate=cost(tokens * width * 4, tokens * width * 4),
        name="stats",
    )(value, same)


def norm_body(active, wide, *refs):
    value_ref, totals_ref, before_ref, after_ref, rows_ref, gain_ref, shift_ref = refs[:7]
    refs = refs[7:]
    if active == "mixed":
        growth_ref, add_ref = refs[:2]
        refs = refs[2:]
    out_ref, stats_ref, scale_ref, bias_ref = refs
    lines = totals_ref.shape[1]
    mean, square = crop_means(totals_ref, before_ref, after_ref, rows_ref)
    scale = lax.rsqrt(square - mean * mean + EPSILON)
    stats_ref[0] = mean
    stats_ref[1] = scale
    if active == "mixed":
        scale_ref[...] = scale * gain_ref[...] * growth_ref[...]
        bias_ref[...] = shift_ref[...] * growth_ref[...] + add_ref[...]
    else:
        scale_ref[...] = scale * gain_ref[...]
        bias_ref[...] = jnp.broadcast_to(shift_ref[...], bias_ref.shape)

    def cells_of(cells, line):
        here = pl.ds(line, 1)
        value = (cells - stats_ref[0, here, :]) * scale_ref[here, :] + bias_ref[here, :]
        if active is not None:
            value = value / (1.0 + jnp.exp(-value))
        return value.astype(BF)

    base = W if wide else 0

    def one(line, carry):
        start = pl.multiple_of(line * W, W)
        out_ref[pl.ds(start + base, W), :] = cells_of(value_ref[pl.ds(start, W), :], line)
        return carry

    lax.fori_loop(0, lines, one, 0, unroll=4)
    if wide:
        out_ref[0:W, :] = cells_of(before_ref[0:W, :], 0)
        out_ref[(lines + 1) * W :, :] = cells_of(after_ref[0:W, :], lines - 1)


def norm(value, totals, before, after, rows, gain, shift, mixed=None, active="plain", wide=True):
    tokens, width = value.shape
    lines = tokens // W
    operands = [value, totals, before, after, rows, gain, shift]
    if mixed is not None:
        operands += list(mixed)
        active = "mixed"
    return pl.pallas_call(
        functools.partial(norm_body, active, wide),
        out_shape=(
            jax.ShapeDtypeStruct((tokens + (2 * W if wide else 0), width), BF),
            jax.ShapeDtypeStruct((2, lines, width), F32),
        ),
        scratch_shapes=[pltpu.VMEM((lines, width), F32), pltpu.VMEM((lines, width), F32)],
        compiler_params=params(),
        cost_estimate=cost(tokens * width * 12, tokens * width * 6, tokens * width),
        name="norm",
    )(*operands)


def sums_body(count, active, *refs):
    parts = refs[:count]
    value_ref, stats_ref, gain_ref, shift_ref, same_ref = refs[count : count + 5]
    refs = refs[count + 5 :]
    if active == "mixed":
        growth_ref, add_ref = refs[:2]
        refs = refs[2:]
    grad_ref, raw_ref, totals_ref, next_ref, prev_ref = refs
    tokens, width = value_ref.shape
    lines = tokens // W

    def one(line, carry):
        here = pl.ds(line, 1)
        cells = pl.ds(pl.multiple_of(line * W, W), W)
        grad = parts[0][cells, :].astype(F32)
        for part in parts[1:]:
            grad = grad + part[cells, :].astype(F32)
        normal = (value_ref[cells, :] - stats_ref[0, here, :]) * stats_ref[1, here, :]
        if active is not None:
            inner = normal * gain_ref[...] + shift_ref[...]
            if active == "mixed":
                inner = inner * growth_ref[here, :] + add_ref[here, :]
            sigmoid = 1.0 / (1.0 + jnp.exp(-inner))
            grad = grad * sigmoid * (1.0 + inner * (1.0 - sigmoid))
        raw_ref[0, here, :] = jnp.sum(grad, axis=0, keepdims=True)
        raw_ref[1, here, :] = jnp.sum(grad * normal, axis=0, keepdims=True)
        if active == "mixed":
            grad = grad * growth_ref[here, :]
        grad_ref[cells, :] = grad
        return carry

    lax.fori_loop(0, lines, one, 0, unroll=4)
    first, second = raw_ref[0] * gain_ref[...], raw_ref[1] * gain_ref[...]
    if active == "mixed":
        first, second = first * growth_ref[...], second * growth_ref[...]
    write_totals(first, second, same_ref, totals_ref, next_ref, prev_ref)
    next_ref[0:W, :] = grad_ref[tokens - W :, :]
    prev_ref[0:W, :] = grad_ref[0:W, :]


def gradient_sums(parts, value, stats_found, gain, shift, same, mixed=None, active=None):
    tokens, width = value.shape
    operands = [*parts, value, stats_found, gain, shift, same]
    if mixed is not None:
        operands += list(mixed)
        active = "mixed"
    return pl.pallas_call(
        functools.partial(sums_body, len(parts), active),
        out_shape=(
            jax.ShapeDtypeStruct((tokens, width), F32),
            jax.ShapeDtypeStruct((2, tokens // W, width), F32),
        )
        + stats_shapes(tokens // W, width),
        compiler_params=params(),
        cost_estimate=cost(tokens * width * 20, tokens * width * 14, tokens * width),
        name="gradient_sums",
    )(*operands)


def norm_gradient(grad, value, line, stats_ref, mean_ref, gain_ref):
    here = pl.ds(line, 1)
    scale = stats_ref[1, here, :]
    normal = (value - stats_ref[0, here, :]) * scale
    return scale * (grad * gain_ref[...] - mean_ref[0, here, :] - normal * mean_ref[1, here, :])


def write_taps(wide_ref, rows_ref, taps_ref):
    tokens = taps_ref.shape[0]
    width = wide_ref.shape[1]
    column = lax.broadcasted_iota(jnp.int32, (W, width), 0)

    def spread_row(line, carry):
        start = pl.multiple_of(line * W, W)
        target = pl.ds(start, W)
        for up in range(3):
            mask = rows_ref[up, pl.ds(line, 1), :]
            values = wide_ref[pl.ds(start + up * W, W), :].astype(F32) * mask
            left = jnp.where(column > 0, pltpu.roll(values, 1, 0), 0.0)
            right = jnp.where(column < W - 1, pltpu.roll(values, W - 1, 0), 0.0)
            for side, moved in enumerate((left, values, right)):
                tap = 8 - (3 * up + side)
                taps_ref[target, tap * width : (tap + 1) * width] = moved.astype(BF)
        return carry

    lax.fori_loop(0, tokens // W, spread_row, 0, unroll=2)


def taps_body(based, ids, *refs):
    grad_ref, value_ref, value_before, value_after, stats_ref, totals_ref = refs[:6]
    before_ref, after_ref, rows_ref, gain_ref = refs[6:10]
    refs = refs[10:]
    if based:
        base_ref, base_before, base_after = refs[:3]
        refs = refs[3:]
    map_ref = refs[0]
    refs = refs[1:]
    if based:
        full_ref = refs[0]
        refs = refs[1:]
    taps_ref = refs[0]
    refs = refs[1:]
    low_ref, same_core, other_core, wide_ref, mean_ref = refs
    tokens, width = grad_ref.shape
    lines = tokens // W
    padded = tokens + 2 * W

    @pl.when(pl.program_id(0) == 0)
    def _():
        mean_ref[0], mean_ref[1] = crop_means(totals_ref, before_ref, after_ref, rows_ref)

        def one(line, carry):
            start = pl.multiple_of(line * W, W)
            cells = pl.ds(start, W)
            found = norm_gradient(
                grad_ref[cells, :], value_ref[cells, :], line, stats_ref, mean_ref, gain_ref
            )
            if based:
                found = found + base_ref[cells, :].astype(F32)
                full_ref[cells, :] = found
            wide_ref[pl.ds(start + W, W), :] = found
            return carry

        lax.fori_loop(0, lines, one, 0, unroll=4)
        for edge_ref, edge_value, line, start in (
            (before_ref, value_before, 0, 0),
            (after_ref, value_after, lines - 1, padded - W),
        ):
            found = norm_gradient(
                edge_ref[0:W, :], edge_value[0:W, :], line, stats_ref, mean_ref, gain_ref
            )
            if based:
                found = found + (base_before if line == 0 else base_after)[0:W, :].astype(F32)
            wide_ref[start : start + W, :] = found

        write_taps(wide_ref, rows_ref, taps_ref)
        low_ref[...] = wide_ref[...].astype(BF)

    core = ids[ids.shape[0] - 1]
    write_products(taps_ref, map_ref, core, same_core, other_core)


def write_products(grad_ref, map_ref, core, same_core, other_core):
    tokens, width = same_core.shape[1:]
    for place, target in ((core, same_core), (1 - core, other_core)):
        rows = pl.ds(pl.multiple_of(place * width, width), width)
        for start in range(0, tokens, 512):
            here = slice(start, start + 512)
            target[0, here, :] = dot(grad_ref[here, :], map_ref[rows, :], NT).astype(BF)


def gradient_taps(
    grad, value, beside, stats_found, totals, before, after, rows, gain, base, ids, maps
):
    tokens, width = grad.shape
    lines = tokens // W
    count = ids.shape[0] - 1
    wide = 9 * width
    operands = [grad, value, *beside, stats_found, totals, before, after, rows, gain]
    if base is not None:
        operands += list(base)
    whole = lambda array: pl.BlockSpec(array.shape, lambda step, ids: (0,) * len(array.shape))
    in_specs = [whole(operand) for operand in operands]
    operands.append(maps)
    in_specs.append(pl.BlockSpec((2 * width, wide), lambda step, ids: (ids[step], 0)))
    taps_shape = jax.ShapeDtypeStruct((tokens, wide), BF)
    shapes, out_specs = [taps_shape], [whole(taps_shape)]
    if base is not None:
        full_shape = jax.ShapeDtypeStruct((tokens, width), F32)
        shapes, out_specs = [full_shape] + shapes, [whole(full_shape)] + out_specs
    low_shape = jax.ShapeDtypeStruct((tokens + 2 * W, width), BF)
    shapes.append(low_shape)
    out_specs.append(whole(low_shape))
    shapes += [jax.ShapeDtypeStruct((count, tokens, width), BF)] * 2
    out_specs += [pl.BlockSpec((1, tokens, width), lambda step, ids: (step, 0, 0))] * 2
    return pl.pallas_call(
        functools.partial(taps_body, base is not None),
        out_shape=shapes,
        grid_spec=pltpu.PrefetchScalarGridSpec(
            num_scalar_prefetch=1,
            grid=(count,),
            in_specs=in_specs,
            out_specs=out_specs,
            scratch_shapes=[
                pltpu.VMEM((tokens + 2 * W, width), F32),
                pltpu.VMEM((2, lines, width), F32),
            ],
        ),
        compiler_params=params(),
        cost_estimate=cost(2 * tokens * count * width * wide, tokens * wide * 4),
        name="gradient_taps",
    )(ids, *operands)


def last_body(grad_ref, value_ref, stats_ref, totals_ref, before_ref, after_ref, rows_ref, gain_ref,
              base_ref, out_ref, mean_ref):
    mean_ref[0], mean_ref[1] = crop_means(totals_ref, before_ref, after_ref, rows_ref)

    def one(line, carry):
        cells = pl.ds(pl.multiple_of(line * W, W), W)
        out_ref[cells, :] = base_ref[cells, :] + norm_gradient(
            grad_ref[cells, :], value_ref[cells, :], line, stats_ref, mean_ref, gain_ref
        )
        return carry

    lax.fori_loop(0, grad_ref.shape[0] // W, one, 0, unroll=4)


def last_gradient(grad, value, stats_found, totals, before, after, rows, gain, base):
    tokens, width = grad.shape
    return pl.pallas_call(
        last_body,
        out_shape=jax.ShapeDtypeStruct((tokens, width), F32),
        scratch_shapes=[pltpu.VMEM((2, tokens // W, width), F32)],
        compiler_params=params(),
        cost_estimate=cost(tokens * width * 10, tokens * width * 16),
        name="last_gradient",
    )(grad, value, stats_found, totals, before, after, rows, gain, base)


def conv_body(count, resid, ids, *refs):
    blocks = refs[:count]
    kernel_ref, rows_ref = refs[count : count + 2]
    refs = refs[count + 2 :]
    if resid:
        input_ref, bias_ref = refs[:2]
        refs = refs[2:]
    same_ref, out_ref, totals_ref, next_ref, prev_ref, all_ref, sums_ref = refs
    tokens, width = out_ref.shape
    for place in range(count):
        lanes = pl.ds(pl.multiple_of(ids[place] * width, width), width)
        all_ref[:, lanes] = blocks[place][...]
    chunk = 256
    lines = chunk // W
    for start in range(0, tokens, chunk):
        here = slice(start, start + chunk)
        sides = [None] * 3
        for up in range(3):
            taps = kernel_ref[:, up * 3 * width : (up + 1) * 3 * width]
            part = dot(all_ref[up * W + start : up * W + start + chunk, :], taps, NN)
            part = part.reshape(lines, W, 3 * width)
            mask = rows_ref[up, start // W : start // W + lines, :][:, None, :]
            for side in range(3):
                piece = part[:, :, side * width : (side + 1) * width]
                piece = piece if up == 1 else piece * mask
                sides[side] = piece if sides[side] is None else sides[side] + piece
        sides = [piece.reshape(chunk, width) for piece in sides]
        column = lax.broadcasted_iota(jnp.int32, (chunk, width), 0) % W
        left = jnp.where(column > 0, pltpu.roll(sides[0], 1, 0), 0.0)
        right = jnp.where(column < W - 1, pltpu.roll(sides[2], chunk - 1, 0), 0.0)
        total = sides[1] + left + right
        if resid:
            total += input_ref[here, :] + bias_ref[...]
        out_ref[here, :] = total
    square_sums(out_ref, sums_ref)
    write_totals(sums_ref[0], sums_ref[1], same_ref, totals_ref, next_ref, prev_ref)
    next_ref[0:W, :] = out_ref[tokens - W :, :]
    prev_ref[0:W, :] = out_ref[0:W, :]


def convolve(blocks, ids, kernel, rows, same, resid):
    count = len(blocks)
    padded, width = blocks[0].shape
    tokens = padded - 2 * W
    lines = tokens // W
    operands = [*blocks, kernel, rows, *resid, same]

    def whole(array):
        return pl.BlockSpec(array.shape, lambda step, ids: (0,) * len(array.shape))

    shapes = (jax.ShapeDtypeStruct((tokens, width), F32),) + stats_shapes(lines, width)
    return pl.pallas_call(
        functools.partial(conv_body, count, len(resid)),
        out_shape=shapes,
        grid_spec=pltpu.PrefetchScalarGridSpec(
            num_scalar_prefetch=1,
            grid=(1,),
            in_specs=[whole(operand) for operand in operands],
            out_specs=[whole(shape) for shape in shapes],
            scratch_shapes=[
                pltpu.VMEM((padded, count * width), BF),
                pltpu.VMEM((2, lines, width), F32),
            ],
        ),
        compiler_params=params(),
        cost_estimate=cost(
            18 * tokens * count * width * width, 18 * count * width * width + tokens * width * 12
        ),
        name="convolve",
    )(ids, *operands)


def project_body(count, width, ids, *refs):
    blocks = refs[:count]
    map_ref, out_ref, all_ref = refs[count:]

    @pl.when(pl.program_id(0) == 0)
    def _():
        for place in range(count):
            first = pl.multiple_of(ids[place] * width, width)
            all_ref[:, pl.ds(first, width)] = blocks[place][...]

    for start in range(0, out_ref.shape[0], 512):
        here = slice(start, start + 512)
        out_ref[here, :] = dot(all_ref[here, :], map_ref[...], NN).astype(out_ref.dtype)


def project(blocks, ids, maps, first, wide):
    count = len(blocks)
    tokens, width = blocks[0].shape
    depth = maps.shape[0]
    start = first // width
    return pl.pallas_call(
        functools.partial(project_body, count, width),
        out_shape=jax.ShapeDtypeStruct((tokens, wide), BF),
        grid_spec=pltpu.PrefetchScalarGridSpec(
            num_scalar_prefetch=1,
            grid=(wide // width,),
            in_specs=[pl.BlockSpec((tokens, width), lambda step, ids: (0, 0))] * count
            + [pl.BlockSpec((depth, width), lambda step, ids: (0, start + step))],
            out_specs=pl.BlockSpec((tokens, width), lambda step, ids: (0, step)),
            scratch_shapes=[pltpu.VMEM((tokens, depth), BF)],
        ),
        compiler_params=params(),
        cost_estimate=cost(2 * tokens * depth * wide, (tokens + depth) * wide * 2),
        name="project",
    )(ids, *blocks, maps)


def spread_body(ids, grad_ref, *refs):
    core = ids[ids.shape[0] - 1]
    write_products(grad_ref, refs[0], core, *refs[1:])


def spread(grad, ids, maps, first=0):
    tokens, wide = grad.shape
    count = ids.shape[0] - 1
    width = maps.shape[0] // lax.axis_size("ch")
    start = first // wide
    return pl.pallas_call(
        spread_body,
        out_shape=[jax.ShapeDtypeStruct((count, tokens, width), BF)] * 2,
        grid_spec=pltpu.PrefetchScalarGridSpec(
            num_scalar_prefetch=1,
            grid=(count,),
            in_specs=[
                pl.BlockSpec((tokens, wide), lambda step, ids: (0, 0)),
                pl.BlockSpec((2 * width, wide), lambda step, ids: (ids[step], start)),
            ],
            out_specs=[pl.BlockSpec((1, tokens, width), lambda step, ids: (step, 0, 0))] * 2,
        ),
        compiler_params=params(),
        cost_estimate=cost(4 * tokens * count * width * wide, (tokens + count * width) * wide * 2),
        name="spread",
    )(ids, grad, maps)


def home_body(count, halved, shift, ids, *refs):
    grad_ref, map_ref = refs[:2]
    blocks = refs[2 : 2 + count]
    same_core, other_core, out_ref, turned_ref = refs[2 + count :]
    tokens = grad_ref.shape[0]
    width = blocks[0].shape[1]
    share = width // 2 if halved else width
    write_products(grad_ref, map_ref, ids[1], same_core, other_core)
    for place in range(count):
        rows = pl.ds(pl.multiple_of(ids[3 + place] * share, share), share)
        lanes = slice(None)
        if halved:
            lanes = pl.ds(pl.multiple_of(ids[2] * share, share), share)
        turned_ref[rows, :] = blocks[place][shift : shift + tokens, lanes].T
    depth, wide = out_ref.shape
    for start in range(0, wide, 3 * width):
        columns = slice(start, start + 3 * width)
        out_ref[:, columns] = dot(turned_ref[...], grad_ref[:, columns], NN).astype(out_ref.dtype)


def home_and_outer(grad, ids, maps, blocks, halved=False, first=0, shift=0):
    count = len(blocks)
    tokens, wide = grad.shape
    width = blocks[0].shape[1]
    depth = count * width // (2 if halved else 1)
    start = first // wide
    part = jax.ShapeDtypeStruct((1, tokens, width), BF)

    def whole(array):
        return pl.BlockSpec(array.shape, lambda step, ids: (0,) * len(array.shape))

    result = jax.ShapeDtypeStruct((depth, wide), F32 if halved else BF)
    return pl.pallas_call(
        functools.partial(home_body, count, halved, shift),
        out_shape=[part, part, result],
        grid_spec=pltpu.PrefetchScalarGridSpec(
            num_scalar_prefetch=1,
            grid=(1,),
            in_specs=[
                whole(grad), pl.BlockSpec((2 * width, wide), lambda step, ids: (ids[0], start)),
            ]
            + [whole(block) for block in blocks],
            out_specs=[whole(part), whole(part), whole(result)],
            scratch_shapes=[pltpu.VMEM((depth, tokens), BF)],
        ),
        compiler_params=params(),
        cost_estimate=cost(
            2 * tokens * (depth + 2 * width) * wide, (tokens + depth + 2 * width) * wide * 2
        ),
        name="home_and_outer",
    )(ids, grad, maps, *blocks)


def half_beside_body(count, ids, *refs):
    pairs = refs[:2]
    wide_ref, rows_ref, own_ref, out_ref, turned_ref, taps_ref = refs[2:]
    tokens = taps_ref.shape[0]
    half = pairs[0].shape[1] // (count // 2)
    tile = out_ref.shape[1]
    step = pl.program_id(0)

    @pl.when(step == 0)
    def _():
        write_taps(wide_ref, rows_ref, taps_ref)
        for place in range(count):
            rows = pl.ds(pl.multiple_of(ids[1 + place] * half, half), half)
            lanes = slice(place // 2 * half, (place // 2 + 1) * half)
            turned_ref[rows, :] = pairs[place % 2][:, lanes].T

    columns = pl.ds(pl.multiple_of(step * tile, tile), tile)
    out_ref[...] = (own_ref[...] + dot(turned_ref[...], taps_ref[:, columns], NN)).astype(BF)


def half_beside(pairs, ids, wide_grad, row_masks, own):
    count = ids.shape[0] - 1
    tokens, both = pairs[0].shape
    depth, wide = own.shape
    padded, width = wide_grad.shape
    tile = 3 * width
    once = lambda step, ids: (0, 0)
    return pl.pallas_call(
        functools.partial(half_beside_body, count),
        out_shape=jax.ShapeDtypeStruct((depth, wide), BF),
        grid_spec=pltpu.PrefetchScalarGridSpec(
            num_scalar_prefetch=1,
            grid=(wide // tile,),
            in_specs=[
                pl.BlockSpec((tokens, both), once),
                pl.BlockSpec((tokens, both), once),
                pl.BlockSpec((padded, width), once),
                pl.BlockSpec(row_masks.shape, lambda step, ids: (0, 0, 0)),
                pl.BlockSpec((depth, tile), lambda step, ids: (0, step)),
            ],
            out_specs=pl.BlockSpec((depth, tile), lambda step, ids: (0, step)),
            scratch_shapes=[pltpu.VMEM((depth, tokens), BF), pltpu.VMEM((tokens, wide), BF)],
        ),
        compiler_params=params(),
        cost_estimate=cost(2 * tokens * depth * wide, (tokens + 3 * depth) * wide * 2),
        name="half_beside",
    )(ids, *pairs, wide_grad, row_masks, own)


def outer_body(count, shift, ids, *refs):
    blocks = refs[:count]
    grad_ref, out_ref, turned_ref = refs[count:]
    tokens = grad_ref.shape[0]
    width = blocks[0].shape[1]

    @pl.when(pl.program_id(0) == 0)
    def _():
        for place in range(count):
            first = pl.multiple_of(ids[place] * width, width)
            turned_ref[pl.ds(first, width), :] = blocks[place][shift : shift + tokens, :].T

    depth = turned_ref.shape[0]
    for start in range(0, depth, 512):
        here = slice(start, start + 512)
        out_ref[here, :] = dot(turned_ref[here, :], grad_ref[...], NN).astype(BF)


def outer(blocks, ids, grad, shift=0, columns=None):
    count = len(blocks)
    tokens = grad.shape[0]
    first, wide = columns or (0, grad.shape[1])
    padded, width = blocks[0].shape
    depth = count * width
    tile = min(wide, 3 * width)
    before = first // tile
    return pl.pallas_call(
        functools.partial(outer_body, count, shift),
        out_shape=jax.ShapeDtypeStruct((depth, wide), BF),
        grid_spec=pltpu.PrefetchScalarGridSpec(
            num_scalar_prefetch=1,
            grid=(wide // tile,),
            in_specs=[pl.BlockSpec((padded, width), lambda step, ids: (0, 0))] * count
            + [pl.BlockSpec((tokens, tile), lambda step, ids: (0, before + step))],
            out_specs=pl.BlockSpec((depth, tile), lambda step, ids: (0, step)),
            scratch_shapes=[pltpu.VMEM((depth, tokens), BF)],
        ),
        compiler_params=params(),
        cost_estimate=cost(2 * tokens * depth * wide, (tokens + depth) * wide * 2),
        name="outer",
    )(ids, *blocks, grad)


def pack_body(first_ref, second_ref, out_ref, order_ref, sorted_ref):
    depth, wide = first_ref.shape
    width = wide // 9
    size = order_ref.shape[0]
    for start in range(0, size, 128):
        row = start + lax.broadcasted_iota(jnp.int32, (128, size), 0)
        column = lax.broadcasted_iota(jnp.int32, (128, size), 1)
        wanted = (row & 63) * 18 + (row >> 6)
        order_ref[start : start + 128, :] = jnp.where(column == wanted, 1.0, 0.0).astype(BF)
    lane = lax.broadcasted_iota(jnp.int32, (depth, 128), 1)
    for block in range(width // 128):
        for pair in range(9):
            cells = []
            for tap in (2 * pair, 2 * pair + 1):
                source = first_ref if tap < 9 else second_ref
                at = tap % 9 * width + block * 128
                cells.append(source[:, at : at + 128].astype(F32))
            low = jnp.where(lane < 64, cells[0], pltpu.roll(cells[1], 64, 1))
            high = jnp.where(lane < 64, pltpu.roll(cells[0], 64, 1), cells[1])
            here = slice(pair * 128, (pair + 1) * 128)
            for half, value in ((0, low), (1, high)):
                at = (2 * block + half) * depth
                sorted_ref[at : at + depth, here] = value.astype(BF)
    found = dot(sorted_ref[...], order_ref[...], NN)
    for block in range(width // 64):
        out_ref[:, block * size : (block + 1) * size] = found[block * depth : (block + 1) * depth]


def pack_kernels(first, second):
    depth, wide = first.shape
    size = 64 * 18
    return pl.pallas_call(
        pack_body,
        out_shape=jax.ShapeDtypeStruct((depth, 2 * wide), F32),
        scratch_shapes=[
            pltpu.VMEM((size, size), BF),
            pltpu.VMEM((2 * wide // size * depth, size), BF),
        ],
        compiler_params=params(),
        cost_estimate=cost(4 * depth * wide * size, depth * wide * 12),
        name="pack_kernels",
    )(first, second)


def attention_body(
    heads, starts, counts, crops, chips, query_ref, grad_ref, low_ref, own_ref, high_ref, ckey_ref,
    cval_ref, map_ref, qcrop_ref, ccrop_ref, home_same, home_other, away_same, away_other, att_ref, dquery_ref, dlow_ref, down_ref, dhigh_ref, dckey_ref,
    dcval_ref, keys, values, keys_t, values_t, dkeys, dvalues, kcrop_ref, score_ref, prob_ref,
    cscore_ref, cprob_ref, slope_ref, cslope_ref, qt_ref, qn_ref, gt_ref, gn_ref, att_t, dq_t,
):
    step = pl.program_id(0)
    window, width = keys.shape
    tokens = own_ref.shape[0]

    @pl.when(step == 0)
    def _():
        def label(line, carry):
            here = pl.ds(pl.multiple_of(line * W, W), W)
            kcrop_ref[here, :] = jnp.full((W, 128), crops[line], jnp.int32)
            return carry

        lax.fori_loop(0, window // W, label, 0, unroll=2)
        for place, target, turned in ((0, keys, keys_t), (1, values, values_t)):
            part = slice(place * width, (place + 1) * width)
            target[0:HALO, :] = low_ref[:, part]
            shifted = slice((place + 1) * width, (place + 2) * width)
            target[HALO : HALO + tokens, :] = own_ref[:, shifted]
            target[HALO + tokens : 2 * HALO + tokens, :] = high_ref[:, part]
            rest = window - 2 * HALO - tokens
            target[2 * HALO + tokens :, :] = jnp.zeros((rest, width), BF)
            for place in range(0, window, KB):
                turned[:, place : place + KB] = target[place : place + KB, :].T
        dkeys[...] = jnp.zeros_like(dkeys)
        dvalues[...] = jnp.zeros_like(dvalues)
        dckey_ref[...] = jnp.zeros_like(dckey_ref)
        dcval_ref[...] = jnp.zeros_like(dcval_ref)

    first = starts[step]
    blocks = counts[step]
    query = (query_ref[...].astype(F32) * (HEAD_DIM**-0.5)).astype(BF)
    query_t = query.T
    grad_t = grad_ref[...].T
    lane = lax.broadcasted_iota(jnp.int32, (QB, width), 1)
    zero = jnp.zeros((width, QB), BF)
    mine = [slice(head * HEAD_DIM, (head + 1) * HEAD_DIM) for head in range(heads)]
    part = [slice(head * QB, (head + 1) * QB) for head in range(heads)]
    for head in range(heads):
        qt_ref[:, part[head]] = zero
        qt_ref[mine[head], part[head]] = query_t[mine[head], :]
        gt_ref[:, part[head]] = zero
        in_head = (lane >= head * HEAD_DIM) & (lane < (head + 1) * HEAD_DIM)
        qn_ref[part[head], :] = jnp.where(in_head, query, jnp.zeros_like(query))
    crop_row = qcrop_ref[...].reshape(1, QB)
    same_context = jnp.concatenate([ccrop_ref[...]] * (QB // 128), axis=1) == crop_row

    def span(block):
        return pl.ds(pl.multiple_of(first + block * KB, 128), KB)

    def folded(values, combine):
        return combine(values.reshape(-1, 8, QB), axis=0)

    largest = []
    products = dot(ckey_ref[...], qt_ref[...], NN)
    for head in range(heads):
        scores = jnp.where(same_context, products[:, part[head]], NEGATIVE)
        cscore_ref[:, part[head]] = scores
        largest.append(folded(scores, jnp.max))

    def pass_one(block, carry):
        here = span(block)
        same = jnp.concatenate([kcrop_ref[here, :]] * (QB // 128), axis=1) == crop_row
        products = dot(keys[here, :], qt_ref[...], NN)
        out = []
        for head in range(heads):
            scores = jnp.where(same, products[:, part[head]], NEGATIVE)
            score_ref[block, :, part[head]] = scores
            out.append(jnp.maximum(carry[head], folded(scores, jnp.max)))
        return tuple(out)

    largest = lax.fori_loop(0, blocks, pass_one, tuple(largest))
    largest = [jnp.max(value, axis=0, keepdims=True) for value in largest]

    sums = []
    for head in range(heads):
        prob = jnp.exp(cscore_ref[:, part[head]] - largest[head])
        sums.append(folded(prob, jnp.sum))
        low = prob.astype(BF)
        cprob_ref[:, part[head]] = low
        att_t[mine[head], :] = dot(cval_ref[...], low, TN)[mine[head], :]

    def pass_two(block, carry):
        here = span(block)
        out = []
        for head in range(heads):
            prob = jnp.exp(score_ref[block, :, part[head]] - largest[head])
            out.append(carry[head] + folded(prob, jnp.sum))
            low = prob.astype(BF)
            prob_ref[block, :, part[head]] = low
            att_t[mine[head], :] += dot(values_t[mine[head], here], low, NN)
        return tuple(out)

    sums = lax.fori_loop(0, blocks, pass_two, tuple(sums))
    offsets = []
    for head in range(heads):
        inverse = 1.0 / jnp.sum(sums[head], axis=0, keepdims=True)
        attended = att_t[mine[head], :] * inverse
        att_t[mine[head], :] = attended
        scaled = grad_t[mine[head], :].astype(F32) * inverse
        gt_ref[mine[head], part[head]] = scaled.astype(BF)
        offsets.append(jnp.sum(scaled * attended, axis=0, keepdims=True))
        gn_ref[part[head], :] = gt_ref[:, part[head]].T
    attended = att_t[...].T.astype(BF)
    att_ref[...] = attended
    core = chips[chips.shape[0] - 1]
    for chip in range(chips.shape[0] - 1):
        targets = (home_same, home_other) if chip == 0 else (away_same, away_other)
        for place, target in ((core, targets[0]), (1 - core, targets[1])):
            rows = pl.ds(pl.multiple_of((2 * chips[chip] + place) * width, width), width)
            target[max(chip - 1, 0)] = dot(attended, map_ref[rows, :], NT).astype(BF)

    slope = dot(cval_ref[...], gt_ref[...], NN)
    for head in range(heads):
        prob = cprob_ref[:, part[head]].astype(F32)
        dscore = (prob * (slope[:, part[head]] - offsets[head])).astype(BF)
        cslope_ref[:, part[head]] = dscore
        dq_t[mine[head], :] = dot(ckey_ref[...], dscore, TN)[mine[head], :]
    dcval_ref[...] += dot(cprob_ref[...], gn_ref[...], NN)
    dckey_ref[...] += dot(cslope_ref[...], qn_ref[...], NN)

    def pass_three(block, carry):
        here = span(block)
        slope = dot(values[here, :], gt_ref[...], NN)
        for head in range(heads):
            prob = prob_ref[block, :, part[head]].astype(F32)
            dscore = (prob * (slope[:, part[head]] - offsets[head])).astype(BF)
            slope_ref[:, part[head]] = dscore
            dq_t[mine[head], :] += dot(keys_t[mine[head], here], dscore, NN)
        dvalues[here, :] += dot(prob_ref[block], gn_ref[...], NN)
        dkeys[here, :] += dot(slope_ref[...], qn_ref[...], NN)
        return carry

    lax.fori_loop(0, blocks, pass_three, 0)
    dquery_ref[...] = (dq_t[...] * (HEAD_DIM**-0.5)).T.astype(BF)

    @pl.when(step == pl.num_programs(0) - 1)
    def _():
        for place, source in ((0, dkeys), (1, dvalues)):
            part = slice(place * width, (place + 1) * width)
            dlow_ref[:, part] = source[0:HALO, :].astype(BF)
            down_ref[:, part] = source[HALO : HALO + tokens, :]
            dhigh_ref[:, part] = source[HALO + tokens : 2 * HALO + tokens, :].astype(BF)


def attend(qkv, grad, low, high, ckey, cval, maps, chips, tables):
    starts, counts, crops, qcrop, ccrop = tables
    tokens, width = grad.shape
    heads = width // HEAD_DIM
    window = crops.shape[0] * W
    context = ckey.shape[0]
    most = ((QB // W + 2 * (CROP_ROWS - 1)) * W + 127 + KB - 1) // KB
    q_block = pl.BlockSpec((QB, width), lambda step, *_: (step, 0))

    def whole(array):
        return pl.BlockSpec(array.shape, lambda step, *_: (0,) * len(array.shape))

    full = [low, qkv, high, ckey, cval]
    others = chips.shape[0] - 2
    map_spec = pl.BlockSpec((maps.shape[0], width), lambda step, *_: (0, 3))
    part_shapes = [jax.ShapeDtypeStruct((count, tokens, width), BF) for count in (1, 1, others, others)]
    part_specs = [
        pl.BlockSpec((shape.shape[0], QB, width), lambda step, *_: (0, step, 0))
        for shape in part_shapes
    ]
    shapes = (
        jax.ShapeDtypeStruct((tokens, width), BF),
        jax.ShapeDtypeStruct((tokens, width), BF),
        jax.ShapeDtypeStruct((HALO, 2 * width), BF),
        jax.ShapeDtypeStruct((tokens, 2 * width), F32),
        jax.ShapeDtypeStruct((HALO, 2 * width), BF),
        jax.ShapeDtypeStruct((context, width), F32),
        jax.ShapeDtypeStruct((context, width), F32),
    )
    flops = 12 * tokens * 1280 * width
    return pl.pallas_call(
        functools.partial(attention_body, heads),
        out_shape=(*part_shapes, *shapes),
        grid_spec=pltpu.PrefetchScalarGridSpec(
            num_scalar_prefetch=4,
            grid=(tokens // QB,),
            in_specs=[q_block, q_block]
            + [whole(array) for array in full]
            + [map_spec, pl.BlockSpec((1, 1, QB), lambda step, *_: (step, 0, 0)), whole(ccrop)],
            out_specs=[*part_specs, q_block, q_block] + [whole(shape) for shape in shapes[2:]],
            scratch_shapes=[
                pltpu.VMEM((window, width), BF),
                pltpu.VMEM((window, width), BF),
                pltpu.VMEM((width, window), BF),
                pltpu.VMEM((width, window), BF),
                pltpu.VMEM((window, width), F32),
                pltpu.VMEM((window, width), F32),
                pltpu.VMEM((window, 128), jnp.int32),
                pltpu.VMEM((most, KB, heads * QB), F32),
                pltpu.VMEM((most, KB, heads * QB), BF),
                pltpu.VMEM((context, heads * QB), F32),
                pltpu.VMEM((context, heads * QB), BF),
                pltpu.VMEM((KB, heads * QB), BF),
                pltpu.VMEM((context, heads * QB), BF),
                pltpu.VMEM((width, heads * QB), BF),
                pltpu.VMEM((heads * QB, width), BF),
                pltpu.VMEM((width, heads * QB), BF),
                pltpu.VMEM((heads * QB, width), BF),
                pltpu.VMEM((width, QB), F32),
                pltpu.VMEM((width, QB), F32),
            ],
        ),
        compiler_params=params(),
        cost_estimate=cost(flops // 3, 20 * tokens * width, tokens * 1280 * heads),
        name="attend",
    )(starts, counts, crops, chips, qkv, grad, *full, maps, qcrop, ccrop)


def along_pix(value, by):
    size = lax.axis_size("pix")
    return lax.ppermute(value, "pix", [(i, i + by) for i in range(size) if 0 <= i + by < size])


def across_pix(value, bit):
    return lax.ppermute(value, "pix", [(i, i ^ bit) for i in range(lax.axis_size("pix"))])


def pix_sum(value):
    bit = 1
    while bit < lax.axis_size("pix"):
        value = value + across_pix(value, bit)
        bit *= 2
    return value


def to_mate(value):
    return lax.ppermute(value, "ch", [(i, i ^ 1) for i in range(lax.axis_size("ch"))])


def to_chip(value, by):
    size = lax.axis_size("ch")
    return lax.ppermute(value, "ch", [(i, (i + 2 * by) % size) for i in range(size)])


def gather_rows(value):
    return lax.all_gather(value, "pix", axis=0, tiled=True)


def paired():
    return lax.axis_size("ch") == 4 and lax.axis_size("pix") == 8


def scatter_lines(value):
    size = lax.axis_size("pix")
    lines = [[2 * i + side for i in range(size // 2)] for side in range(2)]
    return lax.psum_scatter(
        value, "pix", scatter_dimension=0, tiled=True, axis_index_groups=lines
    )


def halves_to_send(blocks, side):
    half = blocks[0].shape[1] // 2
    sent = [
        lax.dynamic_slice_in_dim(block[W:-W], (1 - side) * half, half, axis=1)
        for block in blocks[::2]
    ]
    return jnp.concatenate(sent, axis=1)


def scatter_rows(value):
    return lax.psum_scatter(value, "pix", scatter_dimension=0, tiled=True)


def block_ids():
    size = lax.axis_size("ch")
    here = lax.axis_index("ch")
    ids = [here, here ^ 1]
    for by in range(1, size // 2):
        other = lax.rem(here + size - 2 * by, size)
        ids += [other, other ^ 1]
    return jnp.stack(ids).astype(jnp.int32)


def chip_ids():
    size = lax.axis_size("ch")
    here = lax.axis_index("ch")
    chips = [lax.rem(here // 2 + by, size // 2) for by in range(1, size // 2)]
    home = jnp.stack([here // 2, here % 2]).astype(jnp.int32)
    return home, jnp.stack(chips + [here % 2]).astype(jnp.int32)


def tie(*values):
    return lax.optimization_barrier(values)


def far_blocks(value):
    return [to_chip(value, by) for by in range(1, lax.axis_size("ch") // 2)]


def with_mates(blocks):
    found = []
    for block in blocks:
        found += [block, to_mate(block)]
    return found


def gather_blocks(value):
    far = far_blocks(value)
    return [value, to_mate(value)] + with_mates(far)


def chip_sums(parts):
    own, mate = parts
    return [
        (own[i].astype(F32) + to_mate(mate[i]).astype(F32)).astype(BF) for i in range(own.shape[0])
    ]


def sent_sums(sums):
    return [to_chip(piece, by + 1) for by, piece in enumerate(sums)]


def home_parts(parts):
    return [parts[0][0], to_mate(parts[1][0])]


def unpack_rows(packed):
    lines = packed.shape[0]
    width = packed.shape[1] // W
    return packed.reshape(lines, width, W).transpose(0, 2, 1).reshape(lines * W, width)


def pack_rows(cells):
    width = cells.shape[1]
    lines = cells.shape[0] // W
    return cells.reshape(lines, W, width).transpose(0, 2, 1).reshape(lines, width * W)


def small(left, right):
    return jnp.dot(left, right, precision=HIGHEST)


def turned(left, right):
    return lax.dot_general(left, right, (TN, ((), ())), precision=HIGHEST)


def beside_rows(messages):
    to_next, to_prev = messages
    return along_pix(to_next, 1), along_pix(to_prev, -1)


def local(
    pixels,
    cotangent,
    crop_rows,
    condition,
    context,
    kernels,
    attention,
    embedding,
    gains,
    shifts,
    offsets,
):
    lines = pixels.shape[0]
    width = pixels.shape[1] // W
    tokens = lines * W
    depth_here = kernels.shape[0]
    crop_count = crop_rows.shape[0]
    place = lax.axis_index("pix")
    kernel_local = (
        kernels.reshape(depth_here, width, 18).transpose(0, 2, 1).reshape(depth_here, 18 * width)
    )
    maps_local = (
        attention.reshape(depth_here, width, 6).transpose(0, 2, 1).reshape(depth_here, 6 * width)
    )
    kernel_one = gather_rows(kernel_local[:, : 9 * width])
    two_local = kernel_local[:, 9 * width :]
    four = jnp.concatenate([maps_local[:, : 3 * width], maps_local[:, 5 * width :]], axis=1)
    embedding_local = (
        embedding.reshape(depth_here, width, 2).transpose(0, 2, 1).reshape(depth_here, 2 * width)
    )
    context_flat = context.reshape(-1, context.shape[2])
    own_rows = place * depth_here
    context_own = lax.dynamic_slice_in_dim(context_flat, own_rows, depth_here, axis=1)
    condition_own = lax.dynamic_slice_in_dim(condition, own_rows, depth_here, axis=1)
    summed = pix_sum(
        jnp.concatenate(
            [
                dot(condition_own, embedding_local, NN),
                dot(context_own, maps_local[:, 3 * width : 5 * width], NN),
            ],
            axis=0,
        )
    )
    bounds = jnp.cumsum(crop_rows)
    line = place * lines + jnp.arange(-(CROP_ROWS - 1), lines + CROP_ROWS - 1, dtype=jnp.int32)
    found = jnp.sum((line[:, None] >= bounds[None, :]).astype(jnp.int32), axis=1)
    crop_wide = jnp.where((line >= 0) & (line < bounds[-1]), found, -1)
    near = crop_wide[CROP_ROWS - 2 : CROP_ROWS + lines]
    crop_row = near[1:-1]
    same = (crop_row[:, None] == crop_row[None, :]).astype(F32)
    member = (crop_row[:, None] == jnp.arange(crop_count)[None, :]).astype(F32)
    sizes = jnp.sum(jnp.where(member > 0, crop_rows[None, :], 0), axis=1)
    rows = jnp.stack(
        [
            (near[:-2] == crop_row).astype(F32),
            jnp.ones((lines,), F32),
            (near[2:] == crop_row).astype(F32),
            (crop_row == near[0]).astype(F32),
            (crop_row == near[-1]).astype(F32),
            1.0 / (sizes * (W * GSIZE)).astype(F32),
        ]
    )
    rows = jnp.broadcast_to(rows[:, :, None], (6, lines, width))
    if paired():
        other = (place ^ 1) * lines + jnp.arange(-1, lines + 1, dtype=jnp.int32)
        found = jnp.sum((other[:, None] >= bounds[None, :]).astype(jnp.int32), axis=1)
        found = jnp.where((other >= 0) & (other < bounds[-1]), found, -1)
        other_rows = jnp.stack(
            [
                (found[:-2] == found[1:-1]).astype(F32),
                jnp.ones((lines,), F32),
                (found[2:] == found[1:-1]).astype(F32),
            ]
        )
        other_rows = jnp.broadcast_to(other_rows[:, :, None], (3, lines, width))
        side = place % 2
    crop_end = jnp.sum(jnp.where(member > 0, bounds[None, :], 0), axis=1)
    crop_start = crop_end - sizes
    base = place * lines - (CROP_ROWS - 1)
    step = QB // W
    window_low = (crop_start[::step] - base) * W
    window_high = (crop_end[step - 1 :: step] - base) * W
    starts = window_low // 128 * 128
    counts = (window_high - starts + KB - 1) // KB
    window = -(-(2 * HALO + tokens + KB) // KB) * KB
    key_crop = jnp.pad(
        crop_wide, (0, window // W - crop_wide.shape[0]), constant_values=-2
    ).astype(jnp.int32)
    context_crop = jnp.broadcast_to(
        jnp.repeat(jnp.arange(crop_count, dtype=jnp.int32), CTX)[:, None], (crop_count * CTX, 128)
    )
    query_crop = jnp.repeat(crop_row, W).reshape(-1, 1, QB)
    tables = (starts.astype(jnp.int32), counts.astype(jnp.int32), key_crop, query_crop, context_crop)

    ids = block_ids()
    home, away = chip_ids()
    near_side = side if paired() else jnp.zeros_like(place)
    home_ids = jnp.concatenate([home, near_side.astype(jnp.int32)[None], ids])
    gain = [gains[i : i + 1] for i in range(3)]
    shift = [shifts[i : i + 1] for i in range(3)]
    inputs = unpack_rows(pixels).astype(F32)
    dy_low = unpack_rows(cotangent)
    dy_beside = along_pix(dy_low[-W:], 1), along_pix(dy_low[:W], -1)
    totals, *messages = stats(inputs, same)
    input_beside = beside_rows(messages)
    a_one, stats_one = norm(inputs, totals, *input_beside, rows, gain[0], shift[0])
    one_blocks, kernel_one, two_local, summed = tie(
        gather_blocks(a_one), kernel_one, two_local, summed
    )
    embed_terms = summed[:crop_count]
    ckey = summed[crop_count:, :width].astype(BF)
    cval = summed[crop_count:, width:].astype(BF)
    kernel_two = gather_rows(two_local)
    c_one, totals, *messages = convolve(one_blocks, ids, kernel_one, rows, same, ())
    growth = 1.0 + small(member, embed_terms[:, :width] + offsets[2])
    shift_add = small(member, embed_terms[:, width:] + offsets[3])
    mixed = (growth, shift_add)
    c_beside = beside_rows(messages)
    a_two, stats_two = norm(c_one, totals, *c_beside, rows, gain[1], shift[1], mixed)
    two_blocks, kernel_two, four = tie(gather_blocks(a_two), kernel_two, four)
    four = gather_rows(four)
    resid, totals, *messages = convolve(
        two_blocks, ids, kernel_two, rows, same, (inputs, offsets[0:1])
    )
    resid_beside = beside_rows(messages)
    n_three, stats_three = norm(
        resid, totals, *resid_beside, rows, gain[2], shift[2], active=None, wide=False
    )
    dy_low, n_three, one_blocks, two_blocks = tie(dy_low, n_three, one_blocks, two_blocks)
    three_blocks = gather_blocks(n_three)
    if paired():
        sent = [halves_to_send(blocks, side) for blocks in (one_blocks, two_blocks)]
        three_blocks, sent = tie(three_blocks, sent)
    dy_blocks = gather_blocks(dy_low)
    qkv = project(three_blocks, ids, four, 0, 3 * width)
    first_dy, qkv = lax.optimization_barrier((dy_blocks[0], qkv))
    datt = project([first_dy] + dy_blocks[1:], ids, four, 3 * width, width)
    low = along_pix(qkv[tokens - HALO :, width:], 1)
    high = along_pix(qkv[:HALO, width:], -1)
    if paired():
        low, high, sent = tie(low, high, sent)
        sent, qkv, datt = tie(sent, qkv, datt)
        sent = [across_pix(part, 1) for part in sent]
    chips = jnp.concatenate([home[:1], away])
    found = attend(qkv, datt, low, high, ckey, cval, four, chips, tables)
    if paired():
        found, sent = tie(found, sent)
        one_pairs, two_pairs = [(part, to_mate(part)) for part in sent]
    *parts, att, dquery, dlow, down, dhigh, dckey, dcval = found
    from_prev, from_next = along_pix(dhigh, 1), along_pix(dlow, -1)
    arrived = sent_sums(chip_sums(parts[2:]))
    result = resid + offsets[1:2]
    for piece in home_parts(parts[:2]) + arrived:
        result = result + piece.astype(F32)
    result = pack_rows(result)
    from_prev, from_next, result, att = tie(from_prev, from_next, result, att)
    gap = ((0, tokens - HALO), (0, 0)), ((tokens - HALO, 0), (0, 0))
    down = down + jnp.pad(from_prev.astype(F32), gap[0]) + jnp.pad(from_next.astype(F32), gap[1])
    dqkv = jnp.concatenate([dquery, down.astype(BF)], axis=1)
    sums_three = chip_sums(spread(dqkv, away, four))
    dqkv, sums_three = tie(dqkv, sums_three)
    arrived = sent_sums(sums_three)
    *parts, dmap_three = home_and_outer(dqkv, home_ids, four, three_blocks)
    dmaps = jnp.concatenate([dmap_three, outer(dy_blocks, ids, att)], axis=1)
    parts, arrived, dmaps = tie(parts, arrived, dmaps)
    parts = home_parts(parts) + arrived
    dmaps = scatter_rows(dmaps)
    e_three, raw_three, totals, *messages = gradient_sums(
        parts, resid, stats_three, gain[2], shift[2], same
    )
    e_beside = beside_rows(messages)
    dresid, taps_two, wide_two, *parts = gradient_taps(
        e_three, resid, resid_beside, stats_three, totals, *e_beside, rows, gain[2],
        (dy_low, *dy_beside), away, kernel_two,
    )
    sums_two = chip_sums(parts)
    taps_two, sums_two = tie(taps_two, sums_two)
    arrived = sent_sums(sums_two)
    *parts, dkernel_two = home_and_outer(
        taps_two, home_ids, kernel_two, two_blocks, paired(), shift=W
    )
    if paired():
        beside_two = across_pix(wide_two, 1)
    parts, arrived, dkernel_two = tie(parts, arrived, dkernel_two)
    parts = home_parts(parts) + arrived
    e_two, raw_two, totals, *messages = gradient_sums(
        parts, c_one, stats_two, gain[1], shift[1], same, mixed
    )
    messages, dkernel_two = tie(messages, dkernel_two)
    if paired():
        dkernel_two = half_beside(two_pairs, home_ids[2:], beside_two, other_rows, dkernel_two)
    e_beside, dkernel_two, dmaps = tie(beside_rows(messages), dkernel_two, dmaps)
    dkernel_two = scatter_lines(dkernel_two) if paired() else scatter_rows(dkernel_two)
    taps_one, wide_one, *parts = gradient_taps(
        e_two, c_one, c_beside, stats_two, totals, *e_beside, rows, gain[1], None, away, kernel_one
    )
    sums_one = chip_sums(parts)
    taps_one, sums_one = tie(taps_one, sums_one)
    arrived = sent_sums(sums_one)
    *parts, dkernel_one = home_and_outer(
        taps_one, home_ids, kernel_one, one_blocks, paired(), shift=W
    )
    if paired():
        beside_one = across_pix(wide_one, 1)
        dkernel_one = half_beside(one_pairs, home_ids[2:], beside_one, other_rows, dkernel_one)
    parts, arrived, dkernel_one = tie(parts, arrived, dkernel_one)
    parts = home_parts(parts) + arrived
    dkernel_one, dkernel_two = tie(dkernel_one, dkernel_two)
    dkernel_one = scatter_lines(dkernel_one) if paired() else scatter_rows(dkernel_one)
    demb = jnp.concatenate(
        [turned(member, raw_two[1] * gain[1] + raw_two[0] * shift[1]), turned(member, raw_two[0])]
    )
    e_one, raw_one, totals, *messages = gradient_sums(
        parts, inputs, stats_one, gain[0], shift[0], same, active="plain"
    )
    grad_pixels = last_gradient(
        e_one, inputs, stats_one, totals, *beside_rows(messages), rows, gain[0], dresid
    )
    grad_pixels, raw_one = tie(grad_pixels, raw_one)
    sums = jnp.concatenate(
        [
            raw_one[1].sum(0)[None],
            (raw_two[1] * growth).sum(0)[None],
            raw_three[1].sum(0)[None],
            raw_one[0].sum(0)[None],
            (raw_two[0] * growth).sum(0)[None],
            raw_three[0].sum(0)[None],
            dresid.sum(0)[None],
            dy_low.astype(F32).sum(0)[None],
            demb,
            dckey,
            dcval,
        ],
        axis=0,
    )
    sums = pix_sum(sums)
    grad_gains, grad_shifts = sums[0:3], sums[3:6]
    demb = sums[8 : 8 + 2 * crop_count].reshape(2, crop_count, width)
    grad_offsets = jnp.concatenate([sums[6:8], demb.sum(1)])
    dcontext = sums[8 + 2 * crop_count :].reshape(2, crop_count * CTX, width)
    own_condition = condition_own.astype(F32)
    grad_embedding = jnp.stack([turned(own_condition, demb[i]) for i in range(2)], axis=2)
    own_context = context_own.astype(F32)
    dcontext_maps = [turned(own_context, dcontext[i]) for i in range(2)]
    dmaps = dmaps.astype(F32).reshape(depth_here, 4, width)
    grad_attention = jnp.stack(
        [dmaps[:, 0], dmaps[:, 1], dmaps[:, 2], *dcontext_maps, dmaps[:, 3]], axis=2
    )
    grad_kernels = pack_kernels(dkernel_one, dkernel_two)
    return (
        result,
        pack_rows(grad_pixels),
        grad_kernels,
        grad_attention.reshape(depth_here, 6 * width),
        grad_embedding.reshape(depth_here, 2 * width),
        grad_gains,
        grad_shifts,
        grad_offsets,
    )


def solution(mesh):
    split = P("pix", "ch")
    tall = P(None, "ch")
    return jax.shard_map(
        local,
        mesh=mesh,
        in_specs=(split, split, P(), P(), P(), split, split, split, tall, tall, tall),
        out_specs=(split, split, split, split, split, tall, tall, tall),
        check_vma=False,
    )
```

```python
import functools

import jax
import jax.numpy as jnp
from jax import lax
from jax.experimental import pallas as pl
from jax.experimental.pallas import tpu as pltpu
from jax.sharding import PartitionSpec as P

HEAD_DIM = 64
W = 32
CROP_ROWS = 32
CTX = 4
GSIZE = 32
HALO = (CROP_ROWS - 1) * W
QB = 256
KB = 256

HIGHEST = lax.Precision.HIGHEST
EPSILON = 1e-05
NEGATIVE = -1e30
BF = jnp.bfloat16
F32 = jnp.float32
VMEM_LIMIT = 58 * 1024 * 1024


def dot(left, right, dims):
    return lax.dot_general(left, right, (dims, ((), ())), preferred_element_type=F32)


NN = ((1,), (0,))
NT = ((1,), (1,))
TN = ((0,), (0,))


def params(**more):
    return pltpu.CompilerParams(vmem_limit_bytes=VMEM_LIMIT, **more)


def cost(flops, moved, exps=0):
    return pl.CostEstimate(flops=flops, bytes_accessed=moved, transcendentals=exps)


WITH_PREV, WITH_NEXT, INVERSE = 3, 4, 5
EDGE = 40


def exact(left, right):
    return lax.dot_general(
        left, right, (NN, ((), ())), precision=HIGHEST, preferred_element_type=F32
    )


def write_totals(first, second, same_ref, totals_ref, next_ref, prev_ref):
    lines, width = first.shape
    row = lax.broadcasted_iota(jnp.int32, (width, width), 0) // GSIZE
    column = lax.broadcasted_iota(jnp.int32, (width, width), 1) // GSIZE
    group = (row == column).astype(F32)
    for place, value in ((0, first), (1, second)):
        total = exact(same_ref[...], exact(value, group))
        totals_ref[place] = total
        next_ref[W + place : W + place + 1, :] = total[lines - 1 : lines, :]
        prev_ref[W + place : W + place + 1, :] = total[0:1, :]
    for target in (next_ref, prev_ref):
        target[W + 2 : EDGE, :] = jnp.zeros((EDGE - W - 2, width), F32)


def crop_means(totals_ref, before_ref, after_ref, rows_ref):
    found = []
    for place in range(2):
        line = slice(W + place, W + place + 1)
        total = totals_ref[place] + rows_ref[WITH_PREV] * before_ref[line, :]
        total = total + rows_ref[WITH_NEXT] * after_ref[line, :]
        found.append(total * rows_ref[INVERSE])
    return found


def square_sums(value_ref, sums_ref):
    lines = sums_ref.shape[1]

    def one(line, carry):
        cells = value_ref[pl.ds(pl.multiple_of(line * W, W), W), :]
        sums_ref[0, pl.ds(line, 1), :] = jnp.sum(cells, axis=0, keepdims=True)
        sums_ref[1, pl.ds(line, 1), :] = jnp.sum(cells * cells, axis=0, keepdims=True)
        return carry

    lax.fori_loop(0, lines, one, 0, unroll=4)


def stats_shapes(lines, width):
    return (
        jax.ShapeDtypeStruct((2, lines, width), F32),
        jax.ShapeDtypeStruct((EDGE, width), F32),
        jax.ShapeDtypeStruct((EDGE, width), F32),
    )


def stats_body(value_ref, same_ref, totals_ref, next_ref, prev_ref, sums_ref):
    tokens = value_ref.shape[0]
    square_sums(value_ref, sums_ref)
    write_totals(sums_ref[0], sums_ref[1], same_ref, totals_ref, next_ref, prev_ref)
    next_ref[0:W, :] = value_ref[tokens - W :, :]
    prev_ref[0:W, :] = value_ref[0:W, :]


def stats(value, same):
    tokens, width = value.shape
    return pl.pallas_call(
        stats_body,
        out_shape=stats_shapes(tokens // W, width),
        scratch_shapes=[pltpu.VMEM((2, tokens // W, width), F32)],
        compiler_params=params(),
        cost_estimate=cost(tokens * width * 4, tokens * width * 4),
        name="stats",
    )(value, same)


def norm_body(active, wide, *refs):
    value_ref, totals_ref, before_ref, after_ref, rows_ref, gain_ref, shift_ref = refs[:7]
    refs = refs[7:]
    if active == "mixed":
        growth_ref, add_ref = refs[:2]
        refs = refs[2:]
    out_ref, stats_ref, scale_ref, bias_ref = refs
    lines = totals_ref.shape[1]
    mean, square = crop_means(totals_ref, before_ref, after_ref, rows_ref)
    scale = lax.rsqrt(square - mean * mean + EPSILON)
    stats_ref[0] = mean
    stats_ref[1] = scale
    if active == "mixed":
        scale_ref[...] = scale * gain_ref[...] * growth_ref[...]
        bias_ref[...] = shift_ref[...] * growth_ref[...] + add_ref[...]
    else:
        scale_ref[...] = scale * gain_ref[...]
        bias_ref[...] = jnp.broadcast_to(shift_ref[...], bias_ref.shape)

    def cells_of(cells, line):
        here = pl.ds(line, 1)
        value = (cells - stats_ref[0, here, :]) * scale_ref[here, :] + bias_ref[here, :]
        if active is not None:
            value = value / (1.0 + jnp.exp(-value))
        return value.astype(BF)

    base = W if wide else 0

    def one(line, carry):
        start = pl.multiple_of(line * W, W)
        out_ref[pl.ds(start + base, W), :] = cells_of(value_ref[pl.ds(start, W), :], line)
        return carry

    lax.fori_loop(0, lines, one, 0, unroll=4)
    if wide:
        out_ref[0:W, :] = cells_of(before_ref[0:W, :], 0)
        out_ref[(lines + 1) * W :, :] = cells_of(after_ref[0:W, :], lines - 1)


def norm(value, totals, before, after, rows, gain, shift, mixed=None, active="plain", wide=True):
    tokens, width = value.shape
    lines = tokens // W
    operands = [value, totals, before, after, rows, gain, shift]
    if mixed is not None:
        operands += list(mixed)
        active = "mixed"
    return pl.pallas_call(
        functools.partial(norm_body, active, wide),
        out_shape=(
            jax.ShapeDtypeStruct((tokens + (2 * W if wide else 0), width), BF),
            jax.ShapeDtypeStruct((2, lines, width), F32),
        ),
        scratch_shapes=[pltpu.VMEM((lines, width), F32), pltpu.VMEM((lines, width), F32)],
        compiler_params=params(),
        cost_estimate=cost(tokens * width * 12, tokens * width * 6, tokens * width),
        name="norm",
    )(*operands)


def sums_body(count, active, *refs):
    parts = refs[:count]
    value_ref, stats_ref, gain_ref, shift_ref, same_ref = refs[count : count + 5]
    refs = refs[count + 5 :]
    if active == "mixed":
        growth_ref, add_ref = refs[:2]
        refs = refs[2:]
    grad_ref, raw_ref, totals_ref, next_ref, prev_ref = refs
    tokens, width = value_ref.shape
    lines = tokens // W

    def one(line, carry):
        here = pl.ds(line, 1)
        cells = pl.ds(pl.multiple_of(line * W, W), W)
        grad = parts[0][cells, :].astype(F32)
        for part in parts[1:]:
            grad = grad + part[cells, :].astype(F32)
        normal = (value_ref[cells, :] - stats_ref[0, here, :]) * stats_ref[1, here, :]
        if active is not None:
            inner = normal * gain_ref[...] + shift_ref[...]
            if active == "mixed":
                inner = inner * growth_ref[here, :] + add_ref[here, :]
            sigmoid = 1.0 / (1.0 + jnp.exp(-inner))
            grad = grad * sigmoid * (1.0 + inner * (1.0 - sigmoid))
        raw_ref[0, here, :] = jnp.sum(grad, axis=0, keepdims=True)
        raw_ref[1, here, :] = jnp.sum(grad * normal, axis=0, keepdims=True)
        if active == "mixed":
            grad = grad * growth_ref[here, :]
        grad_ref[cells, :] = grad
        return carry

    lax.fori_loop(0, lines, one, 0, unroll=4)
    first, second = raw_ref[0] * gain_ref[...], raw_ref[1] * gain_ref[...]
    if active == "mixed":
        first, second = first * growth_ref[...], second * growth_ref[...]
    write_totals(first, second, same_ref, totals_ref, next_ref, prev_ref)
    next_ref[0:W, :] = grad_ref[tokens - W :, :]
    prev_ref[0:W, :] = grad_ref[0:W, :]


def gradient_sums(parts, value, stats_found, gain, shift, same, mixed=None, active=None):
    tokens, width = value.shape
    operands = [*parts, value, stats_found, gain, shift, same]
    if mixed is not None:
        operands += list(mixed)
        active = "mixed"
    return pl.pallas_call(
        functools.partial(sums_body, len(parts), active),
        out_shape=(
            jax.ShapeDtypeStruct((tokens, width), F32),
            jax.ShapeDtypeStruct((2, tokens // W, width), F32),
        )
        + stats_shapes(tokens // W, width),
        compiler_params=params(),
        cost_estimate=cost(tokens * width * 20, tokens * width * 14, tokens * width),
        name="gradient_sums",
    )(*operands)


def norm_gradient(grad, value, line, stats_ref, mean_ref, gain_ref):
    here = pl.ds(line, 1)
    scale = stats_ref[1, here, :]
    normal = (value - stats_ref[0, here, :]) * scale
    return scale * (grad * gain_ref[...] - mean_ref[0, here, :] - normal * mean_ref[1, here, :])


def write_taps(wide_ref, rows_ref, taps_ref):
    tokens = taps_ref.shape[0]
    width = wide_ref.shape[1]
    column = lax.broadcasted_iota(jnp.int32, (W, width), 0)

    def spread_row(line, carry):
        start = pl.multiple_of(line * W, W)
        target = pl.ds(start, W)
        for up in range(3):
            mask = rows_ref[up, pl.ds(line, 1), :]
            values = wide_ref[pl.ds(start + up * W, W), :].astype(F32) * mask
            left = jnp.where(column > 0, pltpu.roll(values, 1, 0), 0.0)
            right = jnp.where(column < W - 1, pltpu.roll(values, W - 1, 0), 0.0)
            for side, moved in enumerate((left, values, right)):
                tap = 8 - (3 * up + side)
                taps_ref[target, tap * width : (tap + 1) * width] = moved.astype(BF)
        return carry

    lax.fori_loop(0, tokens // W, spread_row, 0, unroll=2)


def taps_body(based, ids, *refs):
    grad_ref, value_ref, value_before, value_after, stats_ref, totals_ref = refs[:6]
    before_ref, after_ref, rows_ref, gain_ref = refs[6:10]
    refs = refs[10:]
    if based:
        base_ref, base_before, base_after = refs[:3]
        refs = refs[3:]
    map_ref = refs[0]
    refs = refs[1:]
    if based:
        full_ref = refs[0]
        refs = refs[1:]
    taps_ref = refs[0]
    refs = refs[1:]
    low_ref, same_core, other_core, wide_ref, mean_ref = refs
    tokens, width = grad_ref.shape
    lines = tokens // W
    padded = tokens + 2 * W

    @pl.when(pl.program_id(0) == 0)
    def _():
        mean_ref[0], mean_ref[1] = crop_means(totals_ref, before_ref, after_ref, rows_ref)

        def one(line, carry):
            start = pl.multiple_of(line * W, W)
            cells = pl.ds(start, W)
            found = norm_gradient(
                grad_ref[cells, :], value_ref[cells, :], line, stats_ref, mean_ref, gain_ref
            )
            if based:
                found = found + base_ref[cells, :].astype(F32)
                full_ref[cells, :] = found
            wide_ref[pl.ds(start + W, W), :] = found
            return carry

        lax.fori_loop(0, lines, one, 0, unroll=4)
        for edge_ref, edge_value, line, start in (
            (before_ref, value_before, 0, 0),
            (after_ref, value_after, lines - 1, padded - W),
        ):
            found = norm_gradient(
                edge_ref[0:W, :], edge_value[0:W, :], line, stats_ref, mean_ref, gain_ref
            )
            if based:
                found = found + (base_before if line == 0 else base_after)[0:W, :].astype(F32)
            wide_ref[start : start + W, :] = found

        write_taps(wide_ref, rows_ref, taps_ref)
        low_ref[...] = wide_ref[...].astype(BF)

    core = ids[ids.shape[0] - 1]
    write_products(taps_ref, map_ref, core, same_core, other_core)


def write_products(grad_ref, map_ref, core, same_core, other_core):
    tokens, width = same_core.shape[1:]
    for place, target in ((core, same_core), (1 - core, other_core)):
        rows = pl.ds(pl.multiple_of(place * width, width), width)
        for start in range(0, tokens, 512):
            here = slice(start, start + 512)
            target[0, here, :] = dot(grad_ref[here, :], map_ref[rows, :], NT).astype(BF)


def gradient_taps(
    grad, value, beside, stats_found, totals, before, after, rows, gain, base, ids, maps
):
    tokens, width = grad.shape
    lines = tokens // W
    count = ids.shape[0] - 1
    wide = 9 * width
    operands = [grad, value, *beside, stats_found, totals, before, after, rows, gain]
    if base is not None:
        operands += list(base)
    whole = lambda array: pl.BlockSpec(array.shape, lambda step, ids: (0,) * len(array.shape))
    in_specs = [whole(operand) for operand in operands]
    operands.append(maps)
    in_specs.append(pl.BlockSpec((2 * width, wide), lambda step, ids: (ids[step], 0)))
    taps_shape = jax.ShapeDtypeStruct((tokens, wide), BF)
    shapes, out_specs = [taps_shape], [whole(taps_shape)]
    if base is not None:
        full_shape = jax.ShapeDtypeStruct((tokens, width), F32)
        shapes, out_specs = [full_shape] + shapes, [whole(full_shape)] + out_specs
    low_shape = jax.ShapeDtypeStruct((tokens + 2 * W, width), BF)
    shapes.append(low_shape)
    out_specs.append(whole(low_shape))
    shapes += [jax.ShapeDtypeStruct((count, tokens, width), BF)] * 2
    out_specs += [pl.BlockSpec((1, tokens, width), lambda step, ids: (step, 0, 0))] * 2
    return pl.pallas_call(
        functools.partial(taps_body, base is not None),
        out_shape=shapes,
        grid_spec=pltpu.PrefetchScalarGridSpec(
            num_scalar_prefetch=1,
            grid=(count,),
            in_specs=in_specs,
            out_specs=out_specs,
            scratch_shapes=[
                pltpu.VMEM((tokens + 2 * W, width), F32),
                pltpu.VMEM((2, lines, width), F32),
            ],
        ),
        compiler_params=params(),
        cost_estimate=cost(2 * tokens * count * width * wide, tokens * wide * 4),
        name="gradient_taps",
    )(ids, *operands)


def last_body(grad_ref, value_ref, stats_ref, totals_ref, before_ref, after_ref, rows_ref, gain_ref,
              base_ref, out_ref, mean_ref):
    mean_ref[0], mean_ref[1] = crop_means(totals_ref, before_ref, after_ref, rows_ref)

    def one(line, carry):
        cells = pl.ds(pl.multiple_of(line * W, W), W)
        out_ref[cells, :] = base_ref[cells, :] + norm_gradient(
            grad_ref[cells, :], value_ref[cells, :], line, stats_ref, mean_ref, gain_ref
        )
        return carry

    lax.fori_loop(0, grad_ref.shape[0] // W, one, 0, unroll=4)


def last_gradient(grad, value, stats_found, totals, before, after, rows, gain, base):
    tokens, width = grad.shape
    return pl.pallas_call(
        last_body,
        out_shape=jax.ShapeDtypeStruct((tokens, width), F32),
        scratch_shapes=[pltpu.VMEM((2, tokens // W, width), F32)],
        compiler_params=params(),
        cost_estimate=cost(tokens * width * 10, tokens * width * 16),
        name="last_gradient",
    )(grad, value, stats_found, totals, before, after, rows, gain, base)


def conv_body(count, resid, ids, *refs):
    blocks = refs[:count]
    kernel_ref, rows_ref = refs[count : count + 2]
    refs = refs[count + 2 :]
    if resid:
        input_ref, bias_ref = refs[:2]
        refs = refs[2:]
    same_ref, out_ref, totals_ref, next_ref, prev_ref, all_ref, sums_ref = refs
    tokens, width = out_ref.shape
    for place in range(count):
        lanes = pl.ds(pl.multiple_of(ids[place] * width, width), width)
        all_ref[:, lanes] = blocks[place][...]
    chunk = 256
    lines = chunk // W
    for start in range(0, tokens, chunk):
        here = slice(start, start + chunk)
        sides = [None] * 3
        for up in range(3):
            taps = kernel_ref[:, up * 3 * width : (up + 1) * 3 * width]
            part = dot(all_ref[up * W + start : up * W + start + chunk, :], taps, NN)
            part = part.reshape(lines, W, 3 * width)
            mask = rows_ref[up, start // W : start // W + lines, :][:, None, :]
            for side in range(3):
                piece = part[:, :, side * width : (side + 1) * width]
                piece = piece if up == 1 else piece * mask
                sides[side] = piece if sides[side] is None else sides[side] + piece
        sides = [piece.reshape(chunk, width) for piece in sides]
        column = lax.broadcasted_iota(jnp.int32, (chunk, width), 0) % W
        left = jnp.where(column > 0, pltpu.roll(sides[0], 1, 0), 0.0)
        right = jnp.where(column < W - 1, pltpu.roll(sides[2], chunk - 1, 0), 0.0)
        total = sides[1] + left + right
        if resid:
            total += input_ref[here, :] + bias_ref[...]
        out_ref[here, :] = total
    square_sums(out_ref, sums_ref)
    write_totals(sums_ref[0], sums_ref[1], same_ref, totals_ref, next_ref, prev_ref)
    next_ref[0:W, :] = out_ref[tokens - W :, :]
    prev_ref[0:W, :] = out_ref[0:W, :]


def convolve(blocks, ids, kernel, rows, same, resid):
    count = len(blocks)
    padded, width = blocks[0].shape
    tokens = padded - 2 * W
    lines = tokens // W
    operands = [*blocks, kernel, rows, *resid, same]

    def whole(array):
        return pl.BlockSpec(array.shape, lambda step, ids: (0,) * len(array.shape))

    shapes = (jax.ShapeDtypeStruct((tokens, width), F32),) + stats_shapes(lines, width)
    return pl.pallas_call(
        functools.partial(conv_body, count, len(resid)),
        out_shape=shapes,
        grid_spec=pltpu.PrefetchScalarGridSpec(
            num_scalar_prefetch=1,
            grid=(1,),
            in_specs=[whole(operand) for operand in operands],
            out_specs=[whole(shape) for shape in shapes],
            scratch_shapes=[
                pltpu.VMEM((padded, count * width), BF),
                pltpu.VMEM((2, lines, width), F32),
            ],
        ),
        compiler_params=params(),
        cost_estimate=cost(
            18 * tokens * count * width * width, 18 * count * width * width + tokens * width * 12
        ),
        name="convolve",
    )(ids, *operands)


def project_body(count, width, ids, *refs):
    blocks = refs[:count]
    map_ref, out_ref, *edges, all_ref = refs[count:]

    @pl.when(pl.program_id(0) == 0)
    def _():
        for place in range(count):
            first = pl.multiple_of(ids[place] * width, width)
            all_ref[:, pl.ds(first, width)] = blocks[place][...]

    for start in range(0, out_ref.shape[0], 512):
        here = slice(start, start + 512)
        out_ref[here, :] = dot(all_ref[here, :], map_ref[...], NN).astype(out_ref.dtype)
    if edges:
        edges[0][...] = out_ref[0:HALO, :]
        edges[1][...] = out_ref[out_ref.shape[0] - HALO :, :]


def project(blocks, ids, maps, first, wide, edges=False):
    count = len(blocks)
    tokens, width = blocks[0].shape
    depth = maps.shape[0]
    start = first // width
    out_shape = [jax.ShapeDtypeStruct((tokens, wide), BF)]
    out_specs = [pl.BlockSpec((tokens, width), lambda step, ids: (0, step))]
    if edges:
        edge_spec = pl.BlockSpec((HALO, width), lambda step, ids: (0, jnp.maximum(step - 1, 0)))
        out_shape += [jax.ShapeDtypeStruct((HALO, wide - width), BF)] * 2
        out_specs += [edge_spec] * 2
    found = pl.pallas_call(
        functools.partial(project_body, count, width),
        out_shape=out_shape,
        grid_spec=pltpu.PrefetchScalarGridSpec(
            num_scalar_prefetch=1,
            grid=(wide // width,),
            in_specs=[pl.BlockSpec((tokens, width), lambda step, ids: (0, 0))] * count
            + [pl.BlockSpec((depth, width), lambda step, ids: (0, start + step))],
            out_specs=out_specs,
            scratch_shapes=[pltpu.VMEM((tokens, depth), BF)],
        ),
        compiler_params=params(),
        cost_estimate=cost(2 * tokens * depth * wide, (tokens + depth) * wide * 2),
        name="project",
    )(ids, *blocks, maps)
    return found if edges else found[0]


def spread_body(ids, grad_ref, *refs):
    core = ids[ids.shape[0] - 1]
    write_products(grad_ref, refs[0], core, *refs[1:])


def spread(grad, ids, maps, first=0):
    tokens, wide = grad.shape
    count = ids.shape[0] - 1
    width = maps.shape[0] // lax.axis_size("ch")
    start = first // wide
    return pl.pallas_call(
        spread_body,
        out_shape=[jax.ShapeDtypeStruct((count, tokens, width), BF)] * 2,
        grid_spec=pltpu.PrefetchScalarGridSpec(
            num_scalar_prefetch=1,
            grid=(count,),
            in_specs=[
                pl.BlockSpec((tokens, wide), lambda step, ids: (0, 0)),
                pl.BlockSpec((2 * width, wide), lambda step, ids: (ids[step], start)),
            ],
            out_specs=[pl.BlockSpec((1, tokens, width), lambda step, ids: (step, 0, 0))] * 2,
        ),
        compiler_params=params(),
        cost_estimate=cost(4 * tokens * count * width * wide, (tokens + count * width) * wide * 2),
        name="spread",
    )(ids, grad, maps)


def home_body(count, halved, shift, ids, *refs):
    grad_ref, map_ref = refs[:2]
    blocks = refs[2 : 2 + count]
    same_core, other_core, out_ref, turned_ref = refs[2 + count :]
    tokens = grad_ref.shape[0]
    width = blocks[0].shape[1]
    share = width // 2 if halved else width
    write_products(grad_ref, map_ref, ids[1], same_core, other_core)
    for place in range(count):
        rows = pl.ds(pl.multiple_of(ids[3 + place] * share, share), share)
        lanes = slice(None)
        if halved:
            lanes = pl.ds(pl.multiple_of(ids[2] * share, share), share)
        turned_ref[rows, :] = blocks[place][shift : shift + tokens, lanes].T
    depth, wide = out_ref.shape
    for start in range(0, wide, 3 * width):
        columns = slice(start, start + 3 * width)
        out_ref[:, columns] = dot(turned_ref[...], grad_ref[:, columns], NN).astype(out_ref.dtype)


def home_and_outer(grad, ids, maps, blocks, halved=False, first=0, shift=0):
    count = len(blocks)
    tokens, wide = grad.shape
    width = blocks[0].shape[1]
    depth = count * width // (2 if halved else 1)
    start = first // wide
    part = jax.ShapeDtypeStruct((1, tokens, width), BF)

    def whole(array):
        return pl.BlockSpec(array.shape, lambda step, ids: (0,) * len(array.shape))

    result = jax.ShapeDtypeStruct((depth, wide), F32 if halved else BF)
    return pl.pallas_call(
        functools.partial(home_body, count, halved, shift),
        out_shape=[part, part, result],
        grid_spec=pltpu.PrefetchScalarGridSpec(
            num_scalar_prefetch=1,
            grid=(1,),
            in_specs=[
                whole(grad), pl.BlockSpec((2 * width, wide), lambda step, ids: (ids[0], start)),
            ]
            + [whole(block) for block in blocks],
            out_specs=[whole(part), whole(part), whole(result)],
            scratch_shapes=[pltpu.VMEM((depth, tokens), BF)],
        ),
        compiler_params=params(),
        cost_estimate=cost(
            2 * tokens * (depth + 2 * width) * wide, (tokens + depth + 2 * width) * wide * 2
        ),
        name="home_and_outer",
    )(ids, grad, maps, *blocks)


def half_beside_body(count, ids, *refs):
    pairs = refs[:2]
    wide_ref, rows_ref, own_ref, out_ref, turned_ref, taps_ref = refs[2:]
    tokens = taps_ref.shape[0]
    half = pairs[0].shape[1] // (count // 2)
    tile = out_ref.shape[1]
    step = pl.program_id(0)

    @pl.when(step == 0)
    def _():
        write_taps(wide_ref, rows_ref, taps_ref)
        for place in range(count):
            rows = pl.ds(pl.multiple_of(ids[1 + place] * half, half), half)
            lanes = slice(place // 2 * half, (place // 2 + 1) * half)
            turned_ref[rows, :] = pairs[place % 2][:, lanes].T

    columns = pl.ds(pl.multiple_of(step * tile, tile), tile)
    out_ref[...] = (own_ref[...] + dot(turned_ref[...], taps_ref[:, columns], NN)).astype(BF)


def half_beside(pairs, ids, wide_grad, row_masks, own):
    count = ids.shape[0] - 1
    tokens, both = pairs[0].shape
    depth, wide = own.shape
    padded, width = wide_grad.shape
    tile = 3 * width
    once = lambda step, ids: (0, 0)
    return pl.pallas_call(
        functools.partial(half_beside_body, count),
        out_shape=jax.ShapeDtypeStruct((depth, wide), BF),
        grid_spec=pltpu.PrefetchScalarGridSpec(
            num_scalar_prefetch=1,
            grid=(wide // tile,),
            in_specs=[
                pl.BlockSpec((tokens, both), once),
                pl.BlockSpec((tokens, both), once),
                pl.BlockSpec((padded, width), once),
                pl.BlockSpec(row_masks.shape, lambda step, ids: (0, 0, 0)),
                pl.BlockSpec((depth, tile), lambda step, ids: (0, step)),
            ],
            out_specs=pl.BlockSpec((depth, tile), lambda step, ids: (0, step)),
            scratch_shapes=[pltpu.VMEM((depth, tokens), BF), pltpu.VMEM((tokens, wide), BF)],
        ),
        compiler_params=params(),
        cost_estimate=cost(2 * tokens * depth * wide, (tokens + 3 * depth) * wide * 2),
        name="half_beside",
    )(ids, *pairs, wide_grad, row_masks, own)


def outer_body(count, shift, ids, *refs):
    blocks = refs[:count]
    grad_ref, out_ref, turned_ref = refs[count:]
    tokens = grad_ref.shape[0]
    width = blocks[0].shape[1]

    @pl.when(pl.program_id(0) == 0)
    def _():
        for place in range(count):
            first = pl.multiple_of(ids[place] * width, width)
            turned_ref[pl.ds(first, width), :] = blocks[place][shift : shift + tokens, :].T

    depth = turned_ref.shape[0]
    for start in range(0, depth, 512):
        here = slice(start, start + 512)
        out_ref[here, :] = dot(turned_ref[here, :], grad_ref[...], NN).astype(BF)


def outer(blocks, ids, grad, shift=0, columns=None):
    count = len(blocks)
    tokens = grad.shape[0]
    first, wide = columns or (0, grad.shape[1])
    padded, width = blocks[0].shape
    depth = count * width
    tile = min(wide, 3 * width)
    before = first // tile
    return pl.pallas_call(
        functools.partial(outer_body, count, shift),
        out_shape=jax.ShapeDtypeStruct((depth, wide), BF),
        grid_spec=pltpu.PrefetchScalarGridSpec(
            num_scalar_prefetch=1,
            grid=(wide // tile,),
            in_specs=[pl.BlockSpec((padded, width), lambda step, ids: (0, 0))] * count
            + [pl.BlockSpec((tokens, tile), lambda step, ids: (0, before + step))],
            out_specs=pl.BlockSpec((depth, tile), lambda step, ids: (0, step)),
            scratch_shapes=[pltpu.VMEM((depth, tokens), BF)],
        ),
        compiler_params=params(),
        cost_estimate=cost(2 * tokens * depth * wide, (tokens + depth) * wide * 2),
        name="outer",
    )(ids, *blocks, grad)


def pack_body(first_ref, second_ref, out_ref, order_ref, sorted_ref):
    depth, wide = first_ref.shape
    width = wide // 9
    size = order_ref.shape[0]
    for start in range(0, size, 128):
        row = start + lax.broadcasted_iota(jnp.int32, (128, size), 0)
        column = lax.broadcasted_iota(jnp.int32, (128, size), 1)
        wanted = (row & 63) * 18 + (row >> 6)
        order_ref[start : start + 128, :] = jnp.where(column == wanted, 1.0, 0.0).astype(BF)
    lane = lax.broadcasted_iota(jnp.int32, (depth, 128), 1)
    for block in range(width // 128):
        for pair in range(9):
            cells = []
            for tap in (2 * pair, 2 * pair + 1):
                source = first_ref if tap < 9 else second_ref
                at = tap % 9 * width + block * 128
                cells.append(source[:, at : at + 128].astype(F32))
            low = jnp.where(lane < 64, cells[0], pltpu.roll(cells[1], 64, 1))
            high = jnp.where(lane < 64, pltpu.roll(cells[0], 64, 1), cells[1])
            here = slice(pair * 128, (pair + 1) * 128)
            for half, value in ((0, low), (1, high)):
                at = (2 * block + half) * depth
                sorted_ref[at : at + depth, here] = value.astype(BF)
    found = dot(sorted_ref[...], order_ref[...], NN)
    for block in range(width // 64):
        out_ref[:, block * size : (block + 1) * size] = found[block * depth : (block + 1) * depth]


def pack_kernels(first, second):
    depth, wide = first.shape
    size = 64 * 18
    return pl.pallas_call(
        pack_body,
        out_shape=jax.ShapeDtypeStruct((depth, 2 * wide), F32),
        scratch_shapes=[
            pltpu.VMEM((size, size), BF),
            pltpu.VMEM((2 * wide // size * depth, size), BF),
        ],
        compiler_params=params(),
        cost_estimate=cost(4 * depth * wide * size, depth * wide * 12),
        name="pack_kernels",
    )(first, second)


def attention_body(
    heads, starts, counts, crops, chips, query_ref, grad_ref, low_ref, own_ref, high_ref, ckey_ref,
    cval_ref, map_ref, qcrop_ref, ccrop_ref, home_same, home_other, away_same, away_other, att_ref, dquery_ref, dlow_ref, down_ref, dhigh_ref, dckey_ref,
    dcval_ref, keys, values, keys_t, values_t, dkeys, dvalues, kcrop_ref, score_ref, prob_ref,
    cscore_ref, cprob_ref, slope_ref, cslope_ref, qt_ref, qn_ref, gt_ref, gn_ref, att_t, dq_t,
):
    step = pl.program_id(0)
    window, width = keys.shape
    tokens = own_ref.shape[0]

    @pl.when(step == 0)
    def _():
        def label(line, carry):
            here = pl.ds(pl.multiple_of(line * W, W), W)
            kcrop_ref[here, :] = jnp.full((W, 128), crops[line], jnp.int32)
            return carry

        lax.fori_loop(0, window // W, label, 0, unroll=2)
        for place, target, turned in ((0, keys, keys_t), (1, values, values_t)):
            part = slice(place * width, (place + 1) * width)
            target[0:HALO, :] = low_ref[:, part]
            shifted = slice((place + 1) * width, (place + 2) * width)
            target[HALO : HALO + tokens, :] = own_ref[:, shifted]
            target[HALO + tokens : 2 * HALO + tokens, :] = high_ref[:, part]
            rest = window - 2 * HALO - tokens
            target[2 * HALO + tokens :, :] = jnp.zeros((rest, width), BF)
            for place in range(0, window, KB):
                turned[:, place : place + KB] = target[place : place + KB, :].T
        dkeys[...] = jnp.zeros_like(dkeys)
        dvalues[...] = jnp.zeros_like(dvalues)
        dckey_ref[...] = jnp.zeros_like(dckey_ref)
        dcval_ref[...] = jnp.zeros_like(dcval_ref)

    first = starts[step]
    blocks = counts[step]
    query = (query_ref[...].astype(F32) * (HEAD_DIM**-0.5)).astype(BF)
    query_t = query.T
    grad_t = grad_ref[...].T
    lane = lax.broadcasted_iota(jnp.int32, (QB, width), 1)
    zero = jnp.zeros((width, QB), BF)
    mine = [slice(head * HEAD_DIM, (head + 1) * HEAD_DIM) for head in range(heads)]
    part = [slice(head * QB, (head + 1) * QB) for head in range(heads)]
    for head in range(heads):
        qt_ref[:, part[head]] = zero
        qt_ref[mine[head], part[head]] = query_t[mine[head], :]
        gt_ref[:, part[head]] = zero
        in_head = (lane >= head * HEAD_DIM) & (lane < (head + 1) * HEAD_DIM)
        qn_ref[part[head], :] = jnp.where(in_head, query, jnp.zeros_like(query))
    crop_row = qcrop_ref[...].reshape(1, QB)
    same_context = jnp.concatenate([ccrop_ref[...]] * (QB // 128), axis=1) == crop_row

    def span(block):
        return pl.ds(pl.multiple_of(first + block * KB, 128), KB)

    def folded(values, combine):
        return combine(values.reshape(-1, 8, QB), axis=0)

    largest = []
    products = dot(ckey_ref[...], qt_ref[...], NN)
    for head in range(heads):
        scores = jnp.where(same_context, products[:, part[head]], NEGATIVE)
        cscore_ref[:, part[head]] = scores
        largest.append(folded(scores, jnp.max))

    def pass_one(block, carry):
        here = span(block)
        same = jnp.concatenate([kcrop_ref[here, :]] * (QB // 128), axis=1) == crop_row
        products = dot(keys[here, :], qt_ref[...], NN)
        out = []
        for head in range(heads):
            scores = jnp.where(same, products[:, part[head]], NEGATIVE)
            score_ref[block, :, part[head]] = scores
            out.append(jnp.maximum(carry[head], folded(scores, jnp.max)))
        return tuple(out)

    largest = lax.fori_loop(0, blocks, pass_one, tuple(largest))
    largest = [jnp.max(value, axis=0, keepdims=True) for value in largest]

    sums = []
    for head in range(heads):
        prob = jnp.exp(cscore_ref[:, part[head]] - largest[head])
        sums.append(folded(prob, jnp.sum))
        low = prob.astype(BF)
        cprob_ref[:, part[head]] = low
        att_t[mine[head], :] = dot(cval_ref[...], low, TN)[mine[head], :]

    def pass_two(block, carry):
        here = span(block)
        out = []
        for head in range(heads):
            prob = jnp.exp(score_ref[block, :, part[head]] - largest[head])
            out.append(carry[head] + folded(prob, jnp.sum))
            low = prob.astype(BF)
            prob_ref[block, :, part[head]] = low
            att_t[mine[head], :] += dot(values_t[mine[head], here], low, NN)
        return tuple(out)

    sums = lax.fori_loop(0, blocks, pass_two, tuple(sums))
    offsets = []
    for head in range(heads):
        inverse = 1.0 / jnp.sum(sums[head], axis=0, keepdims=True)
        attended = att_t[mine[head], :] * inverse
        att_t[mine[head], :] = attended
        scaled = grad_t[mine[head], :].astype(F32) * inverse
        gt_ref[mine[head], part[head]] = scaled.astype(BF)
        offsets.append(jnp.sum(scaled * attended, axis=0, keepdims=True))
        gn_ref[part[head], :] = gt_ref[:, part[head]].T
    attended = att_t[...].T.astype(BF)
    att_ref[...] = attended
    core = chips[chips.shape[0] - 1]
    for chip in range(chips.shape[0] - 1):
        targets = (home_same, home_other) if chip == 0 else (away_same, away_other)
        for place, target in ((core, targets[0]), (1 - core, targets[1])):
            rows = pl.ds(pl.multiple_of((2 * chips[chip] + place) * width, width), width)
            target[max(chip - 1, 0)] = dot(attended, map_ref[rows, :], NT).astype(BF)

    slope = dot(cval_ref[...], gt_ref[...], NN)
    for head in range(heads):
        prob = cprob_ref[:, part[head]].astype(F32)
        dscore = (prob * (slope[:, part[head]] - offsets[head])).astype(BF)
        cslope_ref[:, part[head]] = dscore
        dq_t[mine[head], :] = dot(ckey_ref[...], dscore, TN)[mine[head], :]
    dcval_ref[...] += dot(cprob_ref[...], gn_ref[...], NN)
    dckey_ref[...] += dot(cslope_ref[...], qn_ref[...], NN)

    def pass_three(block, carry):
        here = span(block)
        slope = dot(values[here, :], gt_ref[...], NN)
        for head in range(heads):
            prob = prob_ref[block, :, part[head]].astype(F32)
            dscore = (prob * (slope[:, part[head]] - offsets[head])).astype(BF)
            slope_ref[:, part[head]] = dscore
            dq_t[mine[head], :] += dot(keys_t[mine[head], here], dscore, NN)
        dvalues[here, :] += dot(prob_ref[block], gn_ref[...], NN)
        dkeys[here, :] += dot(slope_ref[...], qn_ref[...], NN)
        return carry

    lax.fori_loop(0, blocks, pass_three, 0)
    dquery_ref[...] = (dq_t[...] * (HEAD_DIM**-0.5)).T.astype(BF)

    @pl.when(step == pl.num_programs(0) - 1)
    def _():
        for place, source in ((0, dkeys), (1, dvalues)):
            part = slice(place * width, (place + 1) * width)
            dlow_ref[:, part] = source[0:HALO, :].astype(BF)
            down_ref[:, part] = source[HALO : HALO + tokens, :]
            dhigh_ref[:, part] = source[HALO + tokens : 2 * HALO + tokens, :].astype(BF)


def attend(qkv, grad, low, high, ckey, cval, maps, chips, tables):
    starts, counts, crops, qcrop, ccrop = tables
    tokens, width = grad.shape
    heads = width // HEAD_DIM
    window = crops.shape[0] * W
    context = ckey.shape[0]
    most = ((QB // W + 2 * (CROP_ROWS - 1)) * W + 127 + KB - 1) // KB
    q_block = pl.BlockSpec((QB, width), lambda step, *_: (step, 0))

    def whole(array):
        return pl.BlockSpec(array.shape, lambda step, *_: (0,) * len(array.shape))

    full = [low, qkv, high, ckey, cval]
    others = chips.shape[0] - 2
    map_spec = pl.BlockSpec((maps.shape[0], width), lambda step, *_: (0, 3))
    part_shapes = [jax.ShapeDtypeStruct((count, tokens, width), BF) for count in (1, 1, others, others)]
    part_specs = [
        pl.BlockSpec((shape.shape[0], QB, width), lambda step, *_: (0, step, 0))
        for shape in part_shapes
    ]
    shapes = (
        jax.ShapeDtypeStruct((tokens, width), BF),
        jax.ShapeDtypeStruct((tokens, width), BF),
        jax.ShapeDtypeStruct((HALO, 2 * width), BF),
        jax.ShapeDtypeStruct((tokens, 2 * width), F32),
        jax.ShapeDtypeStruct((HALO, 2 * width), BF),
        jax.ShapeDtypeStruct((context, width), F32),
        jax.ShapeDtypeStruct((context, width), F32),
    )
    flops = 12 * tokens * 1280 * width
    return pl.pallas_call(
        functools.partial(attention_body, heads),
        out_shape=(*part_shapes, *shapes),
        grid_spec=pltpu.PrefetchScalarGridSpec(
            num_scalar_prefetch=4,
            grid=(tokens // QB,),
            in_specs=[q_block, q_block]
            + [whole(array) for array in full]
            + [map_spec, pl.BlockSpec((1, 1, QB), lambda step, *_: (step, 0, 0)), whole(ccrop)],
            out_specs=[*part_specs, q_block, q_block] + [whole(shape) for shape in shapes[2:]],
            scratch_shapes=[
                pltpu.VMEM((window, width), BF),
                pltpu.VMEM((window, width), BF),
                pltpu.VMEM((width, window), BF),
                pltpu.VMEM((width, window), BF),
                pltpu.VMEM((window, width), F32),
                pltpu.VMEM((window, width), F32),
                pltpu.VMEM((window, 128), jnp.int32),
                pltpu.VMEM((most, KB, heads * QB), F32),
                pltpu.VMEM((most, KB, heads * QB), BF),
                pltpu.VMEM((context, heads * QB), F32),
                pltpu.VMEM((context, heads * QB), BF),
                pltpu.VMEM((KB, heads * QB), BF),
                pltpu.VMEM((context, heads * QB), BF),
                pltpu.VMEM((width, heads * QB), BF),
                pltpu.VMEM((heads * QB, width), BF),
                pltpu.VMEM((width, heads * QB), BF),
                pltpu.VMEM((heads * QB, width), BF),
                pltpu.VMEM((width, QB), F32),
                pltpu.VMEM((width, QB), F32),
            ],
        ),
        compiler_params=params(),
        cost_estimate=cost(flops // 3, 20 * tokens * width, tokens * 1280 * heads),
        name="attend",
    )(starts, counts, crops, chips, qkv, grad, *full, maps, qcrop, ccrop)


def along_pix(value, by):
    size = lax.axis_size("pix")
    return lax.ppermute(value, "pix", [(i, i + by) for i in range(size) if 0 <= i + by < size])


def across_pix(value, bit):
    return lax.ppermute(value, "pix", [(i, i ^ bit) for i in range(lax.axis_size("pix"))])


def pix_sum(value, bit=1):
    while bit < lax.axis_size("pix"):
        value = value + across_pix(value, bit)
        bit *= 2
    return value


def to_mate(value):
    return lax.ppermute(value, "ch", [(i, i ^ 1) for i in range(lax.axis_size("ch"))])


def to_chip(value, by):
    size = lax.axis_size("ch")
    return lax.ppermute(value, "ch", [(i, (i + 2 * by) % size) for i in range(size)])


def gather_rows(value):
    return lax.all_gather(value, "pix", axis=0, tiled=True)


def paired():
    return lax.axis_size("ch") == 4 and lax.axis_size("pix") == 8


def scatter_lines(value):
    size = lax.axis_size("pix")
    lines = [[2 * i + side for i in range(size // 2)] for side in range(2)]
    return lax.psum_scatter(
        value, "pix", scatter_dimension=0, tiled=True, axis_index_groups=lines
    )


def halves_to_send(blocks, side):
    half = blocks[0].shape[1] // 2
    sent = [
        lax.dynamic_slice_in_dim(block[W:-W], (1 - side) * half, half, axis=1)
        for block in blocks[::2]
    ]
    return jnp.concatenate(sent, axis=1)


def scatter_rows(value):
    return lax.psum_scatter(value, "pix", scatter_dimension=0, tiled=True)


def block_ids():
    size = lax.axis_size("ch")
    here = lax.axis_index("ch")
    ids = [here, here ^ 1]
    for by in range(1, size // 2):
        other = lax.rem(here + size - 2 * by, size)
        ids += [other, other ^ 1]
    return jnp.stack(ids).astype(jnp.int32)


def chip_ids():
    size = lax.axis_size("ch")
    here = lax.axis_index("ch")
    chips = [lax.rem(here // 2 + by, size // 2) for by in range(1, size // 2)]
    home = jnp.stack([here // 2, here % 2]).astype(jnp.int32)
    return home, jnp.stack(chips + [here % 2]).astype(jnp.int32)


def tie(*values):
    return lax.optimization_barrier(values)


def far_blocks(value):
    return [to_chip(value, by) for by in range(1, lax.axis_size("ch") // 2)]


def with_mates(blocks):
    found = []
    for block in blocks:
        found += [block, to_mate(block)]
    return found


def gather_blocks(value):
    far = far_blocks(value)
    return [value, to_mate(value)] + with_mates(far)


def chip_sums(parts):
    own, mate = parts
    return [
        (own[i].astype(F32) + to_mate(mate[i]).astype(F32)).astype(BF) for i in range(own.shape[0])
    ]


def sent_sums(sums):
    return [to_chip(piece, by + 1) for by, piece in enumerate(sums)]


def home_parts(parts):
    return [parts[0][0], to_mate(parts[1][0])]


def unpack_rows(packed):
    lines = packed.shape[0]
    width = packed.shape[1] // W
    return packed.reshape(lines, width, W).transpose(0, 2, 1).reshape(lines * W, width)


def pack_rows(cells):
    width = cells.shape[1]
    lines = cells.shape[0] // W
    return cells.reshape(lines, W, width).transpose(0, 2, 1).reshape(lines, width * W)


def small(left, right):
    return jnp.dot(left, right, precision=HIGHEST)


def turned(left, right):
    return lax.dot_general(left, right, (TN, ((), ())), precision=HIGHEST)


def beside_rows(messages):
    to_next, to_prev = messages
    return along_pix(to_next, 1), along_pix(to_prev, -1)


def local(
    pixels,
    cotangent,
    crop_rows,
    condition,
    context,
    kernels,
    attention,
    embedding,
    gains,
    shifts,
    offsets,
):
    lines = pixels.shape[0]
    width = pixels.shape[1] // W
    tokens = lines * W
    depth_here = kernels.shape[0]
    crop_count = crop_rows.shape[0]
    place = lax.axis_index("pix")
    kernel_local = (
        kernels.reshape(depth_here, width, 18).transpose(0, 2, 1).reshape(depth_here, 18 * width)
    )
    maps_local = (
        attention.reshape(depth_here, width, 6).transpose(0, 2, 1).reshape(depth_here, 6 * width)
    )
    kernel_one = gather_rows(kernel_local[:, : 9 * width])
    two_local = kernel_local[:, 9 * width :]
    four = jnp.concatenate([maps_local[:, : 3 * width], maps_local[:, 5 * width :]], axis=1)
    embedding_local = (
        embedding.reshape(depth_here, width, 2).transpose(0, 2, 1).reshape(depth_here, 2 * width)
    )
    context_flat = context.reshape(-1, context.shape[2])
    own_rows = place * depth_here
    context_own = lax.dynamic_slice_in_dim(context_flat, own_rows, depth_here, axis=1)
    condition_own = lax.dynamic_slice_in_dim(condition, own_rows, depth_here, axis=1)
    summed = jnp.concatenate(
        [
            dot(condition_own, embedding_local, NN),
            dot(context_own, maps_local[:, 3 * width : 5 * width], NN),
        ],
        axis=0,
    )
    summed = summed + across_pix(summed, 1)
    bounds = jnp.cumsum(crop_rows)
    line = place * lines + jnp.arange(-(CROP_ROWS - 1), lines + CROP_ROWS - 1, dtype=jnp.int32)
    found = jnp.sum((line[:, None] >= bounds[None, :]).astype(jnp.int32), axis=1)
    crop_wide = jnp.where((line >= 0) & (line < bounds[-1]), found, -1)
    near = crop_wide[CROP_ROWS - 2 : CROP_ROWS + lines]
    crop_row = near[1:-1]
    same = (crop_row[:, None] == crop_row[None, :]).astype(F32)
    member = (crop_row[:, None] == jnp.arange(crop_count)[None, :]).astype(F32)
    sizes = jnp.sum(jnp.where(member > 0, crop_rows[None, :], 0), axis=1)
    rows = jnp.stack(
        [
            (near[:-2] == crop_row).astype(F32),
            jnp.ones((lines,), F32),
            (near[2:] == crop_row).astype(F32),
            (crop_row == near[0]).astype(F32),
            (crop_row == near[-1]).astype(F32),
            1.0 / (sizes * (W * GSIZE)).astype(F32),
        ]
    )
    rows = jnp.broadcast_to(rows[:, :, None], (6, lines, width))
    if paired():
        other = (place ^ 1) * lines + jnp.arange(-1, lines + 1, dtype=jnp.int32)
        found = jnp.sum((other[:, None] >= bounds[None, :]).astype(jnp.int32), axis=1)
        found = jnp.where((other >= 0) & (other < bounds[-1]), found, -1)
        other_rows = jnp.stack(
            [
                (found[:-2] == found[1:-1]).astype(F32),
                jnp.ones((lines,), F32),
                (found[2:] == found[1:-1]).astype(F32),
            ]
        )
        other_rows = jnp.broadcast_to(other_rows[:, :, None], (3, lines, width))
        side = place % 2
    crop_end = jnp.sum(jnp.where(member > 0, bounds[None, :], 0), axis=1)
    crop_start = crop_end - sizes
    base = place * lines - (CROP_ROWS - 1)
    step = QB // W
    window_low = (crop_start[::step] - base) * W
    window_high = (crop_end[step - 1 :: step] - base) * W
    starts = window_low // 128 * 128
    counts = (window_high - starts + KB - 1) // KB
    window = -(-(2 * HALO + tokens + KB) // KB) * KB
    key_crop = jnp.pad(
        crop_wide, (0, window // W - crop_wide.shape[0]), constant_values=-2
    ).astype(jnp.int32)
    context_crop = jnp.broadcast_to(
        jnp.repeat(jnp.arange(crop_count, dtype=jnp.int32), CTX)[:, None], (crop_count * CTX, 128)
    )
    query_crop = jnp.repeat(crop_row, W).reshape(-1, 1, QB)
    tables = (starts.astype(jnp.int32), counts.astype(jnp.int32), key_crop, query_crop, context_crop)

    ids = block_ids()
    home, away = chip_ids()
    near_side = side if paired() else jnp.zeros_like(place)
    home_ids = jnp.concatenate([home, near_side.astype(jnp.int32)[None], ids])
    gain = [gains[i : i + 1] for i in range(3)]
    shift = [shifts[i : i + 1] for i in range(3)]
    inputs = unpack_rows(pixels).astype(F32)
    dy_low = unpack_rows(cotangent)
    dy_beside = along_pix(dy_low[-W:], 1), along_pix(dy_low[:W], -1)
    totals, *messages = stats(inputs, same)
    messages, summed = tie(messages, summed)
    summed = summed + across_pix(summed, 2)
    input_beside, dy_beside, dy_low, summed = tie(
        beside_rows(messages), dy_beside, dy_low, summed
    )
    summed = pix_sum(summed, 4)
    a_one, stats_one = norm(inputs, totals, *input_beside, rows, gain[0], shift[0])
    one_blocks, kernel_one, two_local, summed = tie(
        gather_blocks(a_one), kernel_one, two_local, summed
    )
    embed_terms = summed[:crop_count]
    ckey = summed[crop_count:, :width].astype(BF)
    cval = summed[crop_count:, width:].astype(BF)
    kernel_two = gather_rows(two_local)
    c_one, totals, *messages = convolve(one_blocks, ids, kernel_one, rows, same, ())
    growth = 1.0 + small(member, embed_terms[:, :width] + offsets[2])
    shift_add = small(member, embed_terms[:, width:] + offsets[3])
    mixed = (growth, shift_add)
    c_beside = beside_rows(messages)
    a_two, stats_two = norm(c_one, totals, *c_beside, rows, gain[1], shift[1], mixed)
    two_blocks, kernel_two, four = tie(gather_blocks(a_two), kernel_two, four)
    four = gather_rows(four)
    resid, totals, *messages = convolve(
        two_blocks, ids, kernel_two, rows, same, (inputs, offsets[0:1])
    )
    resid_beside = beside_rows(messages)
    n_three, stats_three = norm(
        resid, totals, *resid_beside, rows, gain[2], shift[2], active=None, wide=False
    )
    dy_low, n_three, one_blocks, two_blocks = tie(dy_low, n_three, one_blocks, two_blocks)
    three_blocks = gather_blocks(n_three)
    if paired():
        sent = [halves_to_send(blocks, side) for blocks in (one_blocks, two_blocks)]
        three_blocks, sent = tie(three_blocks, sent)
    dy_blocks = gather_blocks(dy_low)
    qkv, head_rows, tail_rows = project(three_blocks, ids, four, 0, 3 * width, edges=True)
    first_dy, qkv = lax.optimization_barrier((dy_blocks[0], qkv))
    datt = project([first_dy] + dy_blocks[1:], ids, four, 3 * width, width)
    low, high = along_pix(tail_rows, 1), along_pix(head_rows, -1)
    if paired():
        low, high, sent = tie(low, high, sent)
        sent, qkv, datt = tie(sent, qkv, datt)
        sent = [across_pix(part, 1) for part in sent]
    chips = jnp.concatenate([home[:1], away])
    found = attend(qkv, datt, low, high, ckey, cval, four, chips, tables)
    if paired():
        found, sent = tie(found, sent)
        one_pairs, two_pairs = [(part, to_mate(part)) for part in sent]
    *parts, att, dquery, dlow, down, dhigh, dckey, dcval = found
    from_prev, from_next = along_pix(dhigh, 1), along_pix(dlow, -1)
    arrived = sent_sums(chip_sums(parts[2:]))
    result = resid + offsets[1:2]
    for piece in home_parts(parts[:2]) + arrived:
        result = result + piece.astype(F32)
    result = pack_rows(result)
    from_prev, from_next, result, att = tie(from_prev, from_next, result, att)
    gap = ((0, tokens - HALO), (0, 0)), ((tokens - HALO, 0), (0, 0))
    down = down + jnp.pad(from_prev.astype(F32), gap[0]) + jnp.pad(from_next.astype(F32), gap[1])
    dqkv = jnp.concatenate([dquery, down.astype(BF)], axis=1)
    sums_three = chip_sums(spread(dqkv, away, four))
    dqkv, sums_three = tie(dqkv, sums_three)
    arrived = sent_sums(sums_three)
    *parts, dmap_three = home_and_outer(dqkv, home_ids, four, three_blocks)
    dmaps = jnp.concatenate([dmap_three, outer(dy_blocks, ids, att)], axis=1)
    parts, arrived, dmaps = tie(parts, arrived, dmaps)
    parts = home_parts(parts) + arrived
    dmaps = scatter_rows(dmaps)
    e_three, raw_three, totals, *messages = gradient_sums(
        parts, resid, stats_three, gain[2], shift[2], same
    )
    e_beside = beside_rows(messages)
    dresid, taps_two, wide_two, *parts = gradient_taps(
        e_three, resid, resid_beside, stats_three, totals, *e_beside, rows, gain[2],
        (dy_low, *dy_beside), away, kernel_two,
    )
    sums_two = chip_sums(parts)
    taps_two, sums_two = tie(taps_two, sums_two)
    arrived = sent_sums(sums_two)
    *parts, dkernel_two = home_and_outer(
        taps_two, home_ids, kernel_two, two_blocks, paired(), shift=W
    )
    if paired():
        beside_two = across_pix(wide_two, 1)
    parts, arrived, dkernel_two = tie(parts, arrived, dkernel_two)
    parts = home_parts(parts) + arrived
    e_two, raw_two, totals, *messages = gradient_sums(
        parts, c_one, stats_two, gain[1], shift[1], same, mixed
    )
    messages, dkernel_two = tie(messages, dkernel_two)
    if paired():
        dkernel_two = half_beside(two_pairs, home_ids[2:], beside_two, other_rows, dkernel_two)
    e_beside, dkernel_two, dmaps = tie(beside_rows(messages), dkernel_two, dmaps)
    dkernel_two = scatter_lines(dkernel_two) if paired() else scatter_rows(dkernel_two)
    taps_one, wide_one, *parts = gradient_taps(
        e_two, c_one, c_beside, stats_two, totals, *e_beside, rows, gain[1], None, away, kernel_one
    )
    sums_one = chip_sums(parts)
    taps_one, sums_one = tie(taps_one, sums_one)
    arrived = sent_sums(sums_one)
    *parts, dkernel_one = home_and_outer(
        taps_one, home_ids, kernel_one, one_blocks, paired(), shift=W
    )
    if paired():
        beside_one = across_pix(wide_one, 1)
        dkernel_one = half_beside(one_pairs, home_ids[2:], beside_one, other_rows, dkernel_one)
    parts, arrived, dkernel_one = tie(parts, arrived, dkernel_one)
    parts = home_parts(parts) + arrived
    demb = jnp.concatenate(
        [turned(member, raw_two[1] * gain[1] + raw_two[0] * shift[1]), turned(member, raw_two[0])]
    )
    e_one, raw_one, totals, *messages = gradient_sums(
        parts, inputs, stats_one, gain[0], shift[0], same, active="plain"
    )
    messages, dkernel_one, dkernel_two = tie(messages, dkernel_one, dkernel_two)
    dkernel_one = scatter_lines(dkernel_one) if paired() else scatter_rows(dkernel_one)
    sums = jnp.concatenate(
        [
            raw_one[1].sum(0)[None],
            (raw_two[1] * growth).sum(0)[None],
            raw_three[1].sum(0)[None],
            raw_one[0].sum(0)[None],
            (raw_two[0] * growth).sum(0)[None],
            raw_three[0].sum(0)[None],
            dresid.sum(0)[None],
            dy_low.astype(F32).sum(0)[None],
            demb,
            dckey,
            dcval,
        ],
        axis=0,
    )
    sums = sums + across_pix(sums, 1)
    e_beside, sums = tie(beside_rows(messages), sums)
    grad_pixels = last_gradient(
        e_one, inputs, stats_one, totals, *e_beside, rows, gain[0], dresid
    )
    sums = sums + across_pix(sums, 2)
    grad_pixels, sums = tie(pack_rows(grad_pixels), sums)
    sums = pix_sum(sums, 4)
    grad_gains, grad_shifts = sums[0:3], sums[3:6]
    demb = sums[8 : 8 + 2 * crop_count].reshape(2, crop_count, width)
    grad_offsets = jnp.concatenate([sums[6:8], demb.sum(1)])
    dcontext = sums[8 + 2 * crop_count :].reshape(2, crop_count * CTX, width)
    own_condition = condition_own.astype(F32)
    grad_embedding = jnp.stack([turned(own_condition, demb[i]) for i in range(2)], axis=2)
    own_context = context_own.astype(F32)
    dcontext_maps = [turned(own_context, dcontext[i]) for i in range(2)]
    dmaps = dmaps.astype(F32).reshape(depth_here, 4, width)
    grad_attention = jnp.stack(
        [dmaps[:, 0], dmaps[:, 1], dmaps[:, 2], *dcontext_maps, dmaps[:, 3]], axis=2
    )
    grad_kernels = pack_kernels(dkernel_one, dkernel_two)
    return (
        result,
        grad_pixels,
        grad_kernels,
        grad_attention.reshape(depth_here, 6 * width),
        grad_embedding.reshape(depth_here, 2 * width),
        grad_gains,
        grad_shifts,
        grad_offsets,
    )


def solution(mesh):
    split = P("pix", "ch")
    tall = P(None, "ch")
    return jax.shard_map(
        local,
        mesh=mesh,
        in_specs=(split, split, P(), P(), P(), split, split, split, tall, tall, tall),
        out_specs=(split, split, split, split, split, tall, tall, tall),
        check_vma=False,
    )
```

```python
import functools

import jax
import jax.numpy as jnp
from jax import lax
from jax.experimental import pallas as pl
from jax.experimental.pallas import tpu as pltpu
from jax.sharding import PartitionSpec as P

HEAD_DIM = 64
W = 32
CROP_ROWS = 32
CTX = 4
GSIZE = 32
HALO = (CROP_ROWS - 1) * W
QB = 256
KB = 512

HIGHEST = lax.Precision.HIGHEST
EPSILON = 1e-05
NEGATIVE = -1e30
BF = jnp.bfloat16
F32 = jnp.float32
VMEM_LIMIT = 58 * 1024 * 1024


def dot(left, right, dims):
    return lax.dot_general(left, right, (dims, ((), ())), preferred_element_type=F32)


NN = ((1,), (0,))
NT = ((1,), (1,))
TN = ((0,), (0,))


def params(**more):
    return pltpu.CompilerParams(vmem_limit_bytes=VMEM_LIMIT, **more)


def cost(flops, moved, exps=0):
    return pl.CostEstimate(flops=flops, bytes_accessed=moved, transcendentals=exps)


WITH_PREV, WITH_NEXT, INVERSE = 3, 4, 5
EDGE = 40


def exact(left, right):
    return lax.dot_general(
        left, right, (NN, ((), ())), precision=HIGHEST, preferred_element_type=F32
    )


def write_totals(first, second, same_ref, totals_ref, next_ref, prev_ref):
    lines, width = first.shape
    row = lax.broadcasted_iota(jnp.int32, (width, width), 0) // GSIZE
    column = lax.broadcasted_iota(jnp.int32, (width, width), 1) // GSIZE
    group = (row == column).astype(F32)
    for place, value in ((0, first), (1, second)):
        total = exact(same_ref[...], exact(value, group))
        totals_ref[place] = total
        next_ref[W + place : W + place + 1, :] = total[lines - 1 : lines, :]
        prev_ref[W + place : W + place + 1, :] = total[0:1, :]
    for target in (next_ref, prev_ref):
        target[W + 2 : EDGE, :] = jnp.zeros((EDGE - W - 2, width), F32)


def crop_means(totals_ref, before_ref, after_ref, rows_ref):
    found = []
    for place in range(2):
        line = slice(W + place, W + place + 1)
        total = totals_ref[place] + rows_ref[WITH_PREV] * before_ref[line, :]
        total = total + rows_ref[WITH_NEXT] * after_ref[line, :]
        found.append(total * rows_ref[INVERSE])
    return found


def square_sums(value_ref, sums_ref):
    lines = sums_ref.shape[1]

    def one(line, carry):
        cells = value_ref[pl.ds(pl.multiple_of(line * W, W), W), :]
        sums_ref[0, pl.ds(line, 1), :] = jnp.sum(cells, axis=0, keepdims=True)
        sums_ref[1, pl.ds(line, 1), :] = jnp.sum(cells * cells, axis=0, keepdims=True)
        return carry

    lax.fori_loop(0, lines, one, 0, unroll=4)


def stats_shapes(lines, width):
    return (
        jax.ShapeDtypeStruct((2, lines, width), F32),
        jax.ShapeDtypeStruct((EDGE, width), F32),
        jax.ShapeDtypeStruct((EDGE, width), F32),
    )


def stats_body(value_ref, same_ref, totals_ref, next_ref, prev_ref, sums_ref):
    tokens = value_ref.shape[0]
    square_sums(value_ref, sums_ref)
    write_totals(sums_ref[0], sums_ref[1], same_ref, totals_ref, next_ref, prev_ref)
    next_ref[0:W, :] = value_ref[tokens - W :, :]
    prev_ref[0:W, :] = value_ref[0:W, :]


def stats(value, same):
    tokens, width = value.shape
    return pl.pallas_call(
        stats_body,
        out_shape=stats_shapes(tokens // W, width),
        scratch_shapes=[pltpu.VMEM((2, tokens // W, width), F32)],
        compiler_params=params(),
        cost_estimate=cost(tokens * width * 4, tokens * width * 4),
        name="stats",
    )(value, same)


def norm_body(active, wide, *refs):
    value_ref, totals_ref, before_ref, after_ref, rows_ref, gain_ref, shift_ref = refs[:7]
    refs = refs[7:]
    if active == "mixed":
        growth_ref, add_ref = refs[:2]
        refs = refs[2:]
    out_ref, stats_ref, scale_ref, bias_ref = refs
    lines = totals_ref.shape[1]
    mean, square = crop_means(totals_ref, before_ref, after_ref, rows_ref)
    scale = lax.rsqrt(square - mean * mean + EPSILON)
    stats_ref[0] = mean
    stats_ref[1] = scale
    if active == "mixed":
        scale_ref[...] = scale * gain_ref[...] * growth_ref[...]
        bias_ref[...] = shift_ref[...] * growth_ref[...] + add_ref[...]
    else:
        scale_ref[...] = scale * gain_ref[...]
        bias_ref[...] = jnp.broadcast_to(shift_ref[...], bias_ref.shape)

    def cells_of(cells, line):
        here = pl.ds(line, 1)
        value = (cells - stats_ref[0, here, :]) * scale_ref[here, :] + bias_ref[here, :]
        if active is not None:
            value = value / (1.0 + jnp.exp(-value))
        return value.astype(BF)

    base = W if wide else 0

    def one(line, carry):
        start = pl.multiple_of(line * W, W)
        out_ref[pl.ds(start + base, W), :] = cells_of(value_ref[pl.ds(start, W), :], line)
        return carry

    lax.fori_loop(0, lines, one, 0, unroll=4)
    if wide:
        out_ref[0:W, :] = cells_of(before_ref[0:W, :], 0)
        out_ref[(lines + 1) * W :, :] = cells_of(after_ref[0:W, :], lines - 1)


def norm(value, totals, before, after, rows, gain, shift, mixed=None, active="plain", wide=True):
    tokens, width = value.shape
    lines = tokens // W
    operands = [value, totals, before, after, rows, gain, shift]
    if mixed is not None:
        operands += list(mixed)
        active = "mixed"
    return pl.pallas_call(
        functools.partial(norm_body, active, wide),
        out_shape=(
            jax.ShapeDtypeStruct((tokens + (2 * W if wide else 0), width), BF),
            jax.ShapeDtypeStruct((2, lines, width), F32),
        ),
        scratch_shapes=[pltpu.VMEM((lines, width), F32), pltpu.VMEM((lines, width), F32)],
        compiler_params=params(),
        cost_estimate=cost(tokens * width * 12, tokens * width * 6, tokens * width),
        name="norm",
    )(*operands)


def sums_body(count, active, *refs):
    parts = refs[:count]
    value_ref, stats_ref, gain_ref, shift_ref, same_ref = refs[count : count + 5]
    refs = refs[count + 5 :]
    if active == "mixed":
        growth_ref, add_ref = refs[:2]
        refs = refs[2:]
    grad_ref, raw_ref, totals_ref, next_ref, prev_ref = refs
    tokens, width = value_ref.shape
    lines = tokens // W

    def one(line, carry):
        here = pl.ds(line, 1)
        cells = pl.ds(pl.multiple_of(line * W, W), W)
        grad = parts[0][cells, :].astype(F32)
        for part in parts[1:]:
            grad = grad + part[cells, :].astype(F32)
        normal = (value_ref[cells, :] - stats_ref[0, here, :]) * stats_ref[1, here, :]
        if active is not None:
            inner = normal * gain_ref[...] + shift_ref[...]
            if active == "mixed":
                inner = inner * growth_ref[here, :] + add_ref[here, :]
            sigmoid = 1.0 / (1.0 + jnp.exp(-inner))
            grad = grad * sigmoid * (1.0 + inner * (1.0 - sigmoid))
        raw_ref[0, here, :] = jnp.sum(grad, axis=0, keepdims=True)
        raw_ref[1, here, :] = jnp.sum(grad * normal, axis=0, keepdims=True)
        if active == "mixed":
            grad = grad * growth_ref[here, :]
        grad_ref[cells, :] = grad
        return carry

    lax.fori_loop(0, lines, one, 0, unroll=4)
    first, second = raw_ref[0] * gain_ref[...], raw_ref[1] * gain_ref[...]
    if active == "mixed":
        first, second = first * growth_ref[...], second * growth_ref[...]
    write_totals(first, second, same_ref, totals_ref, next_ref, prev_ref)
    next_ref[0:W, :] = grad_ref[tokens - W :, :]
    prev_ref[0:W, :] = grad_ref[0:W, :]


def gradient_sums(parts, value, stats_found, gain, shift, same, mixed=None, active=None):
    tokens, width = value.shape
    operands = [*parts, value, stats_found, gain, shift, same]
    if mixed is not None:
        operands += list(mixed)
        active = "mixed"
    return pl.pallas_call(
        functools.partial(sums_body, len(parts), active),
        out_shape=(
            jax.ShapeDtypeStruct((tokens, width), F32),
            jax.ShapeDtypeStruct((2, tokens // W, width), F32),
        )
        + stats_shapes(tokens // W, width),
        compiler_params=params(),
        cost_estimate=cost(tokens * width * 20, tokens * width * 14, tokens * width),
        name="gradient_sums",
    )(*operands)


def norm_gradient(grad, value, line, stats_ref, mean_ref, gain_ref):
    here = pl.ds(line, 1)
    scale = stats_ref[1, here, :]
    normal = (value - stats_ref[0, here, :]) * scale
    return scale * (grad * gain_ref[...] - mean_ref[0, here, :] - normal * mean_ref[1, here, :])


def write_taps(wide_ref, rows_ref, taps_ref):
    tokens = taps_ref.shape[0]
    width = wide_ref.shape[1]
    column = lax.broadcasted_iota(jnp.int32, (W, width), 0)

    def spread_row(line, carry):
        start = pl.multiple_of(line * W, W)
        target = pl.ds(start, W)
        for up in range(3):
            mask = rows_ref[up, pl.ds(line, 1), :]
            values = wide_ref[pl.ds(start + up * W, W), :].astype(F32) * mask
            left = jnp.where(column > 0, pltpu.roll(values, 1, 0), 0.0)
            right = jnp.where(column < W - 1, pltpu.roll(values, W - 1, 0), 0.0)
            for side, moved in enumerate((left, values, right)):
                tap = 8 - (3 * up + side)
                taps_ref[target, tap * width : (tap + 1) * width] = moved.astype(BF)
        return carry

    lax.fori_loop(0, tokens // W, spread_row, 0, unroll=2)


def taps_body(based, ids, *refs):
    grad_ref, value_ref, value_before, value_after, stats_ref, totals_ref = refs[:6]
    before_ref, after_ref, rows_ref, gain_ref = refs[6:10]
    refs = refs[10:]
    if based:
        base_ref, base_before, base_after = refs[:3]
        refs = refs[3:]
    map_ref = refs[0]
    refs = refs[1:]
    if based:
        full_ref = refs[0]
        refs = refs[1:]
    taps_ref = refs[0]
    refs = refs[1:]
    low_ref, same_core, other_core, wide_ref, mean_ref = refs
    tokens, width = grad_ref.shape
    lines = tokens // W
    padded = tokens + 2 * W

    @pl.when(pl.program_id(0) == 0)
    def _():
        mean_ref[0], mean_ref[1] = crop_means(totals_ref, before_ref, after_ref, rows_ref)

        def one(line, carry):
            start = pl.multiple_of(line * W, W)
            cells = pl.ds(start, W)
            found = norm_gradient(
                grad_ref[cells, :], value_ref[cells, :], line, stats_ref, mean_ref, gain_ref
            )
            if based:
                found = found + base_ref[cells, :].astype(F32)
                full_ref[cells, :] = found
            wide_ref[pl.ds(start + W, W), :] = found
            return carry

        lax.fori_loop(0, lines, one, 0, unroll=4)
        for edge_ref, edge_value, line, start in (
            (before_ref, value_before, 0, 0),
            (after_ref, value_after, lines - 1, padded - W),
        ):
            found = norm_gradient(
                edge_ref[0:W, :], edge_value[0:W, :], line, stats_ref, mean_ref, gain_ref
            )
            if based:
                found = found + (base_before if line == 0 else base_after)[0:W, :].astype(F32)
            wide_ref[start : start + W, :] = found

        write_taps(wide_ref, rows_ref, taps_ref)
        low_ref[...] = wide_ref[...].astype(BF)

    core = ids[ids.shape[0] - 1]
    write_products(taps_ref, map_ref, core, same_core, other_core)


def write_products(grad_ref, map_ref, core, same_core, other_core):
    tokens, width = same_core.shape[1:]
    for place, target in ((core, same_core), (1 - core, other_core)):
        rows = pl.ds(pl.multiple_of(place * width, width), width)
        for start in range(0, tokens, 512):
            here = slice(start, start + 512)
            target[0, here, :] = dot(grad_ref[here, :], map_ref[rows, :], NT).astype(BF)


def gradient_taps(
    grad, value, beside, stats_found, totals, before, after, rows, gain, base, ids, maps
):
    tokens, width = grad.shape
    lines = tokens // W
    count = ids.shape[0] - 1
    wide = 9 * width
    operands = [grad, value, *beside, stats_found, totals, before, after, rows, gain]
    if base is not None:
        operands += list(base)
    whole = lambda array: pl.BlockSpec(array.shape, lambda step, ids: (0,) * len(array.shape))
    in_specs = [whole(operand) for operand in operands]
    operands.append(maps)
    in_specs.append(pl.BlockSpec((2 * width, wide), lambda step, ids: (ids[step], 0)))
    taps_shape = jax.ShapeDtypeStruct((tokens, wide), BF)
    shapes, out_specs = [taps_shape], [whole(taps_shape)]
    if base is not None:
        full_shape = jax.ShapeDtypeStruct((tokens, width), F32)
        shapes, out_specs = [full_shape] + shapes, [whole(full_shape)] + out_specs
    low_shape = jax.ShapeDtypeStruct((tokens + 2 * W, width), BF)
    shapes.append(low_shape)
    out_specs.append(whole(low_shape))
    shapes += [jax.ShapeDtypeStruct((count, tokens, width), BF)] * 2
    out_specs += [pl.BlockSpec((1, tokens, width), lambda step, ids: (step, 0, 0))] * 2
    return pl.pallas_call(
        functools.partial(taps_body, base is not None),
        out_shape=shapes,
        grid_spec=pltpu.PrefetchScalarGridSpec(
            num_scalar_prefetch=1,
            grid=(count,),
            in_specs=in_specs,
            out_specs=out_specs,
            scratch_shapes=[
                pltpu.VMEM((tokens + 2 * W, width), F32),
                pltpu.VMEM((2, lines, width), F32),
            ],
        ),
        compiler_params=params(),
        cost_estimate=cost(2 * tokens * count * width * wide, tokens * wide * 4),
        name="gradient_taps",
    )(ids, *operands)


def last_body(grad_ref, value_ref, stats_ref, totals_ref, before_ref, after_ref, rows_ref, gain_ref,
              base_ref, out_ref, mean_ref):
    mean_ref[0], mean_ref[1] = crop_means(totals_ref, before_ref, after_ref, rows_ref)

    def one(line, carry):
        cells = pl.ds(pl.multiple_of(line * W, W), W)
        out_ref[cells, :] = base_ref[cells, :] + norm_gradient(
            grad_ref[cells, :], value_ref[cells, :], line, stats_ref, mean_ref, gain_ref
        )
        return carry

    lax.fori_loop(0, grad_ref.shape[0] // W, one, 0, unroll=4)


def last_gradient(grad, value, stats_found, totals, before, after, rows, gain, base):
    tokens, width = grad.shape
    return pl.pallas_call(
        last_body,
        out_shape=jax.ShapeDtypeStruct((tokens, width), F32),
        scratch_shapes=[pltpu.VMEM((2, tokens // W, width), F32)],
        compiler_params=params(),
        cost_estimate=cost(tokens * width * 10, tokens * width * 16),
        name="last_gradient",
    )(grad, value, stats_found, totals, before, after, rows, gain, base)


def conv_body(count, resid, ids, *refs):
    blocks = refs[:count]
    kernel_ref, rows_ref = refs[count : count + 2]
    refs = refs[count + 2 :]
    if resid:
        input_ref, bias_ref = refs[:2]
        refs = refs[2:]
    same_ref, out_ref, totals_ref, next_ref, prev_ref, all_ref, sums_ref = refs
    tokens, width = out_ref.shape
    for place in range(count):
        lanes = pl.ds(pl.multiple_of(ids[place] * width, width), width)
        all_ref[:, lanes] = blocks[place][...]
    chunk = 256
    lines = chunk // W
    for start in range(0, tokens, chunk):
        here = slice(start, start + chunk)
        sides = [None] * 3
        for up in range(3):
            taps = kernel_ref[:, up * 3 * width : (up + 1) * 3 * width]
            part = dot(all_ref[up * W + start : up * W + start + chunk, :], taps, NN)
            part = part.reshape(lines, W, 3 * width)
            mask = rows_ref[up, start // W : start // W + lines, :][:, None, :]
            for side in range(3):
                piece = part[:, :, side * width : (side + 1) * width]
                piece = piece if up == 1 else piece * mask
                sides[side] = piece if sides[side] is None else sides[side] + piece
        sides = [piece.reshape(chunk, width) for piece in sides]
        column = lax.broadcasted_iota(jnp.int32, (chunk, width), 0) % W
        left = jnp.where(column > 0, pltpu.roll(sides[0], 1, 0), 0.0)
        right = jnp.where(column < W - 1, pltpu.roll(sides[2], chunk - 1, 0), 0.0)
        total = sides[1] + left + right
        if resid:
            total += input_ref[here, :] + bias_ref[...]
        out_ref[here, :] = total
    square_sums(out_ref, sums_ref)
    write_totals(sums_ref[0], sums_ref[1], same_ref, totals_ref, next_ref, prev_ref)
    next_ref[0:W, :] = out_ref[tokens - W :, :]
    prev_ref[0:W, :] = out_ref[0:W, :]


def convolve(blocks, ids, kernel, rows, same, resid):
    count = len(blocks)
    padded, width = blocks[0].shape
    tokens = padded - 2 * W
    lines = tokens // W
    operands = [*blocks, kernel, rows, *resid, same]

    def whole(array):
        return pl.BlockSpec(array.shape, lambda step, ids: (0,) * len(array.shape))

    shapes = (jax.ShapeDtypeStruct((tokens, width), F32),) + stats_shapes(lines, width)
    return pl.pallas_call(
        functools.partial(conv_body, count, len(resid)),
        out_shape=shapes,
        grid_spec=pltpu.PrefetchScalarGridSpec(
            num_scalar_prefetch=1,
            grid=(1,),
            in_specs=[whole(operand) for operand in operands],
            out_specs=[whole(shape) for shape in shapes],
            scratch_shapes=[
                pltpu.VMEM((padded, count * width), BF),
                pltpu.VMEM((2, lines, width), F32),
            ],
        ),
        compiler_params=params(),
        cost_estimate=cost(
            18 * tokens * count * width * width, 18 * count * width * width + tokens * width * 12
        ),
        name="convolve",
    )(ids, *operands)


def project_body(count, width, ids, *refs):
    blocks = refs[:count]
    map_ref, out_ref, *edges, all_ref = refs[count:]

    @pl.when(pl.program_id(0) == 0)
    def _():
        for place in range(count):
            first = pl.multiple_of(ids[place] * width, width)
            all_ref[:, pl.ds(first, width)] = blocks[place][...]

    for start in range(0, out_ref.shape[0], 512):
        here = slice(start, start + 512)
        out_ref[here, :] = dot(all_ref[here, :], map_ref[...], NN).astype(out_ref.dtype)
    if edges:
        edges[0][...] = out_ref[0:HALO, :]
        edges[1][...] = out_ref[out_ref.shape[0] - HALO :, :]


def project(blocks, ids, maps, first, wide, edges=False):
    count = len(blocks)
    tokens, width = blocks[0].shape
    depth = maps.shape[0]
    start = first // width
    out_shape = [jax.ShapeDtypeStruct((tokens, wide), BF)]
    out_specs = [pl.BlockSpec((tokens, width), lambda step, ids: (0, step))]
    if edges:
        edge_spec = pl.BlockSpec((HALO, width), lambda step, ids: (0, jnp.maximum(step - 1, 0)))
        out_shape += [jax.ShapeDtypeStruct((HALO, wide - width), BF)] * 2
        out_specs += [edge_spec] * 2
    found = pl.pallas_call(
        functools.partial(project_body, count, width),
        out_shape=out_shape,
        grid_spec=pltpu.PrefetchScalarGridSpec(
            num_scalar_prefetch=1,
            grid=(wide // width,),
            in_specs=[pl.BlockSpec((tokens, width), lambda step, ids: (0, 0))] * count
            + [pl.BlockSpec((depth, width), lambda step, ids: (0, start + step))],
            out_specs=out_specs,
            scratch_shapes=[pltpu.VMEM((tokens, depth), BF)],
        ),
        compiler_params=params(),
        cost_estimate=cost(2 * tokens * depth * wide, (tokens + depth) * wide * 2),
        name="project",
    )(ids, *blocks, maps)
    return found if edges else found[0]


def spread_body(ids, grad_ref, *refs):
    core = ids[ids.shape[0] - 1]
    write_products(grad_ref, refs[0], core, *refs[1:])


def spread(grad, ids, maps, first=0):
    tokens, wide = grad.shape
    count = ids.shape[0] - 1
    width = maps.shape[0] // lax.axis_size("ch")
    start = first // wide
    return pl.pallas_call(
        spread_body,
        out_shape=[jax.ShapeDtypeStruct((count, tokens, width), BF)] * 2,
        grid_spec=pltpu.PrefetchScalarGridSpec(
            num_scalar_prefetch=1,
            grid=(count,),
            in_specs=[
                pl.BlockSpec((tokens, wide), lambda step, ids: (0, 0)),
                pl.BlockSpec((2 * width, wide), lambda step, ids: (ids[step], start)),
            ],
            out_specs=[pl.BlockSpec((1, tokens, width), lambda step, ids: (step, 0, 0))] * 2,
        ),
        compiler_params=params(),
        cost_estimate=cost(4 * tokens * count * width * wide, (tokens + count * width) * wide * 2),
        name="spread",
    )(ids, grad, maps)


def home_body(count, halved, shift, ids, *refs):
    grad_ref, map_ref = refs[:2]
    blocks = refs[2 : 2 + count]
    same_core, other_core, out_ref, turned_ref = refs[2 + count :]
    tokens = grad_ref.shape[0]
    width = blocks[0].shape[1]
    share = width // 2 if halved else width
    write_products(grad_ref, map_ref, ids[1], same_core, other_core)
    for place in range(count):
        rows = pl.ds(pl.multiple_of(ids[3 + place] * share, share), share)
        lanes = slice(None)
        if halved:
            lanes = pl.ds(pl.multiple_of(ids[2] * share, share), share)
        turned_ref[rows, :] = blocks[place][shift : shift + tokens, lanes].T
    depth, wide = out_ref.shape
    for start in range(0, wide, 3 * width):
        columns = slice(start, start + 3 * width)
        out_ref[:, columns] = dot(turned_ref[...], grad_ref[:, columns], NN).astype(out_ref.dtype)


def home_and_outer(grad, ids, maps, blocks, halved=False, first=0, shift=0):
    count = len(blocks)
    tokens, wide = grad.shape
    width = blocks[0].shape[1]
    depth = count * width // (2 if halved else 1)
    start = first // wide
    part = jax.ShapeDtypeStruct((1, tokens, width), BF)

    def whole(array):
        return pl.BlockSpec(array.shape, lambda step, ids: (0,) * len(array.shape))

    result = jax.ShapeDtypeStruct((depth, wide), F32 if halved else BF)
    return pl.pallas_call(
        functools.partial(home_body, count, halved, shift),
        out_shape=[part, part, result],
        grid_spec=pltpu.PrefetchScalarGridSpec(
            num_scalar_prefetch=1,
            grid=(1,),
            in_specs=[
                whole(grad), pl.BlockSpec((2 * width, wide), lambda step, ids: (ids[0], start)),
            ]
            + [whole(block) for block in blocks],
            out_specs=[whole(part), whole(part), whole(result)],
            scratch_shapes=[pltpu.VMEM((depth, tokens), BF)],
        ),
        compiler_params=params(),
        cost_estimate=cost(
            2 * tokens * (depth + 2 * width) * wide, (tokens + depth + 2 * width) * wide * 2
        ),
        name="home_and_outer",
    )(ids, grad, maps, *blocks)


def half_beside_body(count, ids, *refs):
    pairs = refs[:2]
    wide_ref, rows_ref, own_ref, out_ref, turned_ref, taps_ref = refs[2:]
    tokens = taps_ref.shape[0]
    half = pairs[0].shape[1] // (count // 2)
    tile = out_ref.shape[1]
    step = pl.program_id(0)

    @pl.when(step == 0)
    def _():
        write_taps(wide_ref, rows_ref, taps_ref)
        for place in range(count):
            rows = pl.ds(pl.multiple_of(ids[1 + place] * half, half), half)
            lanes = slice(place // 2 * half, (place // 2 + 1) * half)
            turned_ref[rows, :] = pairs[place % 2][:, lanes].T

    columns = pl.ds(pl.multiple_of(step * tile, tile), tile)
    out_ref[...] = (own_ref[...] + dot(turned_ref[...], taps_ref[:, columns], NN)).astype(BF)


def half_beside(pairs, ids, wide_grad, row_masks, own):
    count = ids.shape[0] - 1
    tokens, both = pairs[0].shape
    depth, wide = own.shape
    padded, width = wide_grad.shape
    tile = 3 * width
    once = lambda step, ids: (0, 0)
    return pl.pallas_call(
        functools.partial(half_beside_body, count),
        out_shape=jax.ShapeDtypeStruct((depth, wide), BF),
        grid_spec=pltpu.PrefetchScalarGridSpec(
            num_scalar_prefetch=1,
            grid=(wide // tile,),
            in_specs=[
                pl.BlockSpec((tokens, both), once),
                pl.BlockSpec((tokens, both), once),
                pl.BlockSpec((padded, width), once),
                pl.BlockSpec(row_masks.shape, lambda step, ids: (0, 0, 0)),
                pl.BlockSpec((depth, tile), lambda step, ids: (0, step)),
            ],
            out_specs=pl.BlockSpec((depth, tile), lambda step, ids: (0, step)),
            scratch_shapes=[pltpu.VMEM((depth, tokens), BF), pltpu.VMEM((tokens, wide), BF)],
        ),
        compiler_params=params(),
        cost_estimate=cost(2 * tokens * depth * wide, (tokens + 3 * depth) * wide * 2),
        name="half_beside",
    )(ids, *pairs, wide_grad, row_masks, own)


def outer_body(count, shift, ids, *refs):
    blocks = refs[:count]
    grad_ref, out_ref, turned_ref = refs[count:]
    tokens = grad_ref.shape[0]
    width = blocks[0].shape[1]

    @pl.when(pl.program_id(0) == 0)
    def _():
        for place in range(count):
            first = pl.multiple_of(ids[place] * width, width)
            turned_ref[pl.ds(first, width), :] = blocks[place][shift : shift + tokens, :].T

    depth = turned_ref.shape[0]
    for start in range(0, depth, 512):
        here = slice(start, start + 512)
        out_ref[here, :] = dot(turned_ref[here, :], grad_ref[...], NN).astype(BF)


def outer(blocks, ids, grad, shift=0, columns=None):
    count = len(blocks)
    tokens = grad.shape[0]
    first, wide = columns or (0, grad.shape[1])
    padded, width = blocks[0].shape
    depth = count * width
    tile = min(wide, 3 * width)
    before = first // tile
    return pl.pallas_call(
        functools.partial(outer_body, count, shift),
        out_shape=jax.ShapeDtypeStruct((depth, wide), BF),
        grid_spec=pltpu.PrefetchScalarGridSpec(
            num_scalar_prefetch=1,
            grid=(wide // tile,),
            in_specs=[pl.BlockSpec((padded, width), lambda step, ids: (0, 0))] * count
            + [pl.BlockSpec((tokens, tile), lambda step, ids: (0, before + step))],
            out_specs=pl.BlockSpec((depth, tile), lambda step, ids: (0, step)),
            scratch_shapes=[pltpu.VMEM((depth, tokens), BF)],
        ),
        compiler_params=params(),
        cost_estimate=cost(2 * tokens * depth * wide, (tokens + depth) * wide * 2),
        name="outer",
    )(ids, *blocks, grad)


def pack_body(first_ref, second_ref, out_ref, order_ref, sorted_ref):
    depth, wide = first_ref.shape
    width = wide // 9
    size = order_ref.shape[0]
    for start in range(0, size, 128):
        row = start + lax.broadcasted_iota(jnp.int32, (128, size), 0)
        column = lax.broadcasted_iota(jnp.int32, (128, size), 1)
        wanted = (row & 63) * 18 + (row >> 6)
        order_ref[start : start + 128, :] = jnp.where(column == wanted, 1.0, 0.0).astype(BF)
    lane = lax.broadcasted_iota(jnp.int32, (depth, 128), 1)
    for block in range(width // 128):
        for pair in range(9):
            cells = []
            for tap in (2 * pair, 2 * pair + 1):
                source = first_ref if tap < 9 else second_ref
                at = tap % 9 * width + block * 128
                cells.append(source[:, at : at + 128].astype(F32))
            low = jnp.where(lane < 64, cells[0], pltpu.roll(cells[1], 64, 1))
            high = jnp.where(lane < 64, pltpu.roll(cells[0], 64, 1), cells[1])
            here = slice(pair * 128, (pair + 1) * 128)
            for half, value in ((0, low), (1, high)):
                at = (2 * block + half) * depth
                sorted_ref[at : at + depth, here] = value.astype(BF)
    found = dot(sorted_ref[...], order_ref[...], NN)
    for block in range(width // 64):
        out_ref[:, block * size : (block + 1) * size] = found[block * depth : (block + 1) * depth]


def pack_kernels(first, second):
    depth, wide = first.shape
    size = 64 * 18
    return pl.pallas_call(
        pack_body,
        out_shape=jax.ShapeDtypeStruct((depth, 2 * wide), F32),
        scratch_shapes=[
            pltpu.VMEM((size, size), BF),
            pltpu.VMEM((2 * wide // size * depth, size), BF),
        ],
        compiler_params=params(),
        cost_estimate=cost(4 * depth * wide * size, depth * wide * 12),
        name="pack_kernels",
    )(first, second)


def attention_body(
    heads, starts, counts, crops, chips, query_ref, grad_ref, low_ref, own_ref, high_ref, ckey_ref,
    cval_ref, map_ref, qcrop_ref, ccrop_ref, home_same, home_other, away_same, away_other, att_ref, dquery_ref, dlow_ref, down_ref, dhigh_ref, dckey_ref,
    dcval_ref, keys, values, keys_t, values_t, dkeys, dvalues, kcrop_ref, score_ref, prob_ref,
    cscore_ref, cprob_ref, slope_ref, cslope_ref, qt_ref, qn_ref, gt_ref, gn_ref, att_t, dq_t,
):
    step = pl.program_id(0)
    window, width = keys.shape
    tokens = own_ref.shape[0]

    @pl.when(step == 0)
    def _():
        def label(line, carry):
            here = pl.ds(pl.multiple_of(line * W, W), W)
            kcrop_ref[here, :] = jnp.full((W, 128), crops[line], jnp.int32)
            return carry

        lax.fori_loop(0, window // W, label, 0, unroll=2)
        for place, target, turned in ((0, keys, keys_t), (1, values, values_t)):
            part = slice(place * width, (place + 1) * width)
            target[0:HALO, :] = low_ref[:, part]
            shifted = slice((place + 1) * width, (place + 2) * width)
            target[HALO : HALO + tokens, :] = own_ref[:, shifted]
            target[HALO + tokens : 2 * HALO + tokens, :] = high_ref[:, part]
            rest = window - 2 * HALO - tokens
            target[2 * HALO + tokens :, :] = jnp.zeros((rest, width), BF)
            for place in range(0, window, KB):
                turned[:, place : place + KB] = target[place : place + KB, :].T
        dkeys[...] = jnp.zeros_like(dkeys)
        dvalues[...] = jnp.zeros_like(dvalues)
        dckey_ref[...] = jnp.zeros_like(dckey_ref)
        dcval_ref[...] = jnp.zeros_like(dcval_ref)

    first = starts[step]
    blocks = counts[step]
    query = (query_ref[...].astype(F32) * (HEAD_DIM**-0.5)).astype(BF)
    query_t = query.T
    grad_t = grad_ref[...].T
    lane = lax.broadcasted_iota(jnp.int32, (QB, width), 1)
    zero = jnp.zeros((width, QB), BF)
    mine = [slice(head * HEAD_DIM, (head + 1) * HEAD_DIM) for head in range(heads)]
    part = [slice(head * QB, (head + 1) * QB) for head in range(heads)]
    for head in range(heads):
        qt_ref[:, part[head]] = zero
        qt_ref[mine[head], part[head]] = query_t[mine[head], :]
        gt_ref[:, part[head]] = zero
        in_head = (lane >= head * HEAD_DIM) & (lane < (head + 1) * HEAD_DIM)
        qn_ref[part[head], :] = jnp.where(in_head, query, jnp.zeros_like(query))
    crop_row = qcrop_ref[...].reshape(1, QB)
    same_context = jnp.concatenate([ccrop_ref[...]] * (QB // 128), axis=1) == crop_row

    def span(block):
        return pl.ds(pl.multiple_of(first + block * KB, 128), KB)

    def folded(values, combine):
        return combine(values.reshape(-1, 8, QB), axis=0)

    largest = []
    products = dot(ckey_ref[...], qt_ref[...], NN)
    for head in range(heads):
        scores = jnp.where(same_context, products[:, part[head]], NEGATIVE)
        cscore_ref[:, part[head]] = scores
        largest.append(folded(scores, jnp.max))

    def pass_one(block, carry):
        here = span(block)
        same = jnp.concatenate([kcrop_ref[here, :]] * (QB // 128), axis=1) == crop_row
        products = dot(keys[here, :], qt_ref[...], NN)
        out = []
        for head in range(heads):
            scores = jnp.where(same, products[:, part[head]], NEGATIVE)
            score_ref[block, :, part[head]] = scores
            out.append(jnp.maximum(carry[head], folded(scores, jnp.max)))
        return tuple(out)

    largest = lax.fori_loop(0, blocks, pass_one, tuple(largest))
    largest = [jnp.max(value, axis=0, keepdims=True) for value in largest]

    sums = []
    for head in range(heads):
        prob = jnp.exp(cscore_ref[:, part[head]] - largest[head])
        sums.append(folded(prob, jnp.sum))
        low = prob.astype(BF)
        cprob_ref[:, part[head]] = low
        att_t[mine[head], :] = dot(cval_ref[...], low, TN)[mine[head], :]

    def pass_two(block, carry):
        here = span(block)
        out = []
        for head in range(heads):
            prob = jnp.exp(score_ref[block, :, part[head]] - largest[head])
            out.append(carry[head] + folded(prob, jnp.sum))
            low = prob.astype(BF)
            prob_ref[block, :, part[head]] = low
            att_t[mine[head], :] += dot(values_t[mine[head], here], low, NN)
        return tuple(out)

    sums = lax.fori_loop(0, blocks, pass_two, tuple(sums))
    offsets = []
    for head in range(heads):
        inverse = 1.0 / jnp.sum(sums[head], axis=0, keepdims=True)
        attended = att_t[mine[head], :] * inverse
        att_t[mine[head], :] = attended
        scaled = grad_t[mine[head], :].astype(F32) * inverse
        gt_ref[mine[head], part[head]] = scaled.astype(BF)
        offsets.append(jnp.sum(scaled * attended, axis=0, keepdims=True))
        gn_ref[part[head], :] = gt_ref[:, part[head]].T
    attended = att_t[...].T.astype(BF)
    att_ref[...] = attended
    core = chips[chips.shape[0] - 1]
    for chip in range(chips.shape[0] - 1):
        targets = (home_same, home_other) if chip == 0 else (away_same, away_other)
        for place, target in ((core, targets[0]), (1 - core, targets[1])):
            rows = pl.ds(pl.multiple_of((2 * chips[chip] + place) * width, width), width)
            target[max(chip - 1, 0)] = dot(attended, map_ref[rows, :], NT).astype(BF)

    slope = dot(cval_ref[...], gt_ref[...], NN)
    for head in range(heads):
        prob = cprob_ref[:, part[head]].astype(F32)
        dscore = (prob * (slope[:, part[head]] - offsets[head])).astype(BF)
        cslope_ref[:, part[head]] = dscore
        dq_t[mine[head], :] = dot(ckey_ref[...], dscore, TN)[mine[head], :]
    dcval_ref[...] += dot(cprob_ref[...], gn_ref[...], NN)
    dckey_ref[...] += dot(cslope_ref[...], qn_ref[...], NN)

    def pass_three(block, carry):
        here = span(block)
        slope = dot(values[here, :], gt_ref[...], NN)
        for head in range(heads):
            prob = prob_ref[block, :, part[head]].astype(F32)
            dscore = (prob * (slope[:, part[head]] - offsets[head])).astype(BF)
            slope_ref[:, part[head]] = dscore
            dq_t[mine[head], :] += dot(keys_t[mine[head], here], dscore, NN)
        dvalues[here, :] += dot(prob_ref[block], gn_ref[...], NN)
        dkeys[here, :] += dot(slope_ref[...], qn_ref[...], NN)
        return carry

    lax.fori_loop(0, blocks, pass_three, 0)
    dquery_ref[...] = (dq_t[...] * (HEAD_DIM**-0.5)).T.astype(BF)

    @pl.when(step == pl.num_programs(0) - 1)
    def _():
        for place, source in ((0, dkeys), (1, dvalues)):
            part = slice(place * width, (place + 1) * width)
            dlow_ref[:, part] = source[0:HALO, :].astype(BF)
            down_ref[:, part] = source[HALO : HALO + tokens, :]
            dhigh_ref[:, part] = source[HALO + tokens : 2 * HALO + tokens, :].astype(BF)


def attend(qkv, grad, low, high, ckey, cval, maps, chips, tables):
    starts, counts, crops, qcrop, ccrop = tables
    tokens, width = grad.shape
    heads = width // HEAD_DIM
    window = crops.shape[0] * W
    context = ckey.shape[0]
    most = ((QB // W + 2 * (CROP_ROWS - 1)) * W + 127 + KB - 1) // KB
    q_block = pl.BlockSpec((QB, width), lambda step, *_: (step, 0))

    def whole(array):
        return pl.BlockSpec(array.shape, lambda step, *_: (0,) * len(array.shape))

    full = [low, qkv, high, ckey, cval]
    others = chips.shape[0] - 2
    map_spec = pl.BlockSpec((maps.shape[0], width), lambda step, *_: (0, 3))
    part_shapes = [jax.ShapeDtypeStruct((count, tokens, width), BF) for count in (1, 1, others, others)]
    part_specs = [
        pl.BlockSpec((shape.shape[0], QB, width), lambda step, *_: (0, step, 0))
        for shape in part_shapes
    ]
    shapes = (
        jax.ShapeDtypeStruct((tokens, width), BF),
        jax.ShapeDtypeStruct((tokens, width), BF),
        jax.ShapeDtypeStruct((HALO, 2 * width), BF),
        jax.ShapeDtypeStruct((tokens, 2 * width), F32),
        jax.ShapeDtypeStruct((HALO, 2 * width), BF),
        jax.ShapeDtypeStruct((context, width), F32),
        jax.ShapeDtypeStruct((context, width), F32),
    )
    flops = 12 * tokens * 1280 * width
    return pl.pallas_call(
        functools.partial(attention_body, heads),
        out_shape=(*part_shapes, *shapes),
        grid_spec=pltpu.PrefetchScalarGridSpec(
            num_scalar_prefetch=4,
            grid=(tokens // QB,),
            in_specs=[q_block, q_block]
            + [whole(array) for array in full]
            + [map_spec, pl.BlockSpec((1, 1, QB), lambda step, *_: (step, 0, 0)), whole(ccrop)],
            out_specs=[*part_specs, q_block, q_block] + [whole(shape) for shape in shapes[2:]],
            scratch_shapes=[
                pltpu.VMEM((window, width), BF),
                pltpu.VMEM((window, width), BF),
                pltpu.VMEM((width, window), BF),
                pltpu.VMEM((width, window), BF),
                pltpu.VMEM((window, width), F32),
                pltpu.VMEM((window, width), F32),
                pltpu.VMEM((window, 128), jnp.int32),
                pltpu.VMEM((most, KB, heads * QB), F32),
                pltpu.VMEM((most, KB, heads * QB), BF),
                pltpu.VMEM((context, heads * QB), F32),
                pltpu.VMEM((context, heads * QB), BF),
                pltpu.VMEM((KB, heads * QB), BF),
                pltpu.VMEM((context, heads * QB), BF),
                pltpu.VMEM((width, heads * QB), BF),
                pltpu.VMEM((heads * QB, width), BF),
                pltpu.VMEM((width, heads * QB), BF),
                pltpu.VMEM((heads * QB, width), BF),
                pltpu.VMEM((width, QB), F32),
                pltpu.VMEM((width, QB), F32),
            ],
        ),
        compiler_params=params(),
        cost_estimate=cost(flops // 3, 20 * tokens * width, tokens * 1280 * heads),
        name="attend",
    )(starts, counts, crops, chips, qkv, grad, *full, maps, qcrop, ccrop)


def along_pix(value, by):
    size = lax.axis_size("pix")
    return lax.ppermute(value, "pix", [(i, i + by) for i in range(size) if 0 <= i + by < size])


def across_pix(value, bit):
    return lax.ppermute(value, "pix", [(i, i ^ bit) for i in range(lax.axis_size("pix"))])


def pix_sum(value, bit=1):
    while bit < lax.axis_size("pix"):
        value = value + across_pix(value, bit)
        bit *= 2
    return value


def to_mate(value):
    return lax.ppermute(value, "ch", [(i, i ^ 1) for i in range(lax.axis_size("ch"))])


def to_chip(value, by):
    size = lax.axis_size("ch")
    return lax.ppermute(value, "ch", [(i, (i + 2 * by) % size) for i in range(size)])


def gather_rows(value):
    return lax.all_gather(value, "pix", axis=0, tiled=True)


def paired():
    return lax.axis_size("ch") == 4 and lax.axis_size("pix") == 8


def scatter_lines(value):
    size = lax.axis_size("pix")
    lines = [[2 * i + side for i in range(size // 2)] for side in range(2)]
    return lax.psum_scatter(
        value, "pix", scatter_dimension=0, tiled=True, axis_index_groups=lines
    )


def halves_to_send(blocks, side):
    half = blocks[0].shape[1] // 2
    sent = [
        lax.dynamic_slice_in_dim(block[W:-W], (1 - side) * half, half, axis=1)
        for block in blocks[::2]
    ]
    return jnp.concatenate(sent, axis=1)


def scatter_rows(value):
    return lax.psum_scatter(value, "pix", scatter_dimension=0, tiled=True)


def block_ids():
    size = lax.axis_size("ch")
    here = lax.axis_index("ch")
    ids = [here, here ^ 1]
    for by in range(1, size // 2):
        other = lax.rem(here + size - 2 * by, size)
        ids += [other, other ^ 1]
    return jnp.stack(ids).astype(jnp.int32)


def chip_ids():
    size = lax.axis_size("ch")
    here = lax.axis_index("ch")
    chips = [lax.rem(here // 2 + by, size // 2) for by in range(1, size // 2)]
    home = jnp.stack([here // 2, here % 2]).astype(jnp.int32)
    return home, jnp.stack(chips + [here % 2]).astype(jnp.int32)


def tie(*values):
    return lax.optimization_barrier(values)


def far_blocks(value):
    return [to_chip(value, by) for by in range(1, lax.axis_size("ch") // 2)]


def with_mates(blocks):
    found = []
    for block in blocks:
        found += [block, to_mate(block)]
    return found


def gather_blocks(value):
    far = far_blocks(value)
    return [value, to_mate(value)] + with_mates(far)


def chip_sums(parts):
    own, mate = parts
    return [
        (own[i].astype(F32) + to_mate(mate[i]).astype(F32)).astype(BF) for i in range(own.shape[0])
    ]


def sent_sums(sums):
    return [to_chip(piece, by + 1) for by, piece in enumerate(sums)]


def home_parts(parts):
    return [parts[0][0], to_mate(parts[1][0])]


def unpack_rows(packed):
    lines = packed.shape[0]
    width = packed.shape[1] // W
    return packed.reshape(lines, width, W).transpose(0, 2, 1).reshape(lines * W, width)


def pack_rows(cells):
    width = cells.shape[1]
    lines = cells.shape[0] // W
    return cells.reshape(lines, W, width).transpose(0, 2, 1).reshape(lines, width * W)


def small(left, right):
    return jnp.dot(left, right, precision=HIGHEST)


def turned(left, right):
    return lax.dot_general(left, right, (TN, ((), ())), precision=HIGHEST)


def beside_rows(messages):
    to_next, to_prev = messages
    return along_pix(to_next, 1), along_pix(to_prev, -1)


def local(
    pixels,
    cotangent,
    crop_rows,
    condition,
    context,
    kernels,
    attention,
    embedding,
    gains,
    shifts,
    offsets,
):
    lines = pixels.shape[0]
    width = pixels.shape[1] // W
    tokens = lines * W
    depth_here = kernels.shape[0]
    crop_count = crop_rows.shape[0]
    place = lax.axis_index("pix")
    kernel_local = (
        kernels.reshape(depth_here, width, 18).transpose(0, 2, 1).reshape(depth_here, 18 * width)
    )
    maps_local = (
        attention.reshape(depth_here, width, 6).transpose(0, 2, 1).reshape(depth_here, 6 * width)
    )
    kernel_one = gather_rows(kernel_local[:, : 9 * width])
    two_local = kernel_local[:, 9 * width :]
    four = jnp.concatenate([maps_local[:, : 3 * width], maps_local[:, 5 * width :]], axis=1)
    embedding_local = (
        embedding.reshape(depth_here, width, 2).transpose(0, 2, 1).reshape(depth_here, 2 * width)
    )
    context_flat = context.reshape(-1, context.shape[2])
    own_rows = place * depth_here
    context_own = lax.dynamic_slice_in_dim(context_flat, own_rows, depth_here, axis=1)
    condition_own = lax.dynamic_slice_in_dim(condition, own_rows, depth_here, axis=1)
    summed = jnp.concatenate(
        [
            dot(condition_own, embedding_local, NN),
            dot(context_own, maps_local[:, 3 * width : 5 * width], NN),
        ],
        axis=0,
    )
    summed = summed + across_pix(summed, 1)
    bounds = jnp.cumsum(crop_rows)
    line = place * lines + jnp.arange(-(CROP_ROWS - 1), lines + CROP_ROWS - 1, dtype=jnp.int32)
    found = jnp.sum((line[:, None] >= bounds[None, :]).astype(jnp.int32), axis=1)
    crop_wide = jnp.where((line >= 0) & (line < bounds[-1]), found, -1)
    near = crop_wide[CROP_ROWS - 2 : CROP_ROWS + lines]
    crop_row = near[1:-1]
    same = (crop_row[:, None] == crop_row[None, :]).astype(F32)
    member = (crop_row[:, None] == jnp.arange(crop_count)[None, :]).astype(F32)
    sizes = jnp.sum(jnp.where(member > 0, crop_rows[None, :], 0), axis=1)
    rows = jnp.stack(
        [
            (near[:-2] == crop_row).astype(F32),
            jnp.ones((lines,), F32),
            (near[2:] == crop_row).astype(F32),
            (crop_row == near[0]).astype(F32),
            (crop_row == near[-1]).astype(F32),
            1.0 / (sizes * (W * GSIZE)).astype(F32),
        ]
    )
    rows = jnp.broadcast_to(rows[:, :, None], (6, lines, width))
    if paired():
        other = (place ^ 1) * lines + jnp.arange(-1, lines + 1, dtype=jnp.int32)
        found = jnp.sum((other[:, None] >= bounds[None, :]).astype(jnp.int32), axis=1)
        found = jnp.where((other >= 0) & (other < bounds[-1]), found, -1)
        other_rows = jnp.stack(
            [
                (found[:-2] == found[1:-1]).astype(F32),
                jnp.ones((lines,), F32),
                (found[2:] == found[1:-1]).astype(F32),
            ]
        )
        other_rows = jnp.broadcast_to(other_rows[:, :, None], (3, lines, width))
        side = place % 2
    crop_end = jnp.sum(jnp.where(member > 0, bounds[None, :], 0), axis=1)
    crop_start = crop_end - sizes
    base = place * lines - (CROP_ROWS - 1)
    step = QB // W
    window_low = (crop_start[::step] - base) * W
    window_high = (crop_end[step - 1 :: step] - base) * W
    starts = window_low // 128 * 128
    counts = (window_high - starts + KB - 1) // KB
    window = -(-(2 * HALO + tokens + KB) // KB) * KB
    key_crop = jnp.pad(
        crop_wide, (0, window // W - crop_wide.shape[0]), constant_values=-2
    ).astype(jnp.int32)
    context_crop = jnp.broadcast_to(
        jnp.repeat(jnp.arange(crop_count, dtype=jnp.int32), CTX)[:, None], (crop_count * CTX, 128)
    )
    query_crop = jnp.repeat(crop_row, W).reshape(-1, 1, QB)
    tables = (starts.astype(jnp.int32), counts.astype(jnp.int32), key_crop, query_crop, context_crop)

    ids = block_ids()
    home, away = chip_ids()
    near_side = side if paired() else jnp.zeros_like(place)
    home_ids = jnp.concatenate([home, near_side.astype(jnp.int32)[None], ids])
    gain = [gains[i : i + 1] for i in range(3)]
    shift = [shifts[i : i + 1] for i in range(3)]
    inputs = unpack_rows(pixels).astype(F32)
    dy_low = unpack_rows(cotangent)
    dy_beside = along_pix(dy_low[-W:], 1), along_pix(dy_low[:W], -1)
    totals, *messages = stats(inputs, same)
    messages, summed = tie(messages, summed)
    summed = summed + across_pix(summed, 2)
    input_beside, dy_beside, dy_low, summed = tie(
        beside_rows(messages), dy_beside, dy_low, summed
    )
    summed = pix_sum(summed, 4)
    a_one, stats_one = norm(inputs, totals, *input_beside, rows, gain[0], shift[0])
    a_one, two_local = tie(a_one, two_local)
    kernel_two = gather_rows(two_local)
    one_blocks, kernel_one, summed = tie(gather_blocks(a_one), kernel_one, summed)
    embed_terms = summed[:crop_count]
    ckey = summed[crop_count:, :width].astype(BF)
    cval = summed[crop_count:, width:].astype(BF)
    c_one, totals, *messages = convolve(one_blocks, ids, kernel_one, rows, same, ())
    growth = 1.0 + small(member, embed_terms[:, :width] + offsets[2])
    shift_add = small(member, embed_terms[:, width:] + offsets[3])
    mixed = (growth, shift_add)
    c_beside = beside_rows(messages)
    a_two, stats_two = norm(c_one, totals, *c_beside, rows, gain[1], shift[1], mixed)
    a_two, four = tie(a_two, four)
    four = gather_rows(four)
    two_blocks, kernel_two = tie(gather_blocks(a_two), kernel_two)
    resid, totals, *messages = convolve(
        two_blocks, ids, kernel_two, rows, same, (inputs, offsets[0:1])
    )
    resid_beside = beside_rows(messages)
    n_three, stats_three = norm(
        resid, totals, *resid_beside, rows, gain[2], shift[2], active=None, wide=False
    )
    dy_low, n_three, one_blocks, two_blocks = tie(dy_low, n_three, one_blocks, two_blocks)
    three_blocks = gather_blocks(n_three)
    if paired():
        sent = [halves_to_send(blocks, side) for blocks in (one_blocks, two_blocks)]
        three_blocks, sent = tie(three_blocks, sent)
    dy_blocks = gather_blocks(dy_low)
    qkv, head_rows, tail_rows = project(three_blocks, ids, four, 0, 3 * width, edges=True)
    first_dy, qkv = lax.optimization_barrier((dy_blocks[0], qkv))
    datt = project([first_dy] + dy_blocks[1:], ids, four, 3 * width, width)
    low, high = along_pix(tail_rows, 1), along_pix(head_rows, -1)
    if paired():
        low, high, sent = tie(low, high, sent)
        sent, qkv, datt = tie(sent, qkv, datt)
        sent = [across_pix(part, 1) for part in sent]
    chips = jnp.concatenate([home[:1], away])
    found = attend(qkv, datt, low, high, ckey, cval, four, chips, tables)
    if paired():
        found, sent = tie(found, sent)
        one_pairs, two_pairs = [(part, to_mate(part)) for part in sent]
    *parts, att, dquery, dlow, down, dhigh, dckey, dcval = found
    from_prev, from_next = along_pix(dhigh, 1), along_pix(dlow, -1)
    arrived = sent_sums(chip_sums(parts[2:]))
    result = resid + offsets[1:2]
    for piece in home_parts(parts[:2]) + arrived:
        result = result + piece.astype(F32)
    result = pack_rows(result)
    from_prev, from_next, result, att = tie(from_prev, from_next, result, att)
    gap = ((0, tokens - HALO), (0, 0)), ((tokens - HALO, 0), (0, 0))
    down = down + jnp.pad(from_prev.astype(F32), gap[0]) + jnp.pad(from_next.astype(F32), gap[1])
    dqkv = jnp.concatenate([dquery, down.astype(BF)], axis=1)
    sums_three = chip_sums(spread(dqkv, away, four))
    dqkv, sums_three = tie(dqkv, sums_three)
    arrived = sent_sums(sums_three)
    *parts, dmap_three = home_and_outer(dqkv, home_ids, four, three_blocks)
    dmaps = jnp.concatenate([dmap_three, outer(dy_blocks, ids, att)], axis=1)
    parts, arrived, dmaps = tie(parts, arrived, dmaps)
    parts = home_parts(parts) + arrived
    dmaps = scatter_rows(dmaps)
    e_three, raw_three, totals, *messages = gradient_sums(
        parts, resid, stats_three, gain[2], shift[2], same
    )
    e_beside = beside_rows(messages)
    dresid, taps_two, wide_two, *parts = gradient_taps(
        e_three, resid, resid_beside, stats_three, totals, *e_beside, rows, gain[2],
        (dy_low, *dy_beside), away, kernel_two,
    )
    sums_two = chip_sums(parts)
    taps_two, sums_two = tie(taps_two, sums_two)
    arrived = sent_sums(sums_two)
    *parts, dkernel_two = home_and_outer(
        taps_two, home_ids, kernel_two, two_blocks, paired(), shift=W
    )
    if paired():
        beside_two = across_pix(wide_two, 1)
    parts, arrived, dkernel_two = tie(parts, arrived, dkernel_two)
    parts = home_parts(parts) + arrived
    e_two, raw_two, totals, *messages = gradient_sums(
        parts, c_one, stats_two, gain[1], shift[1], same, mixed
    )
    messages, dkernel_two = tie(messages, dkernel_two)
    if paired():
        dkernel_two = half_beside(two_pairs, home_ids[2:], beside_two, other_rows, dkernel_two)
    e_beside, dkernel_two, dmaps = tie(beside_rows(messages), dkernel_two, dmaps)
    dkernel_two = scatter_lines(dkernel_two) if paired() else scatter_rows(dkernel_two)
    taps_one, wide_one, *parts = gradient_taps(
        e_two, c_one, c_beside, stats_two, totals, *e_beside, rows, gain[1], None, away, kernel_one
    )
    sums_one = chip_sums(parts)
    taps_one, sums_one = tie(taps_one, sums_one)
    arrived = sent_sums(sums_one)
    *parts, dkernel_one = home_and_outer(
        taps_one, home_ids, kernel_one, one_blocks, paired(), shift=W
    )
    if paired():
        beside_one = across_pix(wide_one, 1)
        dkernel_one = half_beside(one_pairs, home_ids[2:], beside_one, other_rows, dkernel_one)
    parts, arrived, dkernel_one = tie(parts, arrived, dkernel_one)
    parts = home_parts(parts) + arrived
    demb = jnp.concatenate(
        [turned(member, raw_two[1] * gain[1] + raw_two[0] * shift[1]), turned(member, raw_two[0])]
    )
    e_one, raw_one, totals, *messages = gradient_sums(
        parts, inputs, stats_one, gain[0], shift[0], same, active="plain"
    )
    messages, dkernel_one, dkernel_two = tie(messages, dkernel_one, dkernel_two)
    dkernel_one = scatter_lines(dkernel_one) if paired() else scatter_rows(dkernel_one)
    sums = jnp.concatenate(
        [
            raw_one[1].sum(0)[None],
            (raw_two[1] * growth).sum(0)[None],
            raw_three[1].sum(0)[None],
            raw_one[0].sum(0)[None],
            (raw_two[0] * growth).sum(0)[None],
            raw_three[0].sum(0)[None],
            dresid.sum(0)[None],
            dy_low.astype(F32).sum(0)[None],
            demb,
            dckey,
            dcval,
        ],
        axis=0,
    )
    sums = sums + across_pix(sums, 1)
    e_beside, sums = tie(beside_rows(messages), sums)
    grad_pixels = last_gradient(
        e_one, inputs, stats_one, totals, *e_beside, rows, gain[0], dresid
    )
    sums = sums + across_pix(sums, 2)
    grad_pixels, sums = tie(pack_rows(grad_pixels), sums)
    sums = pix_sum(sums, 4)
    grad_gains, grad_shifts = sums[0:3], sums[3:6]
    demb = sums[8 : 8 + 2 * crop_count].reshape(2, crop_count, width)
    grad_offsets = jnp.concatenate([sums[6:8], demb.sum(1)])
    dcontext = sums[8 + 2 * crop_count :].reshape(2, crop_count * CTX, width)
    own_condition = condition_own.astype(F32)
    grad_embedding = jnp.stack([turned(own_condition, demb[i]) for i in range(2)], axis=2)
    own_context = context_own.astype(F32)
    dcontext_maps = [turned(own_context, dcontext[i]) for i in range(2)]
    dmaps = dmaps.astype(F32).reshape(depth_here, 4, width)
    grad_attention = jnp.stack(
        [dmaps[:, 0], dmaps[:, 1], dmaps[:, 2], *dcontext_maps, dmaps[:, 3]], axis=2
    )
    grad_kernels = pack_kernels(dkernel_one, dkernel_two)
    return (
        result,
        grad_pixels,
        grad_kernels,
        grad_attention.reshape(depth_here, 6 * width),
        grad_embedding.reshape(depth_here, 2 * width),
        grad_gains,
        grad_shifts,
        grad_offsets,
    )


def solution(mesh):
    split = P("pix", "ch")
    tall = P(None, "ch")
    return jax.shard_map(
        local,
        mesh=mesh,
        in_specs=(split, split, P(), P(), P(), split, split, split, tall, tall, tall),
        out_specs=(split, split, split, split, split, tall, tall, tall),
        check_vma=False,
    )
```
